32 devices in a mesh: chan: 8 (over y, x, core), freq: 4 (over z).
Axes of the slice: x: 2, y: 2, z: 4, core: 2. Of those that a mesh axis runs over, the one named last changes fastest.
Arguments:
- traces: bfloat16 [1024, 16, 2048], P('chan', 'freq'), may hold values from -32 to 32
- band_bins: int32 [256], replicated, may hold values from 1 to 1023, as said below
- pair_blocks: int32 [8, 3], P('chan'), may hold values from 0 to 7, as said below
Outputs:
- correlations: float32 [8, 128, 3, 128, 128], P('chan', 'freq')
The draws below stay inside these ranges and needn't reach their ends.
Inputs may be any that keep to these rules, and one draw needn't show every extreme that they name: `band_bins`: distinct and increasing. pair_blocks[i, k] lies within 3 blocks of i; pair_blocks[i, 0] is the lowest and pair_blocks[i, 1] the highest such block.
All inputs are finite; a program needn't handle non-finite values.
Results may differ from the reference program's by a relative error of at most 0.005.
Values may be sent and summed in bfloat16 or wider, within the bound.
No kernel may reach another device: no remote copies, remote signals or barrier semaphores. Data moves between devices by JAX's collectives and lax.ppermute only.
A program may use at most 256 MiB of HBM per device.

```python
import math
import jax
import jax.numpy as jnp
from jax import lax

SAMPLES = 2048
BINS = 256
LAGS = 128
REACH = 3
PAIRS = 3
CH_DEV = 128
CHANNELS = 1024
WINDOWS = 16
N_CHAN = 8


def draw_traces(key, part):
    key = jax.random.fold_in(key, 11)
    key_scale, key_base = jax.random.split(key, 2)
    shape = (CHANNELS, WINDOWS, SAMPLES)
    spread = jnp.exp(jax.random.uniform(key_scale, (CHANNELS, WINDOWS, 1), jnp.float32, math.log(0.3), math.log(3.0)))
    base = jnp.clip(jax.random.normal(key_base, shape, jnp.float32), -8.0, 8.0)
    return jnp.clip(base * spread, -32.0, 32.0).astype(jnp.bfloat16)


def draw_band_bins(key, part):
    key = jax.random.fold_in(key, 12)
    half = SAMPLES // 2
    inner = jax.random.permutation(key, half - 3)[:BINS - 2].astype(jnp.int32) + 2
    values = jnp.concatenate([jnp.array([1], jnp.int32), inner, jnp.array([half - 1], jnp.int32)])
    return jnp.sort(values).astype(jnp.int32)


def draw_pair_blocks(key, part):
    key = jax.random.fold_in(key, 13)
    owners = jnp.arange(N_CHAN, dtype=jnp.int32)[:, None]
    lowest = jnp.maximum(-REACH, -owners)
    highest = jnp.minimum(REACH, N_CHAN - 1 - owners)
    picks = jax.random.randint(key, (N_CHAN, PAIRS - 2), 0, 1 << 20, jnp.int32)
    middle = lowest + picks % (highest - lowest + 1)
    offsets = jnp.concatenate([lowest, highest, middle], 1)
    return (owners + offsets).astype(jnp.int32)


def setup_inputs(seed: int = 0) -> dict:
    seeds = jax.random.split(jax.random.key(seed), 4)
    return {
        "traces": draw_traces(jax.random.fold_in(seeds[3], 71), 0),
        "band_bins": draw_band_bins(jax.random.fold_in(seeds[3], 71), 0),
        "pair_blocks": draw_pair_blocks(jax.random.fold_in(seeds[3], 71), 0),
    }


def make_dft_table(band_bins, length):
    sample_idx = jnp.arange(length, dtype=jnp.int32)
    phase_int = band_bins[:, None].astype(jnp.int32) * sample_idx[None, :] % length
    phases = phase_int.astype(jnp.float32) * (2.0 * math.pi / length)
    return jnp.concatenate([jnp.cos(phases), -jnp.sin(phases)], 0).T.astype(jnp.bfloat16)

def make_lag_table(band_bins, length, lag_count):
    lag_idx = jnp.arange(lag_count, dtype=jnp.int32) - lag_count // 2
    phase_int = band_bins[:, None].astype(jnp.int32) * lag_idx[None, :] % length
    phases = phase_int.astype(jnp.float32) * (2.0 * math.pi / length)
    return jnp.concatenate([jnp.cos(phases), -jnp.sin(phases)], 0)

def gram_pair(first_block, second_block):
    rotated = jnp.stack([-second_block[:, :, 1], second_block[:, :, 0]], 2)
    gram_real = jnp.einsum('awcf,bwcf->abf', first_block, second_block, precision=lax.Precision.HIGHEST)
    gram_imag = jnp.einsum('awcf,bwcf->abf', first_block, rotated, precision=lax.Precision.HIGHEST)
    return jnp.stack([gram_real, gram_imag], 2)

def reference(traces, band_bins, pair_blocks):
    dft_matrix = make_dft_table(band_bins, SAMPLES)
    blocks = traces.reshape(N_CHAN, CH_DEV * WINDOWS, SAMPLES)

    def whiten(block):
        spectra = jnp.dot(block, dft_matrix, preferred_element_type=jnp.float32)
        amplitude = jnp.sqrt(lax.optimization_barrier(jnp.sum(spectra * spectra, axis=1, keepdims=True)) / BINS + 1e-06)
        return (spectra / amplitude).astype(jnp.bfloat16).reshape(CH_DEV, WINDOWS, 2, BINS)
    whitened = lax.map(whiten, blocks)
    lag_matrix = make_lag_table(band_bins, SAMPLES, LAGS)
    lag_norm = 1.0 / math.sqrt(WINDOWS * BINS)

    def owner(index):
        own_block = lax.dynamic_index_in_dim(whitened, index, 0, keepdims=False).astype(jnp.float32)
        lag_list = []
        for pair_slot in range(PAIRS):
            partner_index = pair_blocks[index, pair_slot].astype(jnp.int32)
            partner = lax.dynamic_index_in_dim(whitened, partner_index, 0, keepdims=False).astype(jnp.float32)
            cross_gram = gram_pair(own_block, partner)
            lagged = jnp.dot(cross_gram.reshape(CH_DEV * CH_DEV, 2 * BINS), lag_matrix, precision=lax.Precision.HIGHEST, preferred_element_type=jnp.float32) * lag_norm
            lag_list.append(lagged.reshape(CH_DEV, CH_DEV, LAGS))
        return jnp.stack(lag_list, 1)
    return lax.map(owner, jnp.arange(N_CHAN, dtype=jnp.int32))
```

```python
import math

import jax
import jax.numpy as jnp
import numpy as np
from jax import lax
from jax.experimental import pallas as pl
from jax.experimental.pallas import tpu as pltpu
from jax.sharding import PartitionSpec as P

LAGS = 128
REACH = 3
GROUP = 8


def shifted(value, axis, by):
    size = lax.axis_size(axis)
    pairs = [(i, i + by) for i in range(size) if 0 <= i + by < size]
    return lax.ppermute(value, axis, pairs)


def make_dft_table(band_bins, length):
    sample_idx = jnp.arange(length, dtype=jnp.int32)
    phase_int = band_bins[:, None] * sample_idx[None, :] % length
    phases = phase_int.astype(jnp.float32) * (2.0 * math.pi / length)
    return jnp.concatenate([jnp.cos(phases), -jnp.sin(phases)], 0).T.astype(jnp.bfloat16)


def make_lag_table(band_bins, length, lag_count):
    lag_idx = jnp.arange(lag_count, dtype=jnp.int32) - lag_count // 2
    phase_int = band_bins[:, None] * lag_idx[None, :] % length
    phases = phase_int.astype(jnp.float32) * (2.0 * math.pi / length)
    return jnp.concatenate([jnp.cos(phases), -jnp.sin(phases)], 0)


def gram_pair(first_block, second_block):
    rotated = jnp.stack([-second_block[:, :, 1], second_block[:, :, 0]], 2)
    gram_real = jnp.einsum(
        "awcf,bwcf->abf", first_block, second_block, preferred_element_type=jnp.float32
    )
    gram_imag = jnp.einsum(
        "awcf,bwcf->abf", first_block, rotated, preferred_element_type=jnp.float32
    )
    return jnp.stack([gram_real, gram_imag], 2)


def on_any_device(traces, band_bins, pair_blocks):
    channels, windows, length = traces.shape
    band_count = band_bins.shape[0]
    dft_matrix = make_dft_table(band_bins, length)
    spectra = jnp.dot(
        traces.reshape(channels * windows, length), dft_matrix, preferred_element_type=jnp.float32
    )
    amplitude = jnp.sqrt(jnp.sum(spectra * spectra, axis=1, keepdims=True) / band_count + 1e-06)
    whitened = (spectra / amplitude).astype(jnp.bfloat16).reshape(channels, windows, 2, band_count)
    own_block = lax.all_to_all(whitened, "freq", split_axis=3, concat_axis=1, tiled=True)
    below_blocks = [shifted(own_block, "chan", distance) for distance in range(1, REACH + 1)]
    above_blocks = [shifted(own_block, "chan", -distance) for distance in range(1, REACH + 1)]
    stacked = jnp.stack(below_blocks[::-1] + [own_block] + above_blocks, 0)
    my_index = lax.axis_index("chan")
    gram_list = []
    for pair_slot in range(pair_blocks.shape[1]):
        offset = pair_blocks[0, pair_slot] - my_index + REACH
        partner = lax.dynamic_index_in_dim(stacked, offset, 0, keepdims=False)
        gram_list.append(gram_pair(own_block, partner))
    cross_gram = jnp.stack(gram_list, 1)
    lag_matrix = make_lag_table(band_bins, length, LAGS)
    lag_norm = 1.0 / math.sqrt(own_block.shape[1] * band_count)
    gram_block = lax.all_to_all(cross_gram, "freq", split_axis=0, concat_axis=4, tiled=True)
    dims_shape = gram_block.shape
    lagged = (
        jnp.dot(
            gram_block.reshape(-1, 2 * band_count),
            lag_matrix,
            precision=lax.Precision.HIGHEST,
            preferred_element_type=jnp.float32,
        )
        * lag_norm
    )
    result = lagged.reshape(dims_shape[0], dims_shape[1], dims_shape[2], LAGS)
    return result[None]


def spectra_kernel(traces_ref, fine_cos, fine_sin, step_cos, step_sin, out_ref, table, planes):
    bins = fine_cos.shape[0]
    fine = fine_cos.shape[1]
    channels = out_ref.shape[1]
    windows = traces_ref.shape[0] // channels
    for h in range(step_cos.shape[1]):
        sc, ss = step_cos[:, h : h + 1], step_sin[:, h : h + 1]
        cols = slice(h * fine, (h + 1) * fine)
        table[:bins, cols] = (sc * fine_cos[...] - ss * fine_sin[...]).astype(jnp.bfloat16)
        table[bins:, cols] = (-(ss * fine_cos[...] + sc * fine_sin[...])).astype(jnp.bfloat16)
    for half in range(windows // 2):
        rows = traces_ref[half * 2 * channels : (half + 1) * 2 * channels, :]
        spectra = lax.dot_general(
            table[...], rows, (((1,), (1,)), ((), ())), preferred_element_type=jnp.float32
        )
        power = jnp.sum(spectra * spectra, axis=0, keepdims=True)
        white = spectra / jnp.sqrt(power / bins + 1e-06)
        for w in range(2):
            for c in range(2):
                planes[pl.ds((half * 2 + w) * 2 + c, bins, stride=2 * windows), :] = white[
                    c * bins : (c + 1) * bins, w * channels : (w + 1) * channels
                ]
    out_ref[...] = planes[...].astype(jnp.bfloat16)


def make_slab(traces, band_bins):
    channels, windows, length = traces.shape
    bins = band_bins.shape[0]
    fine = 128
    rows = traces.transpose(1, 0, 2).reshape(windows * channels, length)
    sample_idx = jnp.concatenate([jnp.arange(fine), jnp.arange(length // fine) * fine])
    phase_int = band_bins[:, None] * sample_idx[None, :].astype(jnp.int32) % length
    phases = phase_int.astype(jnp.float32) * (2.0 * math.pi / length)
    cos, sin = jnp.cos(phases), jnp.sin(phases)
    return pl.pallas_call(
        spectra_kernel,
        out_shape=jax.ShapeDtypeStruct((bins * windows * 2, channels), jnp.bfloat16),
        scratch_shapes=[
            pltpu.VMEM((2 * bins, length), jnp.bfloat16),
            pltpu.VMEM((bins * windows * 2, channels), jnp.float32),
        ],
        compiler_params=pltpu.CompilerParams(vmem_limit_bytes=48 << 20),
        name="spectra",
    )(rows, cos[:, :fine], sin[:, :fine], cos[:, fine:], sin[:, fine:])


def pairs_kernel(slots, left_ref, lag_ref, *refs, parts, gram_steps, norm):
    n_in = 2 * len(parts)
    sources, out_ref, partner, gram, sems = refs[:n_in], *refs[n_in:]
    step = pl.program_id(0)
    per_step, m, k = left_ref.shape
    slot_count = partner.shape[0]
    channels = partner.shape[3]
    held = sources[0].shape[0]
    group_rows = k // partner.shape[1]

    def copies(act):
        for s in range(slot_count):
            first = 0
            for p, count in enumerate(parts):
                dst = partner.at[s, first : first + count]
                sem = sems.at[s, p]

                @pl.when(slots[s] < held)
                def _():
                    act(pltpu.make_async_copy(sources[2 * p].at[slots[s]], dst, sem))

                @pl.when(slots[s] >= held)
                def _():
                    act(pltpu.make_async_copy(sources[2 * p + 1].at[slots[s] - held], dst, sem))

                first += count

    @pl.when(step == 0)
    def _():
        copies(lambda c: c.start())
        copies(lambda c: c.wait())

    @pl.when(step < gram_steps)
    def _():
        for u in range(per_step):
            g = step * per_step + u
            rows = pl.ds(pl.multiple_of(g * group_rows, group_rows), group_rows)
            right = jnp.concatenate(
                [partner[s, :, rows, :].reshape(k, channels) for s in range(slot_count)], 1
            )
            product = jnp.dot(left_ref[u], right, preferred_element_type=jnp.float32)
            cols = pl.ds(pl.multiple_of(g * 2 * GROUP, 2 * GROUP), 2 * GROUP)
            gram[:, cols, :] = product.astype(jnp.bfloat16).reshape(
                m // (2 * GROUP), 2 * GROUP, slot_count * channels
            )

    @pl.when(step >= gram_steps)
    def _():
        per_lag = out_ref.shape[0]
        for u in range(per_lag):
            a = (step - gram_steps) * per_lag + u
            lagged = (
                jnp.dot(lag_ref[...], gram[a], preferred_element_type=jnp.float32) * norm
            )
            for s in range(slot_count):
                out_ref[u, s] = lagged[:, s * channels : (s + 1) * channels].T


def correlate(slots, left, lag_rows, sources, parts, norm):
    groups, m, k = left.shape
    rows_out = m // (2 * GROUP)
    slot_count = slots.shape[0]
    channels = sources[0].shape[-1]
    slab_rows = sources[0].shape[-2]
    lag_count, entries = lag_rows.shape
    per_step, per_lag = 2, 2
    gram_steps = groups // per_step
    any_spec = pl.BlockSpec(memory_space=pl.ANY)
    return pl.pallas_call(
        lambda *r: pairs_kernel(*r, parts=parts, gram_steps=gram_steps, norm=norm),
        grid_spec=pltpu.PrefetchScalarGridSpec(
            num_scalar_prefetch=1,
            grid=(gram_steps + rows_out // per_lag,),
            in_specs=[
                pl.BlockSpec((per_step, m, k), lambda i, s: (jnp.minimum(i, gram_steps - 1), 0, 0)),
                pl.BlockSpec((lag_count, entries), lambda i, s: (0, 0)),
            ]
            + [any_spec] * len(sources),
            out_specs=pl.BlockSpec(
                (per_lag, slot_count, channels, lag_count),
                lambda i, s: (jnp.maximum(i - gram_steps, 0), 0, 0, 0),
            ),
            scratch_shapes=[
                pltpu.VMEM((slot_count, sum(parts), slab_rows, channels), jnp.bfloat16),
                pltpu.VMEM((rows_out, entries, slot_count * channels), jnp.bfloat16),
                pltpu.SemaphoreType.DMA((slot_count, len(parts))),
            ],
        ),
        out_shape=jax.ShapeDtypeStruct((rows_out, slot_count, channels, lag_count), jnp.float32),
        compiler_params=pltpu.CompilerParams(vmem_limit_bytes=56 << 20),
        name="pairs",
    )(slots, left, lag_rows, *sources)


def make_left(own, row_index, rows_out):
    slabs, slab_rows, channels = own.shape
    mine = lax.dynamic_slice_in_dim(own, row_index * rows_out, rows_out, 2)
    per_bin = slab_rows // 256
    groups = 256 // GROUP
    mine = mine.reshape(slabs, groups, GROUP, per_bin // 2, 2, rows_out)
    rotated = jnp.stack([mine[:, :, :, :, 1], -mine[:, :, :, :, 0]], 4)
    both = jnp.stack([mine, rotated], 0).reshape(2, slabs, groups, GROUP, per_bin, rows_out)
    both = both.transpose(2, 5, 0, 1, 3, 4)
    eye = jnp.eye(GROUP, dtype=jnp.bfloat16)
    left = both[:, :, None] * eye[None, None, :, None, None, :, None]
    return left.reshape(groups, rows_out * GROUP * 2, slabs * GROUP * per_bin)


X_PAIRS = [(i, i ^ 2) for i in range(8)]
Y_PAIRS = [(4, 0), (1, 5), (6, 2), (3, 7)]
YX_PAIRS = [(6, 2), (7, 3), (0, 4), (1, 5)]
CORE_PAIRS = [(i, i ^ 1) for i in range(8)]


def held_blocks():
    table = np.full((8, 8), -1, np.int32)
    for i in range(8):
        table[i, 0] = i
        table[i, 1] = i ^ 2
    for src, dst in Y_PAIRS:
        table[dst, 2] = src
    for src, dst in YX_PAIRS:
        table[dst, 3] = src ^ 2
    for i in range(8):
        table[i, 4:] = table[i ^ 1, :4]
    return table


def spread(part):
    across_x = lax.ppermute(part, "chan", X_PAIRS)
    across_y = lax.ppermute(part, "chan", Y_PAIRS)
    across_both = lax.ppermute(across_x, "chan", YX_PAIRS)
    held = jnp.stack([part, across_x, across_y, across_both], 0)
    return held, lax.ppermute(held, "chan", CORE_PAIRS)


def on_device(traces, band_bins, pair_blocks):
    channels, windows, length = traces.shape
    bins = band_bins.shape[0]
    z = lax.axis_index("freq")
    me = lax.axis_index("chan")
    slab = make_slab(traces, band_bins)

    up1 = lax.ppermute(slab, "freq", [(0, 1), (1, 2), (2, 3)])
    down1 = lax.ppermute(slab, "freq", [(3, 2), (2, 1), (1, 0)])
    up2 = lax.ppermute(up1, "freq", [(1, 2), (2, 3)])
    down2 = lax.ppermute(down1, "freq", [(2, 1), (1, 0)])
    up3 = lax.ppermute(up2, "freq", [(2, 3)])
    down3 = lax.ppermute(down2, "freq", [(1, 0)])

    def choose(*options):
        return lax.select_n(z, *options)

    part0 = slab[None]
    part1 = choose(down1, up1, down1, up1)[None]
    part2 = jnp.stack([choose(down2, down1, up1, up2), choose(down3, down2, up2, up3)], 0)
    sources = []
    for part in (part0, part1, part2):
        sources += spread(part)

    own = jnp.concatenate([part0, part1, part2], 0)
    left = make_left(own, z, channels // 4)
    lag_rows = make_lag_table(band_bins, length, LAGS)
    lag_rows = lag_rows.reshape(2, bins, LAGS).transpose(2, 1, 0).reshape(LAGS, 2 * bins)
    table = jnp.asarray(held_blocks())[me]
    slots = jnp.argmax(table[None, :] == pair_blocks[0][:, None], axis=1).astype(jnp.int32)
    norm = 1.0 / math.sqrt(4 * windows * bins)
    result = correlate(slots, left, lag_rows.astype(jnp.bfloat16), sources, (1, 1, 2), norm)
    return result[None]


def solution(mesh):
    placed = (P("chan", "freq", None), P(), P("chan", None))
    fits = mesh.shape["chan"] == 8 and mesh.shape["freq"] == 4
    return jax.shard_map(
        on_device if fits else on_any_device,
        mesh=mesh,
        in_specs=placed,
        out_specs=P("chan", "freq", None, None, None),
        check_vma=False,
    )
```

```python
import math

import jax
import jax.numpy as jnp
import numpy as np
from jax import lax
from jax.experimental import pallas as pl
from jax.experimental.pallas import tpu as pltpu
from jax.sharding import PartitionSpec as P

LAGS = 128
REACH = 3
GROUP = 8


def shifted(value, axis, by):
    size = lax.axis_size(axis)
    pairs = [(i, i + by) for i in range(size) if 0 <= i + by < size]
    return lax.ppermute(value, axis, pairs)


def make_dft_table(band_bins, length):
    sample_idx = jnp.arange(length, dtype=jnp.int32)
    phase_int = band_bins[:, None] * sample_idx[None, :] % length
    phases = phase_int.astype(jnp.float32) * (2.0 * math.pi / length)
    return jnp.concatenate([jnp.cos(phases), -jnp.sin(phases)], 0).T.astype(jnp.bfloat16)


def make_lag_table(band_bins, length, lag_count):
    lag_idx = jnp.arange(lag_count, dtype=jnp.int32) - lag_count // 2
    phase_int = band_bins[:, None] * lag_idx[None, :] % length
    phases = phase_int.astype(jnp.float32) * (2.0 * math.pi / length)
    return jnp.concatenate([jnp.cos(phases), -jnp.sin(phases)], 0)


def gram_pair(first_block, second_block):
    rotated = jnp.stack([-second_block[:, :, 1], second_block[:, :, 0]], 2)
    gram_real = jnp.einsum(
        "awcf,bwcf->abf", first_block, second_block, preferred_element_type=jnp.float32
    )
    gram_imag = jnp.einsum(
        "awcf,bwcf->abf", first_block, rotated, preferred_element_type=jnp.float32
    )
    return jnp.stack([gram_real, gram_imag], 2)


def on_any_device(traces, band_bins, pair_blocks):
    channels, windows, length = traces.shape
    band_count = band_bins.shape[0]
    dft_matrix = make_dft_table(band_bins, length)
    spectra = jnp.dot(
        traces.reshape(channels * windows, length), dft_matrix, preferred_element_type=jnp.float32
    )
    amplitude = jnp.sqrt(jnp.sum(spectra * spectra, axis=1, keepdims=True) / band_count + 1e-06)
    whitened = (spectra / amplitude).astype(jnp.bfloat16).reshape(channels, windows, 2, band_count)
    own_block = lax.all_to_all(whitened, "freq", split_axis=3, concat_axis=1, tiled=True)
    below_blocks = [shifted(own_block, "chan", distance) for distance in range(1, REACH + 1)]
    above_blocks = [shifted(own_block, "chan", -distance) for distance in range(1, REACH + 1)]
    stacked = jnp.stack(below_blocks[::-1] + [own_block] + above_blocks, 0)
    my_index = lax.axis_index("chan")
    gram_list = []
    for pair_slot in range(pair_blocks.shape[1]):
        offset = pair_blocks[0, pair_slot] - my_index + REACH
        partner = lax.dynamic_index_in_dim(stacked, offset, 0, keepdims=False)
        gram_list.append(gram_pair(own_block, partner))
    cross_gram = jnp.stack(gram_list, 1)
    lag_matrix = make_lag_table(band_bins, length, LAGS)
    lag_norm = 1.0 / math.sqrt(own_block.shape[1] * band_count)
    gram_block = lax.all_to_all(cross_gram, "freq", split_axis=0, concat_axis=4, tiled=True)
    dims_shape = gram_block.shape
    lagged = (
        jnp.dot(
            gram_block.reshape(-1, 2 * band_count),
            lag_matrix,
            precision=lax.Precision.HIGHEST,
            preferred_element_type=jnp.float32,
        )
        * lag_norm
    )
    result = lagged.reshape(dims_shape[0], dims_shape[1], dims_shape[2], LAGS)
    return result[None]


def spectra_kernel(traces_ref, fine_cos, fine_sin, step_cos, step_sin, out_ref, table, planes):
    bins, fine = fine_cos.shape
    groups, _, channels = planes.shape
    windows = traces_ref.shape[0] // channels
    for h in range(step_cos.shape[1]):
        sc, ss = step_cos[:, h : h + 1], step_sin[:, h : h + 1]
        cols = slice(h * fine, (h + 1) * fine)
        table[:bins, cols] = (sc * fine_cos[...] - ss * fine_sin[...]).astype(jnp.bfloat16)
        table[bins:, cols] = (-(ss * fine_cos[...] + sc * fine_sin[...])).astype(jnp.bfloat16)
    for half in range(windows // 2):
        rows = traces_ref[half * 2 * channels : (half + 1) * 2 * channels, :]
        spectra = lax.dot_general(
            table[...], rows, (((1,), (1,)), ((), ())), preferred_element_type=jnp.float32
        )
        power = jnp.sum(spectra * spectra, axis=0, keepdims=True)
        white = spectra / jnp.sqrt(power / bins + 1e-06)
        for w in range(2):
            for c in range(2):
                first = c * GROUP * windows + half * 2 + w
                planes[:, pl.ds(first, GROUP, stride=windows), :] = white[
                    c * bins : (c + 1) * bins, w * channels : (w + 1) * channels
                ].reshape(groups, GROUP, channels)
    out_ref[...] = planes[...].reshape(out_ref.shape).astype(jnp.bfloat16)


def make_slab(traces, band_bins):
    channels, windows, length = traces.shape
    bins = band_bins.shape[0]
    fine = 128
    rows = traces.transpose(1, 0, 2).reshape(windows * channels, length)
    sample_idx = jnp.concatenate([jnp.arange(fine), jnp.arange(length // fine) * fine])
    phase_int = band_bins[:, None] * sample_idx[None, :].astype(jnp.int32) % length
    phases = phase_int.astype(jnp.float32) * (2.0 * math.pi / length)
    cos, sin = jnp.cos(phases), jnp.sin(phases)
    return pl.pallas_call(
        spectra_kernel,
        out_shape=jax.ShapeDtypeStruct((bins * windows * 2, channels), jnp.bfloat16),
        scratch_shapes=[
            pltpu.VMEM((2 * bins, length), jnp.bfloat16),
            pltpu.VMEM((bins // GROUP, GROUP * windows * 2, channels), jnp.float32),
        ],
        compiler_params=pltpu.CompilerParams(vmem_limit_bytes=48 << 20),
        name="spectra",
    )(rows, cos[:, :fine], sin[:, :fine], cos[:, fine:], sin[:, fine:])


def left_kernel(z, *refs, per_step):
    slabs, (out_ref, choice, mask) = refs[:-3], refs[-3:]
    m, k = mask.shape
    channels = slabs[0].shape[1]
    group_rows = k // len(slabs)
    half = group_rows // 2
    rows_out = m // (2 * GROUP)

    @pl.when(pl.program_id(0) == 0)
    def _():
        row = lax.broadcasted_iota(jnp.int32, (m, 2 * channels), 0)
        col = lax.broadcasted_iota(jnp.int32, (m, 2 * channels), 1)
        wanted = row // (2 * GROUP) + z[0] * rows_out + (row % 2) * channels
        choice[...] = jnp.where(col == wanted, 1.0, 0.0).astype(jnp.bfloat16)
        row = lax.broadcasted_iota(jnp.int32, (m, k), 0)
        col = lax.broadcasted_iota(jnp.int32, (m, k), 1)
        bin_of_col = col % half // (half // GROUP)
        mask[...] = jnp.where(bin_of_col == row // 2 % GROUP, 1.0, 0.0)

    for u in range(per_step):
        pieces = []
        for slab in slabs:
            real = slab[u * group_rows : u * group_rows + half, :]
            imag = slab[u * group_rows + half : (u + 1) * group_rows, :]
            pieces.append(jnp.concatenate([real, imag], 1))
            pieces.append(jnp.concatenate([imag, -real], 1))
        both = jnp.concatenate(pieces, 0)
        rows = lax.dot_general(
            choice[...], both, (((1,), (1,)), ((), ())), preferred_element_type=jnp.float32
        )
        out_ref[u] = (rows * mask[...]).astype(jnp.bfloat16)


def make_left(slabs, z, rows_out, bins):
    slab_rows, channels = slabs[0].shape
    groups = bins // GROUP
    m, k = rows_out * GROUP * 2, slab_rows // groups * len(slabs)
    per_step = 4
    return pl.pallas_call(
        lambda *r: left_kernel(*r, per_step=per_step),
        grid_spec=pltpu.PrefetchScalarGridSpec(
            num_scalar_prefetch=1,
            grid=(groups // per_step,),
            in_specs=[
                pl.BlockSpec((slab_rows // groups * per_step, channels), lambda i, s: (i, 0))
            ]
            * len(slabs),
            out_specs=pl.BlockSpec((per_step, m, k), lambda i, s: (i, 0, 0)),
            scratch_shapes=[
                pltpu.VMEM((m, 2 * channels), jnp.bfloat16),
                pltpu.VMEM((m, k), jnp.float32),
            ],
        ),
        out_shape=jax.ShapeDtypeStruct((groups, m, k), jnp.bfloat16),
        compiler_params=pltpu.CompilerParams(vmem_limit_bytes=32 << 20),
        name="left",
    )(z.reshape(1), *slabs)


def pairs_kernel(slots, left_ref, lag_ref, *refs, parts, gram_steps, norm):
    n_in = sum(len(part) for part in parts)
    sources, (out_ref, partner, gram, sems) = refs[:n_in], refs[n_in:]
    step = pl.program_id(0)
    per_step, m, k = left_ref.shape
    slot_count = partner.shape[0]
    channels = partner.shape[3]
    group_rows = k // partner.shape[1]

    def copies(act):
        for s in range(slot_count):
            ref = 0
            for r, part in enumerate(parts):
                slot = slots[s * len(parts) + r]
                first = 0
                for count in part:

                    @pl.when((slot >= first) & (slot < first + count))
                    def _():
                        source = sources[ref].at[slot - first]
                        act(pltpu.make_async_copy(source, partner.at[s, r], sems.at[s, r]))

                    first += count
                    ref += 1

    @pl.when(step == 0)
    def _():
        copies(lambda c: c.start())
        copies(lambda c: c.wait())

    @pl.when(step < gram_steps)
    def _():
        for u in range(per_step):
            g = step * per_step + u
            rows = pl.ds(pl.multiple_of(g * group_rows, group_rows), group_rows)
            right = jnp.concatenate(
                [partner[s, :, rows, :].reshape(k, channels) for s in range(slot_count)], 1
            )
            product = jnp.dot(left_ref[u], right, preferred_element_type=jnp.float32)
            cols = pl.ds(pl.multiple_of(g * 2 * GROUP, 2 * GROUP), 2 * GROUP)
            gram[:, cols, :] = product.astype(jnp.bfloat16).reshape(
                m // (2 * GROUP), 2 * GROUP, slot_count * channels
            )

    @pl.when(step >= gram_steps)
    def _():
        per_lag = out_ref.shape[0]
        for u in range(per_lag):
            a = (step - gram_steps) * per_lag + u
            lagged = (
                jnp.dot(lag_ref[...], gram[a], preferred_element_type=jnp.float32) * norm
            )
            for s in range(slot_count):
                out_ref[u, s] = lagged[:, s * channels : (s + 1) * channels].T


def correlate(slots, left, lag_rows, sources, slot_count, norm):
    groups, m, k = left.shape
    rows_out = m // (2 * GROUP)
    parts = [[value.shape[0] for value in part] for part in sources]
    flat = [value for part in sources for value in part]
    slab_rows, channels = flat[0].shape[1:]
    lag_count, entries = lag_rows.shape
    per_step, per_lag = 2, 2
    gram_steps = groups // per_step
    return pl.pallas_call(
        lambda *r: pairs_kernel(*r, parts=parts, gram_steps=gram_steps, norm=norm),
        grid_spec=pltpu.PrefetchScalarGridSpec(
            num_scalar_prefetch=1,
            grid=(gram_steps + rows_out // per_lag,),
            in_specs=[
                pl.BlockSpec((per_step, m, k), lambda i, s: (jnp.minimum(i, gram_steps - 1), 0, 0)),
                pl.BlockSpec((lag_count, entries), lambda i, s: (0, 0)),
            ]
            + [pl.BlockSpec(memory_space=pl.ANY)] * len(flat),
            out_specs=pl.BlockSpec(
                (per_lag, slot_count, channels, lag_count),
                lambda i, s: (jnp.maximum(i - gram_steps, 0), 0, 0, 0),
            ),
            scratch_shapes=[
                pltpu.VMEM((slot_count, len(parts), slab_rows, channels), jnp.bfloat16),
                pltpu.VMEM((rows_out, entries, slot_count * channels), jnp.bfloat16),
                pltpu.SemaphoreType.DMA((slot_count, len(parts))),
            ],
        ),
        out_shape=jax.ShapeDtypeStruct((rows_out, slot_count, channels, lag_count), jnp.float32),
        compiler_params=pltpu.CompilerParams(vmem_limit_bytes=56 << 20),
        name="pairs",
    )(slots, left, lag_rows, *flat)


X_PAIRS = [(i, i ^ 2) for i in range(8)]
Y_PAIRS = [(4, 0), (1, 5), (6, 2), (3, 7)]
X_ON = [(0, 2), (7, 5)]
Y_ON = [(7, 3), (0, 4)]
Y_ON_ALL = Y_ON + [(6, 2), (1, 5)]
CORE_PAIRS = [(i, i ^ 1) for i in range(8)]


def hop(entry, pairs):
    value, ids = entry
    moved = np.full_like(ids, -1)
    for src, dst in pairs:
        moved[:, dst] = ids[:, src]
    return lax.ppermute(value, "chan", pairs), moved


def join(*entries):
    values, ids = zip(*entries)
    return jnp.concatenate(values, 0), np.concatenate(ids, 0)


def together(*entries):
    values = lax.optimization_barrier(tuple(value for value, _ in entries))
    return [(value, ids) for value, (_, ids) in zip(values, entries)]


def on_device(traces, band_bins, pair_blocks):
    channels, windows, length = traces.shape
    bins = band_bins.shape[0]
    z = lax.axis_index("freq")
    me = lax.axis_index("chan")
    own = np.arange(8)[None]

    def along_z(entry, pairs):
        return lax.ppermute(entry[0], "freq", pairs), entry[1]

    def choose(*entries):
        return lax.select_n(z, *[value for value, _ in entries]), entries[0][1]

    lag_rows = make_lag_table(band_bins, length, LAGS)
    lag_rows = lag_rows.reshape(2, bins, LAGS).transpose(2, 1, 0).reshape(LAGS, 2 * bins)
    lag_rows = lag_rows.astype(jnp.bfloat16)
    q0 = make_slab(traces, band_bins)[None], own

    up1, down1 = along_z(q0, [(0, 1), (1, 2), (2, 3)]), along_z(q0, [(3, 2), (2, 1), (1, 0)])
    x0, y0 = hop(q0, X_PAIRS), hop(q0, Y_PAIRS)
    up1, down1, x0, y0 = together(up1, down1, x0, y0)

    q1 = choose(down1, up1, down1, up1)
    up2, down2 = along_z(up1, [(1, 2), (2, 3)]), along_z(down1, [(2, 1), (1, 0)])
    x1, y1, c0 = hop(q1, X_PAIRS), hop(q1, Y_PAIRS), hop(x0, Y_ON_ALL)
    up2, down2, x1, y1, c0 = together(up2, down2, x1, y1, c0)

    q2 = choose(down2, down1, up1, up2)
    up3, down3 = along_z(up2, [(2, 3)]), along_z(down2, [(1, 0)])
    x2, y2, c1 = hop(q2, X_PAIRS), hop(q2, Y_PAIRS), hop(x1, Y_ON_ALL)
    other0 = hop(join(q0, x0, y0, c0), CORE_PAIRS)
    up3, down3, x2, y2, c1, other0 = together(up3, down3, x2, y2, c1, other0)

    q3 = choose(down3, down2, up2, up3)
    x3, y3, c2 = hop(q3, X_PAIRS), hop(q3, Y_PAIRS), hop(x2, Y_ON_ALL)
    other1 = hop(join(q1, x1, y1, c1), CORE_PAIRS)
    left = make_left([q[0][0] for q in (q0, q1, q2, q3)], z, channels // 4, bins)
    x3, y3, c2, other1, (left, _) = together(x3, y3, c2, other1, (left, None))

    c3, d3 = hop(x3, Y_ON), hop(y3, X_ON)
    other2, other3 = hop(join(q2, x2, y2, c2), CORE_PAIRS), hop(join(q3, x3, y3), CORE_PAIRS)
    c3, d3, other2, other3 = together(c3, d3, other2, other3)
    late3 = hop(join(c3, d3), CORE_PAIRS)

    held = [
        [q0, x0, y0, c0, other0],
        [q1, x1, y1, c1, other1],
        [q2, x2, y2, c2, other2],
        [q3, x3, y3, c3, d3, other3, late3],
    ]
    ids = [np.concatenate([entry[1] for entry in part], 0) for part in held]
    most = max(len(rows) for rows in ids)
    table = np.stack([np.pad(rows, ((0, most - len(rows)), (0, 0)), constant_values=-1) for rows in ids])
    mine = jnp.asarray(table.transpose(2, 0, 1), jnp.int32)[me]
    slots = jnp.argmax(mine[None] == pair_blocks[0][:, None, None], axis=2).astype(jnp.int32)
    norm = 1.0 / math.sqrt(4 * windows * bins)
    result = correlate(
        slots.reshape(-1),
        left,
        lag_rows,
        [[entry[0] for entry in part] for part in held],
        pair_blocks.shape[1],
        norm,
    )
    return result[None]


def solution(mesh):
    placed = (P("chan", "freq", None), P(), P("chan", None))
    fits = mesh.shape["chan"] == 8 and mesh.shape["freq"] == 4
    return jax.shard_map(
        on_device if fits else on_any_device,
        mesh=mesh,
        in_specs=placed,
        out_specs=P("chan", "freq", None, None, None),
        check_vma=False,
    )
```

```python
import math

import jax
import jax.numpy as jnp
import numpy as np
from jax import lax
from jax.experimental import pallas as pl
from jax.experimental.pallas import tpu as pltpu
from jax.sharding import PartitionSpec as P

LAGS = 128
REACH = 3
GROUP = 8


def shifted(value, axis, by):
    size = lax.axis_size(axis)
    pairs = [(i, i + by) for i in range(size) if 0 <= i + by < size]
    return lax.ppermute(value, axis, pairs)


def make_dft_table(band_bins, length):
    sample_idx = jnp.arange(length, dtype=jnp.int32)
    phase_int = band_bins[:, None] * sample_idx[None, :] % length
    phases = phase_int.astype(jnp.float32) * (2.0 * math.pi / length)
    return jnp.concatenate([jnp.cos(phases), -jnp.sin(phases)], 0).T.astype(jnp.bfloat16)


def make_lag_table(band_bins, length, lag_count):
    lag_idx = jnp.arange(lag_count, dtype=jnp.int32) - lag_count // 2
    phase_int = band_bins[:, None] * lag_idx[None, :] % length
    phases = phase_int.astype(jnp.float32) * (2.0 * math.pi / length)
    return jnp.concatenate([jnp.cos(phases), -jnp.sin(phases)], 0)


def gram_pair(first_block, second_block):
    rotated = jnp.stack([-second_block[:, :, 1], second_block[:, :, 0]], 2)
    gram_real = jnp.einsum(
        "awcf,bwcf->abf", first_block, second_block, preferred_element_type=jnp.float32
    )
    gram_imag = jnp.einsum(
        "awcf,bwcf->abf", first_block, rotated, preferred_element_type=jnp.float32
    )
    return jnp.stack([gram_real, gram_imag], 2)


def on_any_device(traces, band_bins, pair_blocks):
    channels, windows, length = traces.shape
    band_count = band_bins.shape[0]
    dft_matrix = make_dft_table(band_bins, length)
    spectra = jnp.dot(
        traces.reshape(channels * windows, length), dft_matrix, preferred_element_type=jnp.float32
    )
    amplitude = jnp.sqrt(jnp.sum(spectra * spectra, axis=1, keepdims=True) / band_count + 1e-06)
    whitened = (spectra / amplitude).astype(jnp.bfloat16).reshape(channels, windows, 2, band_count)
    own_block = lax.all_to_all(whitened, "freq", split_axis=3, concat_axis=1, tiled=True)
    below_blocks = [shifted(own_block, "chan", distance) for distance in range(1, REACH + 1)]
    above_blocks = [shifted(own_block, "chan", -distance) for distance in range(1, REACH + 1)]
    stacked = jnp.stack(below_blocks[::-1] + [own_block] + above_blocks, 0)
    my_index = lax.axis_index("chan")
    gram_list = []
    for pair_slot in range(pair_blocks.shape[1]):
        offset = pair_blocks[0, pair_slot] - my_index + REACH
        partner = lax.dynamic_index_in_dim(stacked, offset, 0, keepdims=False)
        gram_list.append(gram_pair(own_block, partner))
    cross_gram = jnp.stack(gram_list, 1)
    lag_matrix = make_lag_table(band_bins, length, LAGS)
    lag_norm = 1.0 / math.sqrt(own_block.shape[1] * band_count)
    gram_block = lax.all_to_all(cross_gram, "freq", split_axis=0, concat_axis=4, tiled=True)
    dims_shape = gram_block.shape
    lagged = (
        jnp.dot(
            gram_block.reshape(-1, 2 * band_count),
            lag_matrix,
            precision=lax.Precision.HIGHEST,
            preferred_element_type=jnp.float32,
        )
        * lag_norm
    )
    result = lagged.reshape(dims_shape[0], dims_shape[1], dims_shape[2], LAGS)
    return result[None]


def spectra_kernel(traces_ref, fine_cos, fine_sin, step_cos, step_sin, out_ref, table, planes):
    bins, fine = fine_cos.shape
    groups, _, channels = planes.shape
    windows = traces_ref.shape[0] // channels
    for h in range(step_cos.shape[1]):
        sc, ss = step_cos[:, h : h + 1], step_sin[:, h : h + 1]
        cols = slice(h * fine, (h + 1) * fine)
        table[:bins, cols] = (sc * fine_cos[...] - ss * fine_sin[...]).astype(jnp.bfloat16)
        table[bins:, cols] = (-(ss * fine_cos[...] + sc * fine_sin[...])).astype(jnp.bfloat16)
    for half in range(windows // 2):
        rows = traces_ref[half * 2 * channels : (half + 1) * 2 * channels, :]
        spectra = lax.dot_general(
            table[...], rows, (((1,), (1,)), ((), ())), preferred_element_type=jnp.float32
        )
        power = jnp.sum(spectra * spectra, axis=0, keepdims=True)
        white = spectra / jnp.sqrt(power / bins + 1e-06)
        for w in range(2):
            for c in range(2):
                first = c * GROUP * windows + half * 2 + w
                planes[:, pl.ds(first, GROUP, stride=windows), :] = white[
                    c * bins : (c + 1) * bins, w * channels : (w + 1) * channels
                ].reshape(groups, GROUP, channels)
    out_ref[...] = planes[...].reshape(out_ref.shape).astype(jnp.bfloat16)


def make_slab(traces, band_bins):
    channels, windows, length = traces.shape
    bins = band_bins.shape[0]
    fine = 128
    rows = traces.transpose(1, 0, 2).reshape(windows * channels, length)
    sample_idx = jnp.concatenate([jnp.arange(fine), jnp.arange(length // fine) * fine])
    phase_int = band_bins[:, None] * sample_idx[None, :].astype(jnp.int32) % length
    phases = phase_int.astype(jnp.float32) * (2.0 * math.pi / length)
    cos, sin = jnp.cos(phases), jnp.sin(phases)
    return pl.pallas_call(
        spectra_kernel,
        out_shape=jax.ShapeDtypeStruct((bins * windows * 2, channels), jnp.bfloat16),
        scratch_shapes=[
            pltpu.VMEM((2 * bins, length), jnp.bfloat16),
            pltpu.VMEM((bins // GROUP, GROUP * windows * 2, channels), jnp.float32),
        ],
        compiler_params=pltpu.CompilerParams(vmem_limit_bytes=48 << 20),
        name="spectra",
    )(rows, cos[:, :fine], sin[:, :fine], cos[:, fine:], sin[:, fine:])


def left_kernel(z, *refs, per_step):
    slabs, (out_ref, choice, mask) = refs[:-3], refs[-3:]
    m, k = mask.shape
    channels = slabs[0].shape[1]
    group_rows = k // len(slabs)
    half = group_rows // 2
    rows_out = m // (2 * GROUP)

    @pl.when(pl.program_id(0) == 0)
    def _():
        row = lax.broadcasted_iota(jnp.int32, (m, 2 * channels), 0)
        col = lax.broadcasted_iota(jnp.int32, (m, 2 * channels), 1)
        wanted = row // (2 * GROUP) + z[0] * rows_out + (row % 2) * channels
        choice[...] = jnp.where(col == wanted, 1.0, 0.0).astype(jnp.bfloat16)
        row = lax.broadcasted_iota(jnp.int32, (m, k), 0)
        col = lax.broadcasted_iota(jnp.int32, (m, k), 1)
        bin_of_col = col % half // (half // GROUP)
        mask[...] = jnp.where(bin_of_col == row // 2 % GROUP, 1.0, 0.0)

    for u in range(per_step):
        pieces = []
        for slab in slabs:
            real = slab[u * group_rows : u * group_rows + half, :]
            imag = slab[u * group_rows + half : (u + 1) * group_rows, :]
            pieces.append(jnp.concatenate([real, imag], 1))
            pieces.append(jnp.concatenate([imag, -real], 1))
        both = jnp.concatenate(pieces, 0)
        rows = lax.dot_general(
            choice[...], both, (((1,), (1,)), ((), ())), preferred_element_type=jnp.float32
        )
        out_ref[u] = (rows * mask[...]).astype(jnp.bfloat16)


def make_left(slabs, z, rows_out, bins):
    slab_rows, channels = slabs[0].shape
    groups = bins // GROUP
    m, k = rows_out * GROUP * 2, slab_rows // groups * len(slabs)
    per_step = 4
    return pl.pallas_call(
        lambda *r: left_kernel(*r, per_step=per_step),
        grid_spec=pltpu.PrefetchScalarGridSpec(
            num_scalar_prefetch=1,
            grid=(groups // per_step,),
            in_specs=[
                pl.BlockSpec((slab_rows // groups * per_step, channels), lambda i, s: (i, 0))
            ]
            * len(slabs),
            out_specs=pl.BlockSpec((per_step, m, k), lambda i, s: (i, 0, 0)),
            scratch_shapes=[
                pltpu.VMEM((m, 2 * channels), jnp.bfloat16),
                pltpu.VMEM((m, k), jnp.float32),
            ],
        ),
        out_shape=jax.ShapeDtypeStruct((groups, m, k), jnp.bfloat16),
        compiler_params=pltpu.CompilerParams(vmem_limit_bytes=32 << 20),
        name="left",
    )(z.reshape(1), *slabs)


CHUNKS = 4
GROUP_UNROLL = 4
ROW_UNROLL = 4


def pairs_kernel(slots, left_ref, lag_ref, *refs, arrays, norm):
    sources, (out_ref, partner, gram, stage, in_sems, out_sems) = refs[: len(arrays)], refs[len(arrays) :]
    groups, m, k = left_ref.shape
    slot_count, slabs, slab_rows, channels = partner.shape
    group_rows = k // slabs
    chunk_rows = slab_rows // CHUNKS
    lanes = slot_count * channels

    def fetch(source, s, r, chunk):
        rows = pl.ds(chunk * chunk_rows, chunk_rows)
        return pltpu.make_async_copy(source.at[rows], partner.at[s, r, rows], in_sems.at[chunk, s, r])

    for s in range(slot_count):
        for r in range(slabs):
            slot = slots[s * slabs + r]
            for source, (first, count, holds) in zip(sources, arrays):
                if r in holds:

                    @pl.when((slot >= first) & (slot < first + count))
                    def _():
                        for chunk in range(CHUNKS):
                            fetch(source.at[slot - first], s, r, chunk).start()

    per_chunk = groups // CHUNKS

    for chunk in range(CHUNKS):
        for s in range(slot_count):
            for r in range(slabs):
                fetch(sources[0].at[0], s, r, chunk).wait()

        @pl.loop(0, per_chunk // GROUP_UNROLL)
        def _(i):
            for u in range(GROUP_UNROLL):
                g = chunk * per_chunk + i * GROUP_UNROLL + u
                rows = pl.ds(pl.multiple_of(g * group_rows, group_rows), group_rows)
                right = jnp.concatenate(
                    [partner[s, :, rows, :].reshape(k, channels) for s in range(slot_count)], 1
                )
                product = jnp.dot(left_ref[g], right, preferred_element_type=jnp.float32)
                cols = pl.ds(pl.multiple_of(g * 2 * GROUP, 2 * GROUP), 2 * GROUP)
                gram[:, cols, :] = product.astype(jnp.bfloat16).reshape(
                    m // (2 * GROUP), 2 * GROUP, lanes
                )

    steps = gram.shape[0] // ROW_UNROLL

    def write(i, b):
        return pltpu.make_async_copy(
            stage.at[b], out_ref.at[pl.ds(i * ROW_UNROLL, ROW_UNROLL)], out_sems.at[b]
        )

    @pl.loop(0, steps)
    def _(i):
        b = lax.rem(i, 2)

        @pl.when(i >= 2)
        def _():
            write(i - 2, b).wait()

        for u in range(ROW_UNROLL):
            lagged = jnp.dot(
                lag_ref[...], gram[i * ROW_UNROLL + u], preferred_element_type=jnp.float32
            )
            for s in range(slot_count):
                stage[b, u, s] = (lagged[:, s * channels : (s + 1) * channels] * norm).T
        write(i, b).start()

    for i in range(steps - 2, steps):
        write(i, i % 2).wait()


def correlate(slots, left, lag_rows, held, slot_count, norm):
    groups, m, k = left.shape
    rows_out = m // (2 * GROUP)
    arrays, first = [], 0
    for value, holds in held:
        arrays.append((first, value.shape[0], holds))
        first += value.shape[0]
    slab_rows, channels = held[0][0].shape[1:]
    slabs = slots.shape[0] // slot_count
    lag_count, entries = lag_rows.shape
    anywhere = pl.BlockSpec(memory_space=pl.ANY)
    in_vmem = pl.BlockSpec(memory_space=pltpu.VMEM)
    return pl.pallas_call(
        lambda *r: pairs_kernel(*r, arrays=arrays, norm=norm),
        in_specs=[pl.BlockSpec(memory_space=pltpu.SMEM), in_vmem, in_vmem] + [anywhere] * len(held),
        out_specs=anywhere,
        scratch_shapes=[
            pltpu.VMEM((slot_count, slabs, slab_rows, channels), jnp.bfloat16),
            pltpu.VMEM((rows_out, entries, slot_count * channels), jnp.bfloat16),
            pltpu.VMEM((2, ROW_UNROLL, slot_count, channels, lag_count), jnp.float32),
            pltpu.SemaphoreType.DMA((CHUNKS, slot_count, slabs)),
            pltpu.SemaphoreType.DMA((2,)),
        ],
        out_shape=jax.ShapeDtypeStruct((rows_out, slot_count, channels, lag_count), jnp.float32),
        compiler_params=pltpu.CompilerParams(vmem_limit_bytes=36 << 20),
        name="pairs",
    )(slots, left, lag_rows, *[value for value, _ in held])


X_PAIRS = [(i, i ^ 2) for i in range(8)]
Y_PAIRS = [(4, 0), (1, 5), (6, 2), (3, 7)]
Y_ON = [(7, 3), (0, 4)]
X_ON = [(0, 2), (7, 5)]
CORE_PAIRS = [(i, i ^ 1) for i in range(8)]


def moved(what, pairs):
    after = [[None] * 8 for _ in what]
    for src, dst in pairs:
        for old, new in zip(what, after):
            new[dst] = old[src]
    return after


class Held:
    def __init__(self, value, what):
        self.value, self.what = value, what

    def hop(self, pairs):
        return Held(lax.ppermute(self.value, "chan", pairs), moved(self.what, pairs))


def join(*parts):
    return Held(jnp.concatenate([p.value for p in parts], 0), [w for p in parts for w in p.what])


def where_device(me, devices, first, second):
    here = jnp.asarray(np.isin(np.arange(8), devices))[me]
    what = [
        [one[i] if i in devices else other[i] for i in range(8)]
        for one, other in zip(first.what, second.what)
    ]
    return Held(jnp.where(here, first.value, second.value), what)


def together(*parts):
    return lax.optimization_barrier(parts)


jax.tree_util.register_pytree_node(
    Held,
    lambda held: ((held.value,), tuple(tuple(row) for row in held.what)),
    lambda what, children: Held(children[0], [list(row) for row in what]),
)


def on_device(traces, band_bins, pair_blocks):
    channels, windows, length = traces.shape
    bins = band_bins.shape[0]
    z = lax.axis_index("freq")
    me = lax.axis_index("chan")
    slot_count = pair_blocks.shape[1]

    lag_idx = jnp.arange(LAGS, dtype=jnp.int32) - LAGS // 2
    phases = (lag_idx[:, None] * band_bins[None, :] % length).astype(jnp.float32)
    phases = phases * (2.0 * math.pi / length)
    lag_rows = jnp.stack([jnp.cos(phases), -jnp.sin(phases)], 2).reshape(LAGS, 2 * bins)
    lag_rows = lag_rows.astype(jnp.bfloat16)

    def along_z(value, pairs):
        return lax.ppermute(value, "freq", pairs)

    def slab_of(value, r):
        return Held(value, [[(i, r) for i in range(8)]])

    def over_y(straight, came_over_x):
        mixed = where_device(me, [0, 7], came_over_x, straight)
        return mixed.hop(Y_PAIRS + Y_ON)

    s0 = make_slab(traces, band_bins)[None]
    q0 = slab_of(s0, 0)
    y0 = q0.hop(Y_PAIRS)
    down1, up1 = along_z(s0, [(3, 2), (2, 1), (1, 0)]), along_z(s0, [(0, 1), (1, 2), (2, 3)])
    x0 = q0.hop(X_PAIRS)
    y0, down1, up1, x0, lag_rows = together(y0, down1, up1, x0, lag_rows)

    q1 = slab_of(lax.select_n(z, down1, up1, down1, up1), 1)
    up2, down2 = along_z(up1, [(1, 2), (2, 3)]), along_z(down1, [(2, 1), (1, 0)])
    y1 = over_y(q1, x0)
    e0 = y0.hop(X_ON)
    x1 = q1.hop(X_PAIRS)
    up2, down2, y1, e0, x1 = together(up2, down2, y1, e0, x1)

    q2 = slab_of(lax.select_n(z, down2, down1, up1, up2), 2)
    last = along_z(jnp.where(z == 2, up2, down2), [(2, 3), (1, 0)])
    a = join(q0, x0, y0, q1, x1, y1, e0).hop(CORE_PAIRS)
    y2 = over_y(q2, x1)
    e1 = y1.hop(X_ON)
    x2 = q2.hop(X_PAIRS)
    last, a, y2, e1, x2 = together(last, a, y2, e1, x2)

    q3 = slab_of(lax.select_n(z, last, down2, up2, last), 3)
    b = join(q2, x2, y2, e1).hop(CORE_PAIRS)
    y3 = over_y(q3, x2)
    e2 = y2.hop(X_ON)
    x3 = q3.hop(X_PAIRS)
    left = make_left([q.value[0] for q in (q0, q1, q2, q3)], z, channels // 4, bins)
    b, y3, e2, x3, left = together(b, y3, e2, x3, left)

    c = join(q3, x3, y3, e2).hop(CORE_PAIRS)
    y4, e3 = x3.hop(Y_ON), y3.hop(X_ON)

    held = [q0, q1, q2, q3, x0, x1, x2, x3, y0, y1, y2, y3, y4, e0, e1, e2, e3, a, b, c]
    whats = [h.what for h in held] + [moved(y4.what + e3.what, CORE_PAIRS)]
    table = np.zeros((8, 8, 4), np.int32)
    all_holds = [set() for _ in whats]
    index = sum(len(what) for what in whats)
    for what, holds in zip(reversed(whats), reversed(all_holds)):
        for item in reversed(what):
            index -= 1
            for device, block_slab in enumerate(item):
                if block_slab is not None:
                    table[device, block_slab[0], block_slab[1]] = index
                    holds.add(block_slab[1])
    mine = jnp.asarray(table)[me]
    slots = jnp.concatenate([mine[pair_blocks[0, s]] for s in range(slot_count)])

    y4, e3, c, slots = together(y4, e3, c, slots)
    d = join(y4, e3).hop(CORE_PAIRS)
    held = [q0, q1, q2, q3, x0, x1, x2, x3, y0, y1, y2, y3, y4, e0, e1, e2, e3, a, b, c, d]
    places = [(h.value, holds) for h, holds in zip(held, all_holds)]
    norm = 1.0 / math.sqrt(4 * windows * bins)
    return correlate(slots, left, lag_rows, places, slot_count, norm)[None]


def solution(mesh):
    placed = (P("chan", "freq", None), P(), P("chan", None))
    fits = mesh.shape["chan"] == 8 and mesh.shape["freq"] == 4
    return jax.shard_map(
        on_device if fits else on_any_device,
        mesh=mesh,
        in_specs=placed,
        out_specs=P("chan", "freq", None, None, None),
        check_vma=False,
    )
```

```python
import math

import jax
import jax.numpy as jnp
import numpy as np
from jax import lax
from jax.experimental import pallas as pl
from jax.experimental.pallas import tpu as pltpu
from jax.sharding import PartitionSpec as P

LAGS = 128
REACH = 3
GROUP = 8


def shifted(value, axis, by):
    size = lax.axis_size(axis)
    pairs = [(i, i + by) for i in range(size) if 0 <= i + by < size]
    return lax.ppermute(value, axis, pairs)


def make_dft_table(band_bins, length):
    sample_idx = jnp.arange(length, dtype=jnp.int32)
    phase_int = band_bins[:, None] * sample_idx[None, :] % length
    phases = phase_int.astype(jnp.float32) * (2.0 * math.pi / length)
    return jnp.concatenate([jnp.cos(phases), -jnp.sin(phases)], 0).T.astype(jnp.bfloat16)


def make_lag_table(band_bins, length, lag_count):
    lag_idx = jnp.arange(lag_count, dtype=jnp.int32) - lag_count // 2
    phase_int = band_bins[:, None] * lag_idx[None, :] % length
    phases = phase_int.astype(jnp.float32) * (2.0 * math.pi / length)
    return jnp.concatenate([jnp.cos(phases), -jnp.sin(phases)], 0)


def gram_pair(first_block, second_block):
    rotated = jnp.stack([-second_block[:, :, 1], second_block[:, :, 0]], 2)
    gram_real = jnp.einsum(
        "awcf,bwcf->abf", first_block, second_block, preferred_element_type=jnp.float32
    )
    gram_imag = jnp.einsum(
        "awcf,bwcf->abf", first_block, rotated, preferred_element_type=jnp.float32
    )
    return jnp.stack([gram_real, gram_imag], 2)


def on_any_device(traces, band_bins, pair_blocks):
    channels, windows, length = traces.shape
    band_count = band_bins.shape[0]
    dft_matrix = make_dft_table(band_bins, length)
    spectra = jnp.dot(
        traces.reshape(channels * windows, length), dft_matrix, preferred_element_type=jnp.float32
    )
    amplitude = jnp.sqrt(jnp.sum(spectra * spectra, axis=1, keepdims=True) / band_count + 1e-06)
    whitened = (spectra / amplitude).astype(jnp.bfloat16).reshape(channels, windows, 2, band_count)
    own_block = lax.all_to_all(whitened, "freq", split_axis=3, concat_axis=1, tiled=True)
    below_blocks = [shifted(own_block, "chan", distance) for distance in range(1, REACH + 1)]
    above_blocks = [shifted(own_block, "chan", -distance) for distance in range(1, REACH + 1)]
    stacked = jnp.stack(below_blocks[::-1] + [own_block] + above_blocks, 0)
    my_index = lax.axis_index("chan")
    gram_list = []
    for pair_slot in range(pair_blocks.shape[1]):
        offset = pair_blocks[0, pair_slot] - my_index + REACH
        partner = lax.dynamic_index_in_dim(stacked, offset, 0, keepdims=False)
        gram_list.append(gram_pair(own_block, partner))
    cross_gram = jnp.stack(gram_list, 1)
    lag_matrix = make_lag_table(band_bins, length, LAGS)
    lag_norm = 1.0 / math.sqrt(own_block.shape[1] * band_count)
    gram_block = lax.all_to_all(cross_gram, "freq", split_axis=0, concat_axis=4, tiled=True)
    dims_shape = gram_block.shape
    lagged = (
        jnp.dot(
            gram_block.reshape(-1, 2 * band_count),
            lag_matrix,
            precision=lax.Precision.HIGHEST,
            preferred_element_type=jnp.float32,
        )
        * lag_norm
    )
    result = lagged.reshape(dims_shape[0], dims_shape[1], dims_shape[2], LAGS)
    return result[None]


def spectra_kernel(traces_ref, fine_cos, fine_sin, step_cos, step_sin, out_ref, table, planes):
    bins, fine = fine_cos.shape
    groups, _, channels = planes.shape
    windows = traces_ref.shape[0] // channels
    for h in range(step_cos.shape[1]):
        sc, ss = step_cos[:, h : h + 1], step_sin[:, h : h + 1]
        cols = slice(h * fine, (h + 1) * fine)
        table[:bins, cols] = (sc * fine_cos[...] - ss * fine_sin[...]).astype(jnp.bfloat16)
        table[bins:, cols] = (-(ss * fine_cos[...] + sc * fine_sin[...])).astype(jnp.bfloat16)
    for half in range(windows // 2):
        rows = traces_ref[half * 2 * channels : (half + 1) * 2 * channels, :]
        spectra = lax.dot_general(
            table[...], rows, (((1,), (1,)), ((), ())), preferred_element_type=jnp.float32
        )
        power = jnp.sum(spectra * spectra, axis=0, keepdims=True)
        white = spectra / jnp.sqrt(power / bins + 1e-06)
        for w in range(2):
            for c in range(2):
                first = c * GROUP * windows + half * 2 + w
                planes[:, pl.ds(first, GROUP, stride=windows), :] = white[
                    c * bins : (c + 1) * bins, w * channels : (w + 1) * channels
                ].reshape(groups, GROUP, channels)
    out_ref[...] = planes[...].reshape(out_ref.shape).astype(jnp.bfloat16)


def make_slab(traces, band_bins):
    channels, windows, length = traces.shape
    bins = band_bins.shape[0]
    fine = 128
    rows = traces.transpose(1, 0, 2).reshape(windows * channels, length)
    sample_idx = jnp.concatenate([jnp.arange(fine), jnp.arange(length // fine) * fine])
    phase_int = band_bins[:, None] * sample_idx[None, :].astype(jnp.int32) % length
    phases = phase_int.astype(jnp.float32) * (2.0 * math.pi / length)
    cos, sin = jnp.cos(phases), jnp.sin(phases)
    return pl.pallas_call(
        spectra_kernel,
        out_shape=jax.ShapeDtypeStruct((bins * windows * 2, channels), jnp.bfloat16),
        scratch_shapes=[
            pltpu.VMEM((2 * bins, length), jnp.bfloat16),
            pltpu.VMEM((bins // GROUP, GROUP * windows * 2, channels), jnp.float32),
        ],
        compiler_params=pltpu.CompilerParams(vmem_limit_bytes=48 << 20),
        name="spectra",
    )(rows, cos[:, :fine], sin[:, :fine], cos[:, fine:], sin[:, fine:])


def left_kernel(z, *refs, per_step):
    slabs, (out_ref, choice, mask) = refs[:-3], refs[-3:]
    m, k = mask.shape
    channels = slabs[0].shape[1]
    group_rows = k // len(slabs)
    half = group_rows // 2
    rows_out = m // (2 * GROUP)

    @pl.when(pl.program_id(0) == 0)
    def _():
        row = lax.broadcasted_iota(jnp.int32, (m, 2 * channels), 0)
        col = lax.broadcasted_iota(jnp.int32, (m, 2 * channels), 1)
        wanted = row // (2 * GROUP) + z[0] * rows_out + (row % 2) * channels
        choice[...] = jnp.where(col == wanted, 1.0, 0.0).astype(jnp.bfloat16)
        row = lax.broadcasted_iota(jnp.int32, (m, k), 0)
        col = lax.broadcasted_iota(jnp.int32, (m, k), 1)
        bin_of_col = col % half // (half // GROUP)
        mask[...] = jnp.where(bin_of_col == row // 2 % GROUP, 1.0, 0.0)

    for u in range(per_step):
        pieces = []
        for slab in slabs:
            real = slab[u * group_rows : u * group_rows + half, :]
            imag = slab[u * group_rows + half : (u + 1) * group_rows, :]
            pieces.append(jnp.concatenate([real, imag], 1))
            pieces.append(jnp.concatenate([imag, -real], 1))
        both = jnp.concatenate(pieces, 0)
        rows = lax.dot_general(
            choice[...], both, (((1,), (1,)), ((), ())), preferred_element_type=jnp.float32
        )
        out_ref[u] = (rows * mask[...]).astype(jnp.bfloat16)


def make_left(slabs, z, rows_out, bins):
    slab_rows, channels = slabs[0].shape
    groups = bins // GROUP
    m, k = rows_out * GROUP * 2, slab_rows // groups * len(slabs)
    per_step = 4
    return pl.pallas_call(
        lambda *r: left_kernel(*r, per_step=per_step),
        grid_spec=pltpu.PrefetchScalarGridSpec(
            num_scalar_prefetch=1,
            grid=(groups // per_step,),
            in_specs=[
                pl.BlockSpec((slab_rows // groups * per_step, channels), lambda i, s: (i, 0))
            ]
            * len(slabs),
            out_specs=pl.BlockSpec((per_step, m, k), lambda i, s: (i, 0, 0)),
            scratch_shapes=[
                pltpu.VMEM((m, 2 * channels), jnp.bfloat16),
                pltpu.VMEM((m, k), jnp.float32),
            ],
        ),
        out_shape=jax.ShapeDtypeStruct((groups, m, k), jnp.bfloat16),
        compiler_params=pltpu.CompilerParams(vmem_limit_bytes=32 << 20),
        name="left",
    )(z.reshape(1), *slabs)


CHUNKS = 2
GROUP_UNROLL = 4
ROW_UNROLL = 4


def pairs_kernel(slots, left_ref, lag_ref, *refs, arrays, norm):
    sources, refs = refs[: len(arrays)], refs[len(arrays) :]
    out_ref, partner, left, gram, stage, in_sems, left_sems, out_sems = refs
    groups, m, k = left.shape
    slot_count, slabs, slab_rows, channels = partner.shape
    group_rows = k // slabs
    chunk_rows = slab_rows // CHUNKS
    lanes = slot_count * channels

    def fetch(source, s, r, chunk):
        rows = pl.ds(chunk * chunk_rows, chunk_rows)
        return pltpu.make_async_copy(source.at[rows], partner.at[s, r, rows], in_sems.at[chunk, s, r])

    for s in range(slot_count):
        for r in range(slabs):
            slot = slots[s * slabs + r]
            for source, (first, count, holds) in zip(sources, arrays):
                if r in holds:

                    @pl.when((slot >= first) & (slot < first + count))
                    def _():
                        for chunk in range(CHUNKS):
                            fetch(source.at[slot - first], s, r, chunk).start()

    per_chunk = groups // CHUNKS

    def fetch_left(chunk):
        some = pl.ds(chunk * per_chunk, per_chunk)
        return pltpu.make_async_copy(left_ref.at[some], left.at[some], left_sems.at[chunk])

    for chunk in range(CHUNKS):
        fetch_left(chunk).start()

    for chunk in range(CHUNKS):
        fetch_left(chunk).wait()
        for s in range(slot_count):
            for r in range(slabs):
                fetch(sources[0].at[0], s, r, chunk).wait()

        @pl.loop(0, per_chunk // GROUP_UNROLL)
        def _(i):
            for u in range(GROUP_UNROLL):
                g = chunk * per_chunk + i * GROUP_UNROLL + u
                rows = pl.ds(pl.multiple_of(g * group_rows, group_rows), group_rows)
                right = jnp.concatenate(
                    [partner[s, :, rows, :].reshape(k, channels) for s in range(slot_count)], 1
                )
                product = jnp.dot(left[g], right, preferred_element_type=jnp.float32)
                cols = pl.ds(pl.multiple_of(g * 2 * GROUP, 2 * GROUP), 2 * GROUP)
                gram[:, cols, :] = product.astype(jnp.bfloat16).reshape(
                    m // (2 * GROUP), 2 * GROUP, lanes
                )

    steps = gram.shape[0] // ROW_UNROLL

    def write(i, b):
        return pltpu.make_async_copy(
            stage.at[b], out_ref.at[pl.ds(i * ROW_UNROLL, ROW_UNROLL)], out_sems.at[b]
        )

    @pl.loop(0, steps)
    def _(i):
        b = lax.rem(i, 2)

        @pl.when(i >= 2)
        def _():
            write(i - 2, b).wait()

        for u in range(ROW_UNROLL):
            lagged = jnp.dot(
                lag_ref[...], gram[i * ROW_UNROLL + u], preferred_element_type=jnp.float32
            )
            for s in range(slot_count):
                stage[b, u, s] = (lagged[:, s * channels : (s + 1) * channels] * norm).T
        write(i, b).start()

    for i in range(steps - 2, steps):
        write(i, i % 2).wait()


def correlate(slots, left, lag_rows, held, slot_count, norm):
    groups, m, k = left.shape
    rows_out = m // (2 * GROUP)
    arrays, first = [], 0
    for value, holds in held:
        arrays.append((first, value.shape[0], holds))
        first += value.shape[0]
    slab_rows, channels = held[0][0].shape[1:]
    slabs = slots.shape[0] // slot_count
    lag_count, entries = lag_rows.shape
    anywhere = pl.BlockSpec(memory_space=pl.ANY)
    in_vmem = pl.BlockSpec(memory_space=pltpu.VMEM)
    return pl.pallas_call(
        lambda *r: pairs_kernel(*r, arrays=arrays, norm=norm),
        in_specs=[pl.BlockSpec(memory_space=pltpu.SMEM), anywhere, in_vmem] + [anywhere] * len(held),
        out_specs=anywhere,
        scratch_shapes=[
            pltpu.VMEM((slot_count, slabs, slab_rows, channels), jnp.bfloat16),
            pltpu.VMEM((groups, m, k), jnp.bfloat16),
            pltpu.VMEM((rows_out, entries, slot_count * channels), jnp.bfloat16),
            pltpu.VMEM((2, ROW_UNROLL, slot_count, channels, lag_count), jnp.float32),
            pltpu.SemaphoreType.DMA((CHUNKS, slot_count, slabs)),
            pltpu.SemaphoreType.DMA((CHUNKS,)),
            pltpu.SemaphoreType.DMA((2,)),
        ],
        out_shape=jax.ShapeDtypeStruct((rows_out, slot_count, channels, lag_count), jnp.float32),
        compiler_params=pltpu.CompilerParams(vmem_limit_bytes=58 << 20),
        name="pairs",
    )(slots, left, lag_rows, *[value for value, _ in held])


X_PAIRS = [(i, i ^ 2) for i in range(8)]
Y_PAIRS = [(4, 0), (1, 5), (6, 2), (3, 7)]
Y_ON = [(7, 3), (0, 4)]
Y_ON_ALL = Y_ON + [(6, 2), (1, 5)]
X_ON = [(0, 2), (7, 5)]
CORE_PAIRS = [(i, i ^ 1) for i in range(8)]


def moved(what, pairs):
    after = [[None] * 8 for _ in what]
    for src, dst in pairs:
        for old, new in zip(what, after):
            new[dst] = old[src]
    return after


class Held:
    def __init__(self, value, what):
        self.value, self.what = value, what

    def hop(self, pairs):
        return Held(lax.ppermute(self.value, "chan", pairs), moved(self.what, pairs))


def join(*parts):
    return Held(jnp.concatenate([p.value for p in parts], 0), [w for p in parts for w in p.what])


def together(*parts):
    return lax.optimization_barrier(parts)


jax.tree_util.register_pytree_node(
    Held,
    lambda held: ((held.value,), tuple(tuple(row) for row in held.what)),
    lambda what, children: Held(children[0], [list(row) for row in what]),
)


def on_device(traces, band_bins, pair_blocks):
    channels, windows, length = traces.shape
    bins = band_bins.shape[0]
    z = lax.axis_index("freq")
    me = lax.axis_index("chan")
    slot_count = pair_blocks.shape[1]

    lag_idx = jnp.arange(LAGS, dtype=jnp.int32) - LAGS // 2
    phases = (lag_idx[:, None] * band_bins[None, :] % length).astype(jnp.float32)
    phases = phases * (2.0 * math.pi / length)
    lag_rows = jnp.stack([jnp.cos(phases), -jnp.sin(phases)], 2).reshape(LAGS, 2 * bins)
    lag_rows = lag_rows.astype(jnp.bfloat16)

    def along_z(value, pairs):
        return lax.ppermute(value, "freq", pairs)

    def slab_of(value, r):
        return Held(value, [[(i, r) for i in range(8)]])

    s0 = make_slab(traces, band_bins)[None]
    q0 = slab_of(s0, 0)
    down1, up1 = along_z(s0, [(3, 2), (2, 1), (1, 0)]), along_z(s0, [(0, 1), (1, 2), (2, 3)])
    y0 = q0.hop(Y_PAIRS)
    x0 = q0.hop(X_PAIRS)
    y0, down1, up1, x0, lag_rows = together(y0, down1, up1, x0, lag_rows)

    q1 = slab_of(lax.select_n(z, down1, up1, down1, up1), 1)
    up2, down2 = along_z(up1, [(1, 2), (2, 3)]), along_z(down1, [(2, 1), (1, 0)])
    x1 = q1.hop(X_PAIRS)
    y1 = q1.hop(Y_PAIRS)
    c0 = x0.hop(Y_ON_ALL)
    up2, down2, y1, c0, x1 = together(up2, down2, y1, c0, x1)

    q2 = slab_of(lax.select_n(z, down2, down1, up1, up2), 2)
    last = along_z(jnp.where(z == 2, up2, down2), [(2, 3), (1, 0)])
    a0 = join(q0, x0, y0, c0).hop(CORE_PAIRS)
    x2 = q2.hop(X_PAIRS)
    y2 = q2.hop(Y_PAIRS)
    c1 = x1.hop(Y_ON_ALL)
    last, a0, y2, c1, x2 = together(last, a0, y2, c1, x2)

    q3 = slab_of(lax.select_n(z, last, down2, up2, last), 3)
    a1 = join(q1, x1, y1, c1).hop(CORE_PAIRS)
    a2 = join(q2, x2, y2).hop(CORE_PAIRS)
    x3 = q3.hop(X_PAIRS)
    y3 = q3.hop(Y_PAIRS)
    c2 = x2.hop(Y_ON_ALL)
    left = make_left([q.value[0] for q in (q0, q1, q2, q3)], z, channels // 4, bins)
    a1, a2, y3, c2, x3, left = together(a1, a2, y3, c2, x3, left)

    a3 = join(c2, q3, x3, y3).hop(CORE_PAIRS)
    c3, d3 = x3.hop(Y_ON), y3.hop(X_ON)

    held = [q0, q1, q2, q3, x0, x1, x2, x3, y0, y1, y2, y3, c0, c1, c2, c3, d3, a0, a1, a2, a3]
    whats = [h.what for h in held] + [moved(c3.what + d3.what, CORE_PAIRS)]
    table = np.zeros((8, 8, 4), np.int32)
    all_holds = [set() for _ in whats]
    index = sum(len(what) for what in whats)
    for what, holds in zip(reversed(whats), reversed(all_holds)):
        for item in reversed(what):
            index -= 1
            for device, block_slab in enumerate(item):
                if block_slab is not None:
                    table[device, block_slab[0], block_slab[1]] = index
                    holds.add(block_slab[1])
    mine = jnp.asarray(table)[me]
    slots = jnp.concatenate([mine[pair_blocks[0, s]] for s in range(slot_count)])

    c3, d3, a3, slots = together(c3, d3, a3, slots)
    a4 = join(c3, d3).hop(CORE_PAIRS)
    held = [q0, q1, q2, q3, x0, x1, x2, x3, y0, y1, y2, y3, c0, c1, c2, c3, d3, a0, a1, a2, a3, a4]
    places = [(h.value, holds) for h, holds in zip(held, all_holds)]
    norm = 1.0 / math.sqrt(4 * windows * bins)
    return correlate(slots, left, lag_rows, places, slot_count, norm)[None]


def solution(mesh):
    placed = (P("chan", "freq", None), P(), P("chan", None))
    fits = mesh.shape["chan"] == 8 and mesh.shape["freq"] == 4
    return jax.shard_map(
        on_device if fits else on_any_device,
        mesh=mesh,
        in_specs=placed,
        out_specs=P("chan", "freq", None, None, None),
        check_vma=False,
    )
```

```python
import math

import jax
import jax.numpy as jnp
import numpy as np
from jax import lax
from jax.experimental import pallas as pl
from jax.experimental.pallas import tpu as pltpu
from jax.sharding import PartitionSpec as P

LAGS = 128
REACH = 3
GROUP = 8


def shifted(value, axis, by):
    size = lax.axis_size(axis)
    pairs = [(i, i + by) for i in range(size) if 0 <= i + by < size]
    return lax.ppermute(value, axis, pairs)


def make_dft_table(band_bins, length):
    sample_idx = jnp.arange(length, dtype=jnp.int32)
    phase_int = band_bins[:, None] * sample_idx[None, :] % length
    phases = phase_int.astype(jnp.float32) * (2.0 * math.pi / length)
    return jnp.concatenate([jnp.cos(phases), -jnp.sin(phases)], 0).T.astype(jnp.bfloat16)


def make_lag_table(band_bins, length, lag_count):
    lag_idx = jnp.arange(lag_count, dtype=jnp.int32) - lag_count // 2
    phase_int = band_bins[:, None] * lag_idx[None, :] % length
    phases = phase_int.astype(jnp.float32) * (2.0 * math.pi / length)
    return jnp.concatenate([jnp.cos(phases), -jnp.sin(phases)], 0)


def gram_pair(first_block, second_block):
    rotated = jnp.stack([-second_block[:, :, 1], second_block[:, :, 0]], 2)
    gram_real = jnp.einsum(
        "awcf,bwcf->abf", first_block, second_block, preferred_element_type=jnp.float32
    )
    gram_imag = jnp.einsum(
        "awcf,bwcf->abf", first_block, rotated, preferred_element_type=jnp.float32
    )
    return jnp.stack([gram_real, gram_imag], 2)


def on_any_device(traces, band_bins, pair_blocks):
    channels, windows, length = traces.shape
    band_count = band_bins.shape[0]
    dft_matrix = make_dft_table(band_bins, length)
    spectra = jnp.dot(
        traces.reshape(channels * windows, length), dft_matrix, preferred_element_type=jnp.float32
    )
    amplitude = jnp.sqrt(jnp.sum(spectra * spectra, axis=1, keepdims=True) / band_count + 1e-06)
    whitened = (spectra / amplitude).astype(jnp.bfloat16).reshape(channels, windows, 2, band_count)
    own_block = lax.all_to_all(whitened, "freq", split_axis=3, concat_axis=1, tiled=True)
    below_blocks = [shifted(own_block, "chan", distance) for distance in range(1, REACH + 1)]
    above_blocks = [shifted(own_block, "chan", -distance) for distance in range(1, REACH + 1)]
    stacked = jnp.stack(below_blocks[::-1] + [own_block] + above_blocks, 0)
    my_index = lax.axis_index("chan")
    gram_list = []
    for pair_slot in range(pair_blocks.shape[1]):
        offset = pair_blocks[0, pair_slot] - my_index + REACH
        partner = lax.dynamic_index_in_dim(stacked, offset, 0, keepdims=False)
        gram_list.append(gram_pair(own_block, partner))
    cross_gram = jnp.stack(gram_list, 1)
    lag_matrix = make_lag_table(band_bins, length, LAGS)
    lag_norm = 1.0 / math.sqrt(own_block.shape[1] * band_count)
    gram_block = lax.all_to_all(cross_gram, "freq", split_axis=0, concat_axis=4, tiled=True)
    dims_shape = gram_block.shape
    lagged = (
        jnp.dot(
            gram_block.reshape(-1, 2 * band_count),
            lag_matrix,
            precision=lax.Precision.HIGHEST,
            preferred_element_type=jnp.float32,
        )
        * lag_norm
    )
    result = lagged.reshape(dims_shape[0], dims_shape[1], dims_shape[2], LAGS)
    return result[None]


def spectra_kernel(traces_ref, fine_cos, fine_sin, step_cos, step_sin, out_ref, table, planes):
    bins, fine = fine_cos.shape
    groups, _, channels = planes.shape
    windows = traces_ref.shape[0] // channels
    for h in range(step_cos.shape[1]):
        sc, ss = step_cos[:, h : h + 1], step_sin[:, h : h + 1]
        cols = slice(h * fine, (h + 1) * fine)
        table[:bins, cols] = (sc * fine_cos[...] - ss * fine_sin[...]).astype(jnp.bfloat16)
        table[bins:, cols] = (-(ss * fine_cos[...] + sc * fine_sin[...])).astype(jnp.bfloat16)
    for half in range(windows // 2):
        rows = traces_ref[half * 2 * channels : (half + 1) * 2 * channels, :]
        spectra = lax.dot_general(
            table[...], rows, (((1,), (1,)), ((), ())), preferred_element_type=jnp.float32
        )
        power = jnp.sum(spectra * spectra, axis=0, keepdims=True)
        white = spectra / jnp.sqrt(power / bins + 1e-06)
        for w in range(2):
            for c in range(2):
                first = c * GROUP * windows + half * 2 + w
                planes[:, pl.ds(first, GROUP, stride=windows), :] = white[
                    c * bins : (c + 1) * bins, w * channels : (w + 1) * channels
                ].reshape(groups, GROUP, channels)
    out_ref[...] = planes[...].reshape(out_ref.shape).astype(jnp.bfloat16)


def make_slab(traces, band_bins):
    channels, windows, length = traces.shape
    bins = band_bins.shape[0]
    fine = 128
    rows = traces.transpose(1, 0, 2).reshape(windows * channels, length)
    sample_idx = jnp.concatenate([jnp.arange(fine), jnp.arange(length // fine) * fine])
    phase_int = band_bins[:, None] * sample_idx[None, :].astype(jnp.int32) % length
    phases = phase_int.astype(jnp.float32) * (2.0 * math.pi / length)
    cos, sin = jnp.cos(phases), jnp.sin(phases)
    return pl.pallas_call(
        spectra_kernel,
        out_shape=jax.ShapeDtypeStruct((bins * windows * 2, channels), jnp.bfloat16),
        scratch_shapes=[
            pltpu.VMEM((2 * bins, length), jnp.bfloat16),
            pltpu.VMEM((bins // GROUP, GROUP * windows * 2, channels), jnp.float32),
        ],
        compiler_params=pltpu.CompilerParams(vmem_limit_bytes=12 << 20),
        name="spectra",
    )(rows, cos[:, :fine], sin[:, :fine], cos[:, fine:], sin[:, fine:])


def left_kernel(z, *refs, per_step):
    slabs, (out_ref, choice, mask) = refs[:-3], refs[-3:]
    m, k = mask.shape
    channels = slabs[0].shape[1]
    group_rows = k // len(slabs)
    half = group_rows // 2
    rows_out = m // (2 * GROUP)

    @pl.when(pl.program_id(0) == 0)
    def _():
        row = lax.broadcasted_iota(jnp.int32, (m, 2 * channels), 0)
        col = lax.broadcasted_iota(jnp.int32, (m, 2 * channels), 1)
        wanted = row // (2 * GROUP) + z[0] * rows_out + (row % 2) * channels
        choice[...] = jnp.where(col == wanted, 1.0, 0.0).astype(jnp.bfloat16)
        row = lax.broadcasted_iota(jnp.int32, (m, k), 0)
        col = lax.broadcasted_iota(jnp.int32, (m, k), 1)
        bin_of_col = col % half // (half // GROUP)
        mask[...] = jnp.where(bin_of_col == row // 2 % GROUP, 1.0, 0.0)

    for u in range(per_step):
        pieces = []
        for slab in slabs:
            real = slab[u * group_rows : u * group_rows + half, :]
            imag = slab[u * group_rows + half : (u + 1) * group_rows, :]
            pieces.append(jnp.concatenate([real, imag], 1))
            pieces.append(jnp.concatenate([imag, -real], 1))
        both = jnp.concatenate(pieces, 0)
        rows = lax.dot_general(
            choice[...], both, (((1,), (1,)), ((), ())), preferred_element_type=jnp.float32
        )
        out_ref[u] = (rows * mask[...]).astype(jnp.bfloat16)


def make_left(slabs, z, rows_out, bins):
    slab_rows, channels = slabs[0].shape
    groups = bins // GROUP
    m, k = rows_out * GROUP * 2, slab_rows // groups * len(slabs)
    per_step = 4
    return pl.pallas_call(
        lambda *r: left_kernel(*r, per_step=per_step),
        grid_spec=pltpu.PrefetchScalarGridSpec(
            num_scalar_prefetch=1,
            grid=(groups // per_step,),
            in_specs=[
                pl.BlockSpec((slab_rows // groups * per_step, channels), lambda i, s: (i, 0))
            ]
            * len(slabs),
            out_specs=pl.BlockSpec((per_step, m, k), lambda i, s: (i, 0, 0)),
            scratch_shapes=[
                pltpu.VMEM((m, 2 * channels), jnp.bfloat16),
                pltpu.VMEM((m, k), jnp.float32),
            ],
        ),
        out_shape=jax.ShapeDtypeStruct((groups, m, k), jnp.bfloat16),
        compiler_params=pltpu.CompilerParams(vmem_limit_bytes=10 << 20),
        name="left",
    )(z.reshape(1), *slabs)


CHUNKS = 2
GROUP_UNROLL = 4
ROW_UNROLL = 4


def pairs_kernel(slots, left_ref, lag_ref, *refs, arrays, norm):
    sources, refs = refs[: len(arrays)], refs[len(arrays) :]
    out_ref, partner, gram, stage, in_sems, out_sems = refs
    groups, m, k = left_ref.shape
    slot_count, slabs, slab_rows, channels = partner.shape
    group_rows = k // slabs
    chunk_rows = slab_rows // CHUNKS
    lanes = slot_count * channels

    def fetch(source, s, r, chunk):
        rows = pl.ds(chunk * chunk_rows, chunk_rows)
        return pltpu.make_async_copy(source.at[rows], partner.at[s, r, rows], in_sems.at[chunk, s, r])

    for s in range(slot_count):
        for r in range(slabs):
            slot = slots[s * slabs + r]
            for source, (first, count, holds) in zip(sources, arrays):
                if r in holds:

                    @pl.when((slot >= first) & (slot < first + count))
                    def _():
                        for chunk in range(CHUNKS):
                            fetch(source.at[slot - first], s, r, chunk).start()

    per_chunk = groups // CHUNKS

    for chunk in range(CHUNKS):
        for s in range(slot_count):
            for r in range(slabs):
                fetch(sources[0].at[0], s, r, chunk).wait()

        @pl.loop(0, per_chunk // GROUP_UNROLL)
        def _(i):
            for u in range(GROUP_UNROLL):
                g = chunk * per_chunk + i * GROUP_UNROLL + u
                rows = pl.ds(pl.multiple_of(g * group_rows, group_rows), group_rows)
                right = jnp.concatenate(
                    [partner[s, :, rows, :].reshape(k, channels) for s in range(slot_count)], 1
                )
                product = jnp.dot(left_ref[g], right, preferred_element_type=jnp.float32)
                cols = pl.ds(pl.multiple_of(g * 2 * GROUP, 2 * GROUP), 2 * GROUP)
                gram[:, cols, :] = product.astype(jnp.bfloat16).reshape(
                    m // (2 * GROUP), 2 * GROUP, lanes
                )

    steps = gram.shape[0] // ROW_UNROLL

    def write(i, b):
        return pltpu.make_async_copy(
            stage.at[b], out_ref.at[pl.ds(i * ROW_UNROLL, ROW_UNROLL)], out_sems.at[b]
        )

    @pl.loop(0, steps)
    def _(i):
        b = lax.rem(i, 2)

        @pl.when(i >= 2)
        def _():
            write(i - 2, b).wait()

        for u in range(ROW_UNROLL):
            lagged = jnp.dot(
                lag_ref[...], gram[i * ROW_UNROLL + u], preferred_element_type=jnp.float32
            )
            for s in range(slot_count):
                stage[b, u, s] = (lagged[:, s * channels : (s + 1) * channels] * norm).T
        write(i, b).start()

    for i in range(steps - 2, steps):
        write(i, i % 2).wait()


def correlate(slots, left, lag_rows, held, slot_count, norm):
    groups, m, k = left.shape
    rows_out = m // (2 * GROUP)
    arrays, first = [], 0
    for value, holds in held:
        arrays.append((first, value.shape[0], holds))
        first += value.shape[0]
    slab_rows, channels = held[0][0].shape[1:]
    slabs = slots.shape[0] // slot_count
    lag_count, entries = lag_rows.shape
    anywhere = pl.BlockSpec(memory_space=pl.ANY)
    in_vmem = pl.BlockSpec(memory_space=pltpu.VMEM)
    return pl.pallas_call(
        lambda *r: pairs_kernel(*r, arrays=arrays, norm=norm),
        in_specs=[pl.BlockSpec(memory_space=pltpu.SMEM), in_vmem, in_vmem] + [anywhere] * len(held),
        out_specs=anywhere,
        scratch_shapes=[
            pltpu.VMEM((slot_count, slabs, slab_rows, channels), jnp.bfloat16),
            pltpu.VMEM((rows_out, entries, slot_count * channels), jnp.bfloat16),
            pltpu.VMEM((2, ROW_UNROLL, slot_count, channels, lag_count), jnp.float32),
            pltpu.SemaphoreType.DMA((CHUNKS, slot_count, slabs)),
            pltpu.SemaphoreType.DMA((2,)),
        ],
        out_shape=jax.ShapeDtypeStruct((rows_out, slot_count, channels, lag_count), jnp.float32),
        compiler_params=pltpu.CompilerParams(vmem_limit_bytes=25 << 20),
        name="pairs",
    )(slots, left, lag_rows, *[value for value, _ in held])


X_PAIRS = [(i, i ^ 2) for i in range(8)]
Y_PAIRS = [(4, 0), (1, 5), (6, 2), (3, 7)]
Y_ON = [(7, 3), (0, 4)]
Y_ON_ALL = Y_ON + [(6, 2), (1, 5)]
X_ON = [(0, 2), (7, 5)]
CORE_PAIRS = [(i, i ^ 1) for i in range(8)]


def moved(what, pairs):
    after = [[None] * 8 for _ in what]
    for src, dst in pairs:
        for old, new in zip(what, after):
            new[dst] = old[src]
    return after


class Held:
    def __init__(self, value, what):
        self.value, self.what = value, what

    def hop(self, pairs):
        return Held(lax.ppermute(self.value, "chan", pairs), moved(self.what, pairs))


def join(*parts):
    return Held(jnp.concatenate([p.value for p in parts], 0), [w for p in parts for w in p.what])


def together(*parts):
    return lax.optimization_barrier(parts)


jax.tree_util.register_pytree_node(
    Held,
    lambda held: ((held.value,), tuple(tuple(row) for row in held.what)),
    lambda what, children: Held(children[0], [list(row) for row in what]),
)


def on_device(traces, band_bins, pair_blocks):
    channels, windows, length = traces.shape
    bins = band_bins.shape[0]
    z = lax.axis_index("freq")
    me = lax.axis_index("chan")
    slot_count = pair_blocks.shape[1]

    lag_idx = jnp.arange(LAGS, dtype=jnp.int32) - LAGS // 2
    phases = (lag_idx[:, None] * band_bins[None, :] % length).astype(jnp.float32)
    phases = phases * (2.0 * math.pi / length)
    lag_rows = jnp.stack([jnp.cos(phases), -jnp.sin(phases)], 2).reshape(LAGS, 2 * bins)
    lag_rows = lag_rows.astype(jnp.bfloat16)

    def along_z(value, pairs):
        return lax.ppermute(value, "freq", pairs)

    def slab_of(value, r):
        return Held(value, [[(i, r) for i in range(8)]])

    s0 = make_slab(traces, band_bins)[None]
    q0 = slab_of(s0, 0)
    y0 = q0.hop(Y_PAIRS)
    x0 = q0.hop(X_PAIRS)
    down1, up1 = along_z(s0, [(3, 2), (2, 1), (1, 0)]), along_z(s0, [(0, 1), (1, 2), (2, 3)])
    y0, down1, up1, x0, lag_rows = together(y0, down1, up1, x0, lag_rows)

    q1 = slab_of(lax.select_n(z, down1, up1, down1, up1), 1)
    up2, down2 = along_z(up1, [(1, 2), (2, 3)]), along_z(down1, [(2, 1), (1, 0)])
    x1 = q1.hop(X_PAIRS)
    y1 = q1.hop(Y_PAIRS)
    c0 = x0.hop(Y_ON_ALL)
    up2, down2, y1, c0, x1 = together(up2, down2, y1, c0, x1)

    q2 = slab_of(lax.select_n(z, down2, down1, up1, up2), 2)
    last = along_z(jnp.where(z == 2, up2, down2), [(2, 3), (1, 0)])
    a0 = join(q0, x0, y0, c0).hop(CORE_PAIRS)
    x2 = q2.hop(X_PAIRS)
    y2 = q2.hop(Y_PAIRS)
    c1 = x1.hop(Y_ON_ALL)
    last, a0, y2, c1, x2 = together(last, a0, y2, c1, x2)

    q3 = slab_of(lax.select_n(z, last, down2, up2, last), 3)
    a1 = join(q1, x1, y1, c1).hop(CORE_PAIRS)
    a2 = join(q2, x2, y2).hop(CORE_PAIRS)
    x3 = q3.hop(X_PAIRS)
    y3 = q3.hop(Y_PAIRS)
    c2 = x2.hop(Y_ON_ALL)
    left = make_left([q.value[0] for q in (q0, q1, q2, q3)], z, channels // 4, bins)
    a1, a2, y3, c2, x3, left = together(a1, a2, y3, c2, x3, left)

    a3 = join(c2, q3, x3, y3).hop(CORE_PAIRS)
    c3, d3 = x3.hop(Y_ON), y3.hop(X_ON)

    held = [q0, q1, q2, q3, x0, x1, x2, x3, y0, y1, y2, y3, c0, c1, c2, c3, d3, a0, a1, a2, a3]
    whats = [h.what for h in held] + [moved(c3.what + d3.what, CORE_PAIRS)]
    table = np.zeros((8, 8, 4), np.int32)
    all_holds = [set() for _ in whats]
    index = sum(len(what) for what in whats)
    for what, holds in zip(reversed(whats), reversed(all_holds)):
        for item in reversed(what):
            index -= 1
            for device, block_slab in enumerate(item):
                if block_slab is not None:
                    table[device, block_slab[0], block_slab[1]] = index
                    holds.add(block_slab[1])
    ids = np.arange(8, dtype=np.int32)
    wanted = (ids[None, None, :, None] == pair_blocks[0][:, None, None, None]) & (
        ids[None, :, None, None] == me
    )
    slots = jnp.sum(jnp.where(wanted, table[None], 0), axis=(1, 2)).reshape(-1)

    c3, d3, a3, slots = together(c3, d3, a3, slots)
    a4 = join(c3, d3).hop(CORE_PAIRS)
    held = [q0, q1, q2, q3, x0, x1, x2, x3, y0, y1, y2, y3, c0, c1, c2, c3, d3, a0, a1, a2, a3, a4]
    places = [(h.value, holds) for h, holds in zip(held, all_holds)]
    norm = 1.0 / math.sqrt(4 * windows * bins)
    return correlate(slots, left, lag_rows, places, slot_count, norm)[None]


def solution(mesh):
    placed = (P("chan", "freq", None), P(), P("chan", None))
    fits = mesh.shape["chan"] == 8 and mesh.shape["freq"] == 4
    return jax.shard_map(
        on_device if fits else on_any_device,
        mesh=mesh,
        in_specs=placed,
        out_specs=P("chan", "freq", None, None, None),
        check_vma=False,
    )
```

```python
import math

import jax
import jax.numpy as jnp
import numpy as np
from jax import lax
from jax.experimental import pallas as pl
from jax.experimental.pallas import tpu as pltpu
from jax.sharding import PartitionSpec as P

LAGS = 128
REACH = 3
GROUP = 8


def shifted(value, axis, by):
    size = lax.axis_size(axis)
    pairs = [(i, i + by) for i in range(size) if 0 <= i + by < size]
    return lax.ppermute(value, axis, pairs)


def make_dft_table(band_bins, length):
    sample_idx = jnp.arange(length, dtype=jnp.int32)
    phase_int = band_bins[:, None] * sample_idx[None, :] % length
    phases = phase_int.astype(jnp.float32) * (2.0 * math.pi / length)
    return jnp.concatenate([jnp.cos(phases), -jnp.sin(phases)], 0).T.astype(jnp.bfloat16)


def make_lag_table(band_bins, length, lag_count):
    lag_idx = jnp.arange(lag_count, dtype=jnp.int32) - lag_count // 2
    phase_int = band_bins[:, None] * lag_idx[None, :] % length
    phases = phase_int.astype(jnp.float32) * (2.0 * math.pi / length)
    return jnp.concatenate([jnp.cos(phases), -jnp.sin(phases)], 0)


def gram_pair(first_block, second_block):
    rotated = jnp.stack([-second_block[:, :, 1], second_block[:, :, 0]], 2)
    gram_real = jnp.einsum(
        "awcf,bwcf->abf", first_block, second_block, preferred_element_type=jnp.float32
    )
    gram_imag = jnp.einsum(
        "awcf,bwcf->abf", first_block, rotated, preferred_element_type=jnp.float32
    )
    return jnp.stack([gram_real, gram_imag], 2)


def on_any_device(traces, band_bins, pair_blocks):
    channels, windows, length = traces.shape
    band_count = band_bins.shape[0]
    dft_matrix = make_dft_table(band_bins, length)
    spectra = jnp.dot(
        traces.reshape(channels * windows, length), dft_matrix, preferred_element_type=jnp.float32
    )
    amplitude = jnp.sqrt(jnp.sum(spectra * spectra, axis=1, keepdims=True) / band_count + 1e-06)
    whitened = (spectra / amplitude).astype(jnp.bfloat16).reshape(channels, windows, 2, band_count)
    own_block = lax.all_to_all(whitened, "freq", split_axis=3, concat_axis=1, tiled=True)
    below_blocks = [shifted(own_block, "chan", distance) for distance in range(1, REACH + 1)]
    above_blocks = [shifted(own_block, "chan", -distance) for distance in range(1, REACH + 1)]
    stacked = jnp.stack(below_blocks[::-1] + [own_block] + above_blocks, 0)
    my_index = lax.axis_index("chan")
    gram_list = []
    for pair_slot in range(pair_blocks.shape[1]):
        offset = pair_blocks[0, pair_slot] - my_index + REACH
        partner = lax.dynamic_index_in_dim(stacked, offset, 0, keepdims=False)
        gram_list.append(gram_pair(own_block, partner))
    cross_gram = jnp.stack(gram_list, 1)
    lag_matrix = make_lag_table(band_bins, length, LAGS)
    lag_norm = 1.0 / math.sqrt(own_block.shape[1] * band_count)
    gram_block = lax.all_to_all(cross_gram, "freq", split_axis=0, concat_axis=4, tiled=True)
    dims_shape = gram_block.shape
    lagged = (
        jnp.dot(
            gram_block.reshape(-1, 2 * band_count),
            lag_matrix,
            precision=lax.Precision.HIGHEST,
            preferred_element_type=jnp.float32,
        )
        * lag_norm
    )
    result = lagged.reshape(dims_shape[0], dims_shape[1], dims_shape[2], LAGS)
    return result[None]


def spectra_kernel(traces_ref, fine_cos, fine_sin, step_cos, step_sin, out_ref, table, planes):
    bins, fine = fine_cos.shape
    groups, _, channels = planes.shape
    windows = traces_ref.shape[0] // channels
    for h in range(step_cos.shape[1]):
        sc, ss = step_cos[:, h : h + 1], step_sin[:, h : h + 1]
        cols = slice(h * fine, (h + 1) * fine)
        table[:bins, cols] = (sc * fine_cos[...] - ss * fine_sin[...]).astype(jnp.bfloat16)
        table[bins:, cols] = (-(ss * fine_cos[...] + sc * fine_sin[...])).astype(jnp.bfloat16)
    for half in range(windows // 2):
        rows = traces_ref[half * 2 * channels : (half + 1) * 2 * channels, :]
        spectra = lax.dot_general(
            table[...], rows, (((1,), (1,)), ((), ())), preferred_element_type=jnp.float32
        )
        power = jnp.sum(spectra * spectra, axis=0, keepdims=True)
        white = spectra / jnp.sqrt(power / bins + 1e-06)
        for w in range(2):
            for c in range(2):
                first = c * GROUP * windows + half * 2 + w
                planes[:, pl.ds(first, GROUP, stride=windows), :] = white[
                    c * bins : (c + 1) * bins, w * channels : (w + 1) * channels
                ].reshape(groups, GROUP, channels)
    out_ref[...] = planes[...].reshape(out_ref.shape).astype(jnp.bfloat16)


def make_slab(traces, band_bins):
    channels, windows, length = traces.shape
    bins = band_bins.shape[0]
    fine = 128
    rows = traces.transpose(1, 0, 2).reshape(windows * channels, length)
    sample_idx = jnp.concatenate([jnp.arange(fine), jnp.arange(length // fine) * fine])
    phase_int = band_bins[:, None] * sample_idx[None, :].astype(jnp.int32) % length
    phases = phase_int.astype(jnp.float32) * (2.0 * math.pi / length)
    cos, sin = jnp.cos(phases), jnp.sin(phases)
    return pl.pallas_call(
        spectra_kernel,
        out_shape=jax.ShapeDtypeStruct((bins * windows * 2, channels), jnp.bfloat16),
        scratch_shapes=[
            pltpu.VMEM((2 * bins, length), jnp.bfloat16),
            pltpu.VMEM((bins // GROUP, GROUP * windows * 2, channels), jnp.float32),
        ],
        compiler_params=pltpu.CompilerParams(vmem_limit_bytes=12 << 20),
        name="spectra",
    )(rows, cos[:, :fine], sin[:, :fine], cos[:, fine:], sin[:, fine:])


def left_kernel(z, *refs, per_step):
    slabs, (out_ref, choice, mask) = refs[:-3], refs[-3:]
    m, k = mask.shape
    channels = slabs[0].shape[-1]
    group_rows = slabs[0].shape[0] // per_step
    half = group_rows // 2
    rows_out = m // (2 * GROUP)

    @pl.when(pl.program_id(0) == 0)
    def _():
        row = lax.broadcasted_iota(jnp.int32, (m, 2 * channels), 0)
        col = lax.broadcasted_iota(jnp.int32, (m, 2 * channels), 1)
        wanted = row // (2 * GROUP) + z[0] * rows_out + (row % 2) * channels
        choice[...] = jnp.where(col == wanted, 1.0, 0.0).astype(jnp.bfloat16)
        row = lax.broadcasted_iota(jnp.int32, (m, k), 0)
        col = lax.broadcasted_iota(jnp.int32, (m, k), 1)
        bin_of_col = col % half // (half // GROUP)
        mask[...] = jnp.where(bin_of_col == row // 2 % GROUP, 1.0, 0.0)

    for u in range(per_step):
        pieces = []
        for slab in slabs:
            real = slab[u * group_rows : u * group_rows + half, :]
            imag = slab[u * group_rows + half : (u + 1) * group_rows, :]
            pieces.append(jnp.concatenate([real, imag], 1))
            pieces.append(jnp.concatenate([imag, -real], 1))
        both = jnp.concatenate(pieces, 0)
        rows = lax.dot_general(
            choice[...], both, (((1,), (1,)), ((), ())), preferred_element_type=jnp.float32
        )
        out_ref[u] = (rows * mask[...]).astype(jnp.bfloat16)


def make_left(slabs, z, rows_out, bins):
    slab_rows, channels = slabs[0].shape
    groups = bins // GROUP
    m, k = rows_out * GROUP * 2, slab_rows // groups * 4
    per_step = 4
    step_rows = slab_rows // groups * per_step
    return pl.pallas_call(
        lambda *r: left_kernel(*r, per_step=per_step),
        grid_spec=pltpu.PrefetchScalarGridSpec(
            num_scalar_prefetch=1,
            grid=(groups // per_step,),
            in_specs=[pl.BlockSpec((step_rows, channels), lambda i, s: (i, 0))] * len(slabs),
            out_specs=pl.BlockSpec((per_step, m, k), lambda i, s: (i, 0, 0)),
            scratch_shapes=[
                pltpu.VMEM((m, 2 * channels), jnp.bfloat16),
                pltpu.VMEM((m, k), jnp.float32),
            ],
        ),
        out_shape=jax.ShapeDtypeStruct((groups, m, k), jnp.bfloat16),
        compiler_params=pltpu.CompilerParams(vmem_limit_bytes=10 << 20),
        name="left",
    )(z.reshape(1), *slabs)


CHUNKS = 4
GROUP_UNROLL = 8
ROW_UNROLL = 8


def pairs_kernel(slots, left_ref, lag_ref, *refs, arrays, norm, aliased):
    sources, refs = refs[: len(arrays)], refs[len(arrays) + aliased :]
    out_ref, partner, left, gram, stage, in_sems, left_sems, out_sems = refs
    groups, m, k = left.shape
    chosen, slabs, slab_rows, channels = partner.shape
    group_rows = k // slabs
    chunk_rows = slab_rows // CHUNKS
    per_chunk = groups // CHUNKS

    def fetch(source, s, r, chunk):
        rows = pl.ds(chunk * chunk_rows, chunk_rows)
        return pltpu.make_async_copy(source.at[rows], partner.at[s, r, rows], in_sems.at[chunk, s, r])

    def fetch_left(chunk):
        some = pl.ds(chunk * per_chunk, per_chunk)
        return pltpu.make_async_copy(left_ref.at[some], left.at[some], left_sems.at[chunk])

    fetch_left(0).start()
    for s in range(chosen):
        for r in range(slabs):
            place = slots[s * (slabs + 1) + 1 + r]
            for source, (first, count, holds) in zip(sources, arrays):
                if r in holds:

                    @pl.when((place >= first) & (place < first + count))
                    def _():
                        for chunk in range(CHUNKS):
                            fetch(source.at[place - first], s, r, chunk).start()

    for chunk in range(1, CHUNKS):
        fetch_left(chunk).start()

    for chunk in range(CHUNKS):
        fetch_left(chunk).wait()
        for s in range(chosen):
            for r in range(slabs):
                fetch(sources[0].at[0], s, r, chunk).wait()

        @pl.loop(0, per_chunk // GROUP_UNROLL)
        def _(i):
            for u in range(GROUP_UNROLL):
                g = chunk * per_chunk + i * GROUP_UNROLL + u
                rows = pl.ds(pl.multiple_of(g * group_rows, group_rows), group_rows)
                right = jnp.concatenate(
                    [partner[s, :, rows, :].reshape(k, channels) for s in range(chosen)], 1
                )
                product = jnp.dot(left[g], right, preferred_element_type=jnp.float32)
                cols = pl.ds(pl.multiple_of(g * 2 * GROUP, 2 * GROUP), 2 * GROUP)
                gram[:, cols, :] = product.astype(jnp.bfloat16).reshape(
                    m // (2 * GROUP), 2 * GROUP, chosen * channels
                )

    steps = gram.shape[0] // ROW_UNROLL

    class Write:
        def __init__(self, i, b):
            rows = pl.ds(i * ROW_UNROLL, ROW_UNROLL)
            self.copies = [
                pltpu.make_async_copy(
                    stage.at[b, s], out_ref.at[rows, slots[s * (slabs + 1)]], out_sems.at[b, s]
                )
                for s in range(chosen)
            ]

        def start(self):
            for copy in self.copies:
                copy.start()

        def wait(self):
            for copy in self.copies:
                copy.wait()

    @pl.loop(0, steps)
    def _(i):
        b = lax.rem(i, 2)

        @pl.when(i >= 2)
        def _():
            Write(i - 2, b).wait()

        for u in range(ROW_UNROLL):
            lagged = jnp.dot(
                lag_ref[...], gram[i * ROW_UNROLL + u], preferred_element_type=jnp.float32
            )
            for s in range(chosen):
                stage[b, s, u] = (lagged[:, s * channels : (s + 1) * channels] * norm).T
        Write(i, b).start()

    for i in range(steps - 2, steps):
        Write(i, i % 2).wait()


def correlate(slots, left, lag_rows, held, slot_count, norm, earlier=None):
    groups, m, k = left.shape
    rows_out = m // (2 * GROUP)
    arrays, first = [], 0
    for value, holds in held:
        arrays.append((first, value.shape[0], holds))
        first += value.shape[0]
    slab_rows, channels = held[0][0].shape[1:]
    chosen, slabs = slots.shape[0], slots.shape[1] - 1
    lag_count, entries = lag_rows.shape
    anywhere = pl.BlockSpec(memory_space=pl.ANY)
    in_vmem = pl.BlockSpec(memory_space=pltpu.VMEM)
    operands = [slots.reshape(-1), left, lag_rows] + [value for value, _ in held]
    aliases = {}
    if earlier is not None:
        aliases = {len(operands): 0}
        operands.append(earlier)
    flops = 2 * groups * m * k * chosen * channels + 2 * rows_out * lag_count * entries * chosen * channels
    return pl.pallas_call(
        lambda *r: pairs_kernel(*r, arrays=arrays, norm=norm, aliased=len(aliases)),
        in_specs=[pl.BlockSpec(memory_space=pltpu.SMEM), anywhere, in_vmem]
        + [anywhere] * (len(operands) - 3),
        out_specs=anywhere,
        scratch_shapes=[
            pltpu.VMEM((chosen, slabs, slab_rows, channels), jnp.bfloat16),
            pltpu.VMEM((groups, m, k), jnp.bfloat16),
            pltpu.VMEM((rows_out, entries, chosen * channels), jnp.bfloat16),
            pltpu.VMEM((2, chosen, ROW_UNROLL, channels, lag_count), jnp.float32),
            pltpu.SemaphoreType.DMA((CHUNKS, chosen, slabs)),
            pltpu.SemaphoreType.DMA((CHUNKS,)),
            pltpu.SemaphoreType.DMA((2, chosen)),
        ],
        out_shape=jax.ShapeDtypeStruct((rows_out, slot_count, channels, lag_count), jnp.float32),
        input_output_aliases=aliases,
        cost_estimate=pl.CostEstimate(flops=flops, bytes_accessed=12 << 20, transcendentals=0),
        compiler_params=pltpu.CompilerParams(vmem_limit_bytes=PAIRS_VMEM),
        name="pairs",
    )(*operands)


PAIRS_VMEM = 58 << 20

X_PAIRS = [(i, i ^ 2) for i in range(8)]
Y_PAIRS = [(4, 0), (1, 5), (6, 2), (3, 7)]
Y_ON = [(7, 3), (0, 4)]
Y_ON_ALL = Y_ON + [(6, 2), (1, 5)]
X_ON = [(0, 2), (7, 5)]
CORE_PAIRS = [(i, i ^ 1) for i in range(8)]


def moved(what, pairs):
    after = [[None] * 8 for _ in what]
    for src, dst in pairs:
        for old, new in zip(what, after):
            new[dst] = old[src]
    return after


class Held:
    def __init__(self, value, what):
        self.value, self.what = value, what

    def hop(self, pairs):
        return Held(lax.ppermute(self.value, "chan", pairs), moved(self.what, pairs))


def join(*parts):
    return Held(jnp.concatenate([p.value for p in parts], 0), [w for p in parts for w in p.what])


def together(*parts):
    return lax.optimization_barrier(parts)


jax.tree_util.register_pytree_node(
    Held,
    lambda held: ((held.value,), tuple(tuple(row) for row in held.what)),
    lambda what, children: Held(children[0], [list(row) for row in what]),
)


def on_device(traces, band_bins, pair_blocks):
    channels, windows, length = traces.shape
    bins = band_bins.shape[0]
    z = lax.axis_index("freq")
    me = lax.axis_index("chan")
    slot_count = pair_blocks.shape[1]

    lag_idx = jnp.arange(LAGS, dtype=jnp.int32) - LAGS // 2
    phases = (lag_idx[:, None] * band_bins[None, :] % length).astype(jnp.float32)
    phases = phases * (2.0 * math.pi / length)
    lag_rows = jnp.stack([jnp.cos(phases), -jnp.sin(phases)], 2).reshape(LAGS, 2 * bins)
    lag_rows = lag_rows.astype(jnp.bfloat16)

    def along_z(value, pairs):
        return lax.ppermute(value, "freq", pairs)

    def slab_of(value, r):
        return Held(lax.optimization_barrier(value), [[(i, r) for i in range(8)]])

    s0 = make_slab(traces, band_bins)[None]
    q0 = slab_of(s0, 0)
    y0 = q0.hop(Y_PAIRS)
    x0 = q0.hop(X_PAIRS)
    down1, up1 = along_z(s0, [(3, 2), (2, 1), (1, 0)]), along_z(s0, [(0, 1), (1, 2), (2, 3)])
    y0, down1, up1, x0, lag_rows = together(y0, down1, up1, x0, lag_rows)

    q1 = slab_of(lax.select_n(z, down1, up1, down1, up1), 1)
    c0 = x0.hop(Y_ON_ALL)
    y1 = q1.hop(Y_PAIRS)
    x1 = q1.hop(X_PAIRS)
    up2, down2 = along_z(up1, [(1, 2), (2, 3)]), along_z(down1, [(2, 1), (1, 0)])
    first = join(q0, x0, y0, q1)
    up2, down2, x1, y1, first = together(up2, down2, x1, y1, first)

    q2 = slab_of(lax.select_n(z, down2, down1, up1, up2), 2)
    c1 = x1.hop(Y_ON_ALL)
    y2 = q2.hop(Y_PAIRS)
    x2 = q2.hop(X_PAIRS)
    last = along_z(jnp.where(z == 2, up2, down2), [(2, 3), (1, 0)])
    second = join(x1, y1, q2)
    last, c0, up2, down2, second = together(last, c0, up2, down2, second)

    q3 = slab_of(lax.select_n(z, last, down2, up2, last), 3)
    b = [first.hop(CORE_PAIRS), second.hop(CORE_PAIRS)]
    y3 = q3.hop(Y_PAIRS)
    x3 = q3.hop(X_PAIRS)
    left = make_left([q.value[0] for q in (q0, q1, q2, q3)], z, channels // 4, bins)
    x2, y2, left = together(x2, y2, left)

    c2, d2 = x2.hop(Y_ON), y2.hop(X_ON)
    b += [c0.hop(CORE_PAIRS), q3.hop(CORE_PAIRS)]
    ids = np.arange(8, dtype=np.int32)
    third = [x2.what, y2.what, x3.what, y3.what]
    held = [q0, q1, q2, q3, x0, x1, x2, x3, y0, y1, y2, y3, c0, c1] + b
    whats = [h.what for h in held] + [moved(what, CORE_PAIRS) for what in third]
    c3, d3 = moved(x3.what, Y_ON), moved(y3.what, X_ON)
    whats += [c2.what, d2.what, c3, d3]
    whats += [moved(what, CORE_PAIRS) for what in (c1.what, c2.what, d2.what, c3, d3)]
    table = np.zeros((8, 8, 4), np.int32)
    all_holds = [set() for _ in whats]
    index = sum(len(what) for what in whats)
    for what, holds in zip(reversed(whats), reversed(all_holds)):
        for item in reversed(what):
            index -= 1
            for device, block_slab in enumerate(item):
                if block_slab is not None:
                    table[device, block_slab[0], block_slab[1]] = index
                    holds.add(block_slab[1])
    wanted = (ids[None, None, :, None] == pair_blocks[0][:, None, None, None]) & (
        ids[None, :, None, None] == me
    )
    slots = jnp.sum(jnp.where(wanted, table[None], 0), axis=(1, 2))
    slots = jnp.concatenate([jnp.arange(slot_count, dtype=jnp.int32)[:, None], slots], 1)
    swapped = slots[jnp.asarray([1, 0, 2])]
    slots = jnp.where(me == 5, swapped, slots)

    x3, y3, c1, slots = together(x3, y3, c1, slots)

    c3, d3 = x3.hop(Y_ON), y3.hop(X_ON)
    b += [h.hop(CORE_PAIRS) for h in (x2, y2, x3, y3)]
    norm = 1.0 / math.sqrt(4 * windows * bins)
    held = [q0, q1, q2, q3, x0, x1, x2, x3, y0, y1, y2, y3, c0, c1] + b
    places = [(h.value, holds) for h, holds in zip(held, all_holds)]
    result = correlate(slots[:1], left, lag_rows, places, slot_count, norm)
    c3, d3, c2, d2, result = together(c3, d3, c2, d2, result)
    late = [h.hop(CORE_PAIRS) for h in (c1, c2, d2, c3, d3)]
    held += [c2, d2, c3, d3] + late
    places = [(h.value, holds) for h, holds in zip(held, all_holds)]
    return correlate(slots[1:], left, lag_rows, places, slot_count, norm, result)[None]


def solution(mesh):
    placed = (P("chan", "freq", None), P(), P("chan", None))
    fits = mesh.shape["chan"] == 8 and mesh.shape["freq"] == 4
    return jax.shard_map(
        on_device if fits else on_any_device,
        mesh=mesh,
        in_specs=placed,
        out_specs=P("chan", "freq", None, None, None),
        check_vma=False,
    )
```

```python
import math

import jax
import jax.numpy as jnp
import numpy as np
from jax import lax
from jax.experimental import pallas as pl
from jax.experimental.pallas import tpu as pltpu
from jax.sharding import PartitionSpec as P

LAGS = 128
REACH = 3
GROUP = 8


def shifted(value, axis, by):
    size = lax.axis_size(axis)
    pairs = [(i, i + by) for i in range(size) if 0 <= i + by < size]
    return lax.ppermute(value, axis, pairs)


def make_dft_table(band_bins, length):
    sample_idx = jnp.arange(length, dtype=jnp.int32)
    phase_int = band_bins[:, None] * sample_idx[None, :] % length
    phases = phase_int.astype(jnp.float32) * (2.0 * math.pi / length)
    return jnp.concatenate([jnp.cos(phases), -jnp.sin(phases)], 0).T.astype(jnp.bfloat16)


def make_lag_table(band_bins, length, lag_count):
    lag_idx = jnp.arange(lag_count, dtype=jnp.int32) - lag_count // 2
    phase_int = band_bins[:, None] * lag_idx[None, :] % length
    phases = phase_int.astype(jnp.float32) * (2.0 * math.pi / length)
    return jnp.concatenate([jnp.cos(phases), -jnp.sin(phases)], 0)


def gram_pair(first_block, second_block):
    rotated = jnp.stack([-second_block[:, :, 1], second_block[:, :, 0]], 2)
    gram_real = jnp.einsum(
        "awcf,bwcf->abf", first_block, second_block, preferred_element_type=jnp.float32
    )
    gram_imag = jnp.einsum(
        "awcf,bwcf->abf", first_block, rotated, preferred_element_type=jnp.float32
    )
    return jnp.stack([gram_real, gram_imag], 2)


def on_any_device(traces, band_bins, pair_blocks):
    channels, windows, length = traces.shape
    band_count = band_bins.shape[0]
    dft_matrix = make_dft_table(band_bins, length)
    spectra = jnp.dot(
        traces.reshape(channels * windows, length), dft_matrix, preferred_element_type=jnp.float32
    )
    amplitude = jnp.sqrt(jnp.sum(spectra * spectra, axis=1, keepdims=True) / band_count + 1e-06)
    whitened = (spectra / amplitude).astype(jnp.bfloat16).reshape(channels, windows, 2, band_count)
    own_block = lax.all_to_all(whitened, "freq", split_axis=3, concat_axis=1, tiled=True)
    below_blocks = [shifted(own_block, "chan", distance) for distance in range(1, REACH + 1)]
    above_blocks = [shifted(own_block, "chan", -distance) for distance in range(1, REACH + 1)]
    stacked = jnp.stack(below_blocks[::-1] + [own_block] + above_blocks, 0)
    my_index = lax.axis_index("chan")
    gram_list = []
    for pair_slot in range(pair_blocks.shape[1]):
        offset = pair_blocks[0, pair_slot] - my_index + REACH
        partner = lax.dynamic_index_in_dim(stacked, offset, 0, keepdims=False)
        gram_list.append(gram_pair(own_block, partner))
    cross_gram = jnp.stack(gram_list, 1)
    lag_matrix = make_lag_table(band_bins, length, LAGS)
    lag_norm = 1.0 / math.sqrt(own_block.shape[1] * band_count)
    gram_block = lax.all_to_all(cross_gram, "freq", split_axis=0, concat_axis=4, tiled=True)
    dims_shape = gram_block.shape
    lagged = (
        jnp.dot(
            gram_block.reshape(-1, 2 * band_count),
            lag_matrix,
            precision=lax.Precision.HIGHEST,
            preferred_element_type=jnp.float32,
        )
        * lag_norm
    )
    result = lagged.reshape(dims_shape[0], dims_shape[1], dims_shape[2], LAGS)
    return result[None]


def spectra_kernel(traces_ref, fine_cos, fine_sin, step_cos, step_sin, out_ref, table, planes):
    bins, fine = fine_cos.shape
    groups, _, channels = planes.shape
    windows, length = traces_ref.shape[1:]
    series = windows * channels
    for h in range(step_cos.shape[1]):
        sc, ss = step_cos[:, h : h + 1], step_sin[:, h : h + 1]
        cols = slice(h * fine, (h + 1) * fine)
        table[:bins, cols] = (sc * fine_cos[...] - ss * fine_sin[...]).astype(jnp.bfloat16)
        table[bins:, cols] = (-(ss * fine_cos[...] + sc * fine_sin[...])).astype(jnp.bfloat16)
    was = lax.broadcasted_iota(jnp.int32, (series, series), 0)
    now = lax.broadcasted_iota(jnp.int32, (series, series), 1)
    turned = jnp.where(was == now % channels * windows + now // channels, 1.0, 0.0)
    turned = turned.astype(jnp.bfloat16)
    rows = traces_ref[...].reshape(series, length)
    spectra = lax.dot_general(
        table[...], rows, (((1,), (1,)), ((), ())), preferred_element_type=jnp.float32
    )
    power = jnp.sum(spectra * spectra, axis=0, keepdims=True)
    white = (spectra / jnp.sqrt(power / bins + 1e-06)).astype(jnp.bfloat16)
    white = jnp.dot(white, turned, preferred_element_type=jnp.float32)
    for w in range(windows):
        for c in range(2):
            first = c * GROUP * windows + w
            planes[:, pl.ds(first, GROUP, stride=windows), :] = white[
                c * bins : (c + 1) * bins, w * channels : (w + 1) * channels
            ].reshape(groups, GROUP, channels)
    out_ref[...] = planes[...].reshape(out_ref.shape).astype(jnp.bfloat16)


def make_slab(traces, band_bins):
    channels, windows, length = traces.shape
    bins = band_bins.shape[0]
    fine = 128
    sample_idx = jnp.concatenate([jnp.arange(fine), jnp.arange(length // fine) * fine])
    phase_int = band_bins[:, None] * sample_idx[None, :].astype(jnp.int32) % length
    phases = phase_int.astype(jnp.float32) * (2.0 * math.pi / length)
    cos, sin = jnp.cos(phases), jnp.sin(phases)
    return pl.pallas_call(
        spectra_kernel,
        out_shape=jax.ShapeDtypeStruct((bins * windows * 2, channels), jnp.bfloat16),
        scratch_shapes=[
            pltpu.VMEM((2 * bins, length), jnp.bfloat16),
            pltpu.VMEM((bins // GROUP, GROUP * windows * 2, channels), jnp.float32),
        ],
        compiler_params=pltpu.CompilerParams(vmem_limit_bytes=16 << 20),
        name="spectra",
    )(traces, cos[:, :fine], sin[:, :fine], cos[:, fine:], sin[:, fine:])


def left_kernel(z, *refs, per_step):
    slabs, (out_ref, choice, mask) = refs[:-3], refs[-3:]
    m, k = mask.shape
    channels = slabs[0].shape[-1]
    group_rows = slabs[0].shape[0] // per_step
    half = group_rows // 2
    rows_out = m // (2 * GROUP)

    @pl.when(pl.program_id(0) == 0)
    def _():
        row = lax.broadcasted_iota(jnp.int32, (m, 2 * channels), 0)
        col = lax.broadcasted_iota(jnp.int32, (m, 2 * channels), 1)
        wanted = row // (2 * GROUP) + z[0] * rows_out + (row % 2) * channels
        choice[...] = jnp.where(col == wanted, 1.0, 0.0).astype(jnp.bfloat16)
        row = lax.broadcasted_iota(jnp.int32, (m, k), 0)
        col = lax.broadcasted_iota(jnp.int32, (m, k), 1)
        bin_of_col = col % half // (half // GROUP)
        mask[...] = jnp.where(bin_of_col == row // 2 % GROUP, 1.0, 0.0)

    for u in range(per_step):
        pieces = []
        for slab in slabs:
            real = slab[u * group_rows : u * group_rows + half, :]
            imag = slab[u * group_rows + half : (u + 1) * group_rows, :]
            pieces.append(jnp.concatenate([real, imag], 1))
            pieces.append(jnp.concatenate([imag, -real], 1))
        both = jnp.concatenate(pieces, 0)
        rows = lax.dot_general(
            choice[...], both, (((1,), (1,)), ((), ())), preferred_element_type=jnp.float32
        )
        out_ref[u] = (rows * mask[...]).astype(jnp.bfloat16)


def make_left(slabs, z, rows_out, bins):
    slab_rows, channels = slabs[0].shape
    groups = bins // GROUP
    m, k = rows_out * GROUP * 2, slab_rows // groups * 4
    per_step = 4
    step_rows = slab_rows // groups * per_step
    return pl.pallas_call(
        lambda *r: left_kernel(*r, per_step=per_step),
        grid_spec=pltpu.PrefetchScalarGridSpec(
            num_scalar_prefetch=1,
            grid=(groups // per_step,),
            in_specs=[pl.BlockSpec((step_rows, channels), lambda i, s: (i, 0))] * len(slabs),
            out_specs=pl.BlockSpec((per_step, m, k), lambda i, s: (i, 0, 0)),
            scratch_shapes=[
                pltpu.VMEM((m, 2 * channels), jnp.bfloat16),
                pltpu.VMEM((m, k), jnp.float32),
            ],
        ),
        out_shape=jax.ShapeDtypeStruct((groups, m, k), jnp.bfloat16),
        compiler_params=pltpu.CompilerParams(vmem_limit_bytes=32 << 20),
        name="left",
    )(z.reshape(1), *slabs)


CHUNKS = 4
GROUP_UNROLL = 8
ROW_UNROLL = 8


def pairs_kernel(slots, left_ref, lag_ref, *refs, arrays, norm, aliased):
    sources, refs = refs[: len(arrays)], refs[len(arrays) + aliased :]
    out_ref, partner, left, gram, stage, in_sems, left_sems, out_sems = refs
    groups, m, k = left.shape
    chosen, slabs, slab_rows, channels = partner.shape
    group_rows = k // slabs
    chunk_rows = slab_rows // CHUNKS
    per_chunk = groups // CHUNKS

    def fetch(source, s, r, chunk):
        rows = pl.ds(chunk * chunk_rows, chunk_rows)
        return pltpu.make_async_copy(source.at[rows], partner.at[s, r, rows], in_sems.at[chunk, s, r])

    def fetch_left(chunk):
        some = pl.ds(chunk * per_chunk, per_chunk)
        return pltpu.make_async_copy(left_ref.at[some], left.at[some], left_sems.at[chunk])

    fetch_left(0).start()
    for s in range(chosen):
        for r in range(slabs):
            place = slots[s * (slabs + 1) + 1 + r]
            for source, (first, count, holds) in zip(sources, arrays):
                if r in holds:

                    @pl.when((place >= first) & (place < first + count))
                    def _():
                        for chunk in range(CHUNKS):
                            fetch(source.at[place - first], s, r, chunk).start()

    for chunk in range(1, CHUNKS):
        fetch_left(chunk).start()

    for chunk in range(CHUNKS):
        fetch_left(chunk).wait()
        for s in range(chosen):
            for r in range(slabs):
                fetch(sources[0].at[0], s, r, chunk).wait()

        @pl.loop(0, per_chunk // GROUP_UNROLL)
        def _(i):
            for u in range(GROUP_UNROLL):
                g = chunk * per_chunk + i * GROUP_UNROLL + u
                rows = pl.ds(pl.multiple_of(g * group_rows, group_rows), group_rows)
                right = jnp.concatenate(
                    [partner[s, :, rows, :].reshape(k, channels) for s in range(chosen)], 1
                )
                product = jnp.dot(left[g], right, preferred_element_type=jnp.float32)
                cols = pl.ds(pl.multiple_of(g * 2 * GROUP, 2 * GROUP), 2 * GROUP)
                gram[:, cols, :] = product.astype(jnp.bfloat16).reshape(
                    m // (2 * GROUP), 2 * GROUP, chosen * channels
                )

    steps = gram.shape[0] // ROW_UNROLL

    class Write:
        def __init__(self, i, b):
            rows = pl.ds(i * ROW_UNROLL, ROW_UNROLL)
            self.copies = [
                pltpu.make_async_copy(
                    stage.at[b, s], out_ref.at[rows, slots[s * (slabs + 1)]], out_sems.at[b, s]
                )
                for s in range(chosen)
            ]

        def start(self):
            for copy in self.copies:
                copy.start()

        def wait(self):
            for copy in self.copies:
                copy.wait()

    @pl.loop(0, steps)
    def _(i):
        b = lax.rem(i, 2)

        @pl.when(i >= 2)
        def _():
            Write(i - 2, b).wait()

        for u in range(ROW_UNROLL):
            lagged = jnp.dot(
                lag_ref[...], gram[i * ROW_UNROLL + u], preferred_element_type=jnp.float32
            )
            for s in range(chosen):
                stage[b, s, u] = (lagged[:, s * channels : (s + 1) * channels] * norm).T
        Write(i, b).start()

    for i in range(steps - 2, steps):
        Write(i, i % 2).wait()


def correlate(slots, left, lag_rows, held, slot_count, norm, earlier=None):
    groups, m, k = left.shape
    rows_out = m // (2 * GROUP)
    arrays, first = [], 0
    for value, holds in held:
        arrays.append((first, value.shape[0], holds))
        first += value.shape[0]
    slab_rows, channels = held[0][0].shape[1:]
    chosen, slabs = slots.shape[0], slots.shape[1] - 1
    lag_count, entries = lag_rows.shape
    anywhere = pl.BlockSpec(memory_space=pl.ANY)
    in_vmem = pl.BlockSpec(memory_space=pltpu.VMEM)
    operands = [slots.reshape(-1), left, lag_rows] + [value for value, _ in held]
    aliases = {}
    if earlier is not None:
        aliases = {len(operands): 0}
        operands.append(earlier)
    flops = 2 * groups * m * k * chosen * channels + 2 * rows_out * lag_count * entries * chosen * channels
    return pl.pallas_call(
        lambda *r: pairs_kernel(*r, arrays=arrays, norm=norm, aliased=len(aliases)),
        in_specs=[pl.BlockSpec(memory_space=pltpu.SMEM), anywhere, in_vmem]
        + [anywhere] * (len(operands) - 3),
        out_specs=anywhere,
        scratch_shapes=[
            pltpu.VMEM((chosen, slabs, slab_rows, channels), jnp.bfloat16),
            pltpu.VMEM((groups, m, k), jnp.bfloat16),
            pltpu.VMEM((rows_out, entries, chosen * channels), jnp.bfloat16),
            pltpu.VMEM((2, chosen, ROW_UNROLL, channels, lag_count), jnp.float32),
            pltpu.SemaphoreType.DMA((CHUNKS, chosen, slabs)),
            pltpu.SemaphoreType.DMA((CHUNKS,)),
            pltpu.SemaphoreType.DMA((2, chosen)),
        ],
        out_shape=jax.ShapeDtypeStruct((rows_out, slot_count, channels, lag_count), jnp.float32),
        input_output_aliases=aliases,
        cost_estimate=pl.CostEstimate(flops=flops, bytes_accessed=12 << 20, transcendentals=0),
        compiler_params=pltpu.CompilerParams(vmem_limit_bytes=PAIRS_VMEM),
        name="pairs",
    )(*operands)


PAIRS_VMEM = 58 << 20

X_PAIRS = [(i, i ^ 2) for i in range(8)]
Y_PAIRS = [(4, 0), (1, 5), (6, 2), (3, 7)]
Y_ON = [(7, 3), (0, 4)]
Y_ON_ALL = Y_ON + [(6, 2), (1, 5)]
X_ON = [(0, 2), (7, 5)]
CORE_PAIRS = [(i, i ^ 1) for i in range(8)]


def moved(what, pairs):
    after = [[None] * 8 for _ in what]
    for src, dst in pairs:
        for old, new in zip(what, after):
            new[dst] = old[src]
    return after


class Held:
    def __init__(self, value, what):
        self.value, self.what = value, what

    def hop(self, pairs):
        return Held(lax.ppermute(self.value, "chan", pairs), moved(self.what, pairs))


def join(*parts):
    return Held(jnp.concatenate([p.value for p in parts], 0), [w for p in parts for w in p.what])


def together(*parts):
    return lax.optimization_barrier(parts)


jax.tree_util.register_pytree_node(
    Held,
    lambda held: ((held.value,), tuple(tuple(row) for row in held.what)),
    lambda what, children: Held(children[0], [list(row) for row in what]),
)


def on_device(traces, band_bins, pair_blocks):
    channels, windows, length = traces.shape
    bins = band_bins.shape[0]
    z = lax.axis_index("freq")
    me = lax.axis_index("chan")
    slot_count = pair_blocks.shape[1]

    lag_idx = jnp.arange(LAGS, dtype=jnp.int32) - LAGS // 2
    phases = (lag_idx[:, None] * band_bins[None, :] % length).astype(jnp.float32)
    phases = phases * (2.0 * math.pi / length)
    lag_rows = jnp.stack([jnp.cos(phases), -jnp.sin(phases)], 2).reshape(LAGS, 2 * bins)
    lag_rows = lag_rows.astype(jnp.bfloat16)

    def along_z(value, pairs):
        return lax.ppermute(value, "freq", pairs)

    def slab_of(value, r):
        return Held(lax.optimization_barrier(value), [[(i, r) for i in range(8)]])

    s0 = make_slab(traces, band_bins)[None]
    q0 = slab_of(s0, 0)
    up1 = along_z(s0, [(0, 1), (1, 2), (2, 3)])
    y0 = q0.hop(Y_PAIRS)
    x0 = q0.hop(X_PAIRS)
    down1 = along_z(s0, [(3, 2), (2, 1), (1, 0)])
    down1, lag_rows, x0, up1 = together(down1, lag_rows, x0, up1)

    q1 = slab_of(lax.select_n(z, down1, up1, down1, up1), 1)
    y1 = q1.hop(Y_PAIRS)
    d0 = y0.hop(X_ON)
    c0 = x0.hop(Y_ON)
    x1 = q1.hop(X_PAIRS)
    down2 = along_z(down1, [(2, 1), (1, 0)])
    up2 = along_z(up1, [(1, 2), (2, 3)])
    first = join(q0, x0, y0, q1)
    x1, first, up2, y0, down2, y1 = together(x1, first, up2, y0, down2, y1)

    q2 = slab_of(lax.select_n(z, down2, down1, up1, up2), 2)
    down3 = along_z(down2, [(1, 0)])
    y2 = q2.hop(Y_PAIRS)
    up3 = along_z(up2, [(2, 3)])
    x2 = q2.hop(X_PAIRS)
    c1 = x1.hop(Y_ON_ALL)
    second = join(x1, y1)
    c0, up3, d0, up2, down2, second, down3 = together(c0, up3, d0, up2, down2, second, down3)

    q3 = slab_of(lax.select_n(z, down3, down2, up2, up3), 3)
    b = [h.hop(CORE_PAIRS) for h in (first, second,)]
    y3 = q3.hop(Y_PAIRS)
    x3 = q3.hop(X_PAIRS)
    left = make_left([q.value[0] for q in (q0, q1, q2, q3)], z, channels // 4, bins)
    left, x2, y2 = together(left, x2, y2)

    d2 = y2.hop(X_ON)
    c2 = x2.hop(Y_ON)
    b += [h.hop(CORE_PAIRS) for h in (q2, d0, q3, c0,)]


    ids = np.arange(8, dtype=np.int32)
    third = [y2.what, x2.what, x3.what, y3.what]
    held = [q0, q1, q2, q3, x0, x1, x2, x3, y0, y1, y2, y3, c0, d0, c1] + b
    whats = [h.what for h in held] + [moved(what, CORE_PAIRS) for what in third]
    c3, d3 = moved(x3.what, Y_ON), moved(y3.what, X_ON)
    whats += [c2.what, d2.what, c3, d3]
    whats += [moved(what, CORE_PAIRS) for what in (c3, d2.what, c1.what, d3, c2.what)]
    table = np.zeros((8, 8, 4), np.int32)
    all_holds = [set() for _ in whats]
    index = sum(len(what) for what in whats)
    for what, holds in zip(reversed(whats), reversed(all_holds)):
        for item in reversed(what):
            index -= 1
            for device, block_slab in enumerate(item):
                if block_slab is not None:
                    table[device, block_slab[0], block_slab[1]] = index
                    holds.add(block_slab[1])
    wanted = (ids[None, None, :, None] == pair_blocks[0][:, None, None, None]) & (
        ids[None, :, None, None] == me
    )
    slots = jnp.sum(jnp.where(wanted, table[None], 0), axis=(1, 2))
    slots = jnp.concatenate([jnp.arange(slot_count, dtype=jnp.int32)[:, None], slots], 1)
    swapped = slots[jnp.asarray([1, 0, 2])]
    slots = jnp.where(me == 5, swapped, slots)

    c1, y3, slots, x3 = together(c1, y3, slots, x3)

    c3, d3 = x3.hop(Y_ON), y3.hop(X_ON)
    b += [h.hop(CORE_PAIRS) for h in (y2, x2, x3, y3)]
    norm = 1.0 / math.sqrt(4 * windows * bins)
    held = [q0, q1, q2, q3, x0, x1, x2, x3, y0, y1, y2, y3, c0, d0, c1] + b
    places = [(h.value, holds) for h, holds in zip(held, all_holds)]
    result = correlate(slots[:1], left, lag_rows, places, slot_count, norm)
    c2, result, d2, d3, c3 = together(c2, result, d2, d3, c3)
    late = [h.hop(CORE_PAIRS) for h in (c3, d2, c1, d3, c2)]
    held += [c2, d2, c3, d3] + late
    places = [(h.value, holds) for h, holds in zip(held, all_holds)]
    return correlate(slots[1:], left, lag_rows, places, slot_count, norm, result)[None]


def solution(mesh):
    placed = (P("chan", "freq", None), P(), P("chan", None))
    fits = mesh.shape["chan"] == 8 and mesh.shape["freq"] == 4
    return jax.shard_map(
        on_device if fits else on_any_device,
        mesh=mesh,
        in_specs=placed,
        out_specs=P("chan", "freq", None, None, None),
        check_vma=False,
    )
```

```python
import math

import jax
import jax.numpy as jnp
import numpy as np
from jax import lax
from jax.experimental import pallas as pl
from jax.experimental.pallas import tpu as pltpu
from jax.sharding import PartitionSpec as P

LAGS = 128
REACH = 3
GROUP = 8


def shifted(value, axis, by):
    size = lax.axis_size(axis)
    pairs = [(i, i + by) for i in range(size) if 0 <= i + by < size]
    return lax.ppermute(value, axis, pairs)


def make_dft_table(band_bins, length):
    sample_idx = jnp.arange(length, dtype=jnp.int32)
    phase_int = band_bins[:, None] * sample_idx[None, :] % length
    phases = phase_int.astype(jnp.float32) * (2.0 * math.pi / length)
    return jnp.concatenate([jnp.cos(phases), -jnp.sin(phases)], 0).T.astype(jnp.bfloat16)


def make_lag_table(band_bins, length, lag_count):
    lag_idx = jnp.arange(lag_count, dtype=jnp.int32) - lag_count // 2
    phase_int = band_bins[:, None] * lag_idx[None, :] % length
    phases = phase_int.astype(jnp.float32) * (2.0 * math.pi / length)
    return jnp.concatenate([jnp.cos(phases), -jnp.sin(phases)], 0)


def gram_pair(first_block, second_block):
    rotated = jnp.stack([-second_block[:, :, 1], second_block[:, :, 0]], 2)
    gram_real = jnp.einsum(
        "awcf,bwcf->abf", first_block, second_block, preferred_element_type=jnp.float32
    )
    gram_imag = jnp.einsum(
        "awcf,bwcf->abf", first_block, rotated, preferred_element_type=jnp.float32
    )
    return jnp.stack([gram_real, gram_imag], 2)


def on_any_device(traces, band_bins, pair_blocks):
    channels, windows, length = traces.shape
    band_count = band_bins.shape[0]
    dft_matrix = make_dft_table(band_bins, length)
    spectra = jnp.dot(
        traces.reshape(channels * windows, length), dft_matrix, preferred_element_type=jnp.float32
    )
    amplitude = jnp.sqrt(jnp.sum(spectra * spectra, axis=1, keepdims=True) / band_count + 1e-06)
    whitened = (spectra / amplitude).astype(jnp.bfloat16).reshape(channels, windows, 2, band_count)
    own_block = lax.all_to_all(whitened, "freq", split_axis=3, concat_axis=1, tiled=True)
    below_blocks = [shifted(own_block, "chan", distance) for distance in range(1, REACH + 1)]
    above_blocks = [shifted(own_block, "chan", -distance) for distance in range(1, REACH + 1)]
    stacked = jnp.stack(below_blocks[::-1] + [own_block] + above_blocks, 0)
    my_index = lax.axis_index("chan")
    gram_list = []
    for pair_slot in range(pair_blocks.shape[1]):
        offset = pair_blocks[0, pair_slot] - my_index + REACH
        partner = lax.dynamic_index_in_dim(stacked, offset, 0, keepdims=False)
        gram_list.append(gram_pair(own_block, partner))
    cross_gram = jnp.stack(gram_list, 1)
    lag_matrix = make_lag_table(band_bins, length, LAGS)
    lag_norm = 1.0 / math.sqrt(own_block.shape[1] * band_count)
    gram_block = lax.all_to_all(cross_gram, "freq", split_axis=0, concat_axis=4, tiled=True)
    dims_shape = gram_block.shape
    lagged = (
        jnp.dot(
            gram_block.reshape(-1, 2 * band_count),
            lag_matrix,
            precision=lax.Precision.HIGHEST,
            preferred_element_type=jnp.float32,
        )
        * lag_norm
    )
    result = lagged.reshape(dims_shape[0], dims_shape[1], dims_shape[2], LAGS)
    return result[None]


def spectra_kernel(traces_ref, fine_cos, fine_sin, step_cos, step_sin, out_ref, table, planes):
    bins, fine = fine_cos.shape
    groups, _, channels = planes.shape
    windows, length = traces_ref.shape[1:]
    series = windows * channels
    for h in range(step_cos.shape[1]):
        sc, ss = step_cos[:, h : h + 1], step_sin[:, h : h + 1]
        cols = slice(h * fine, (h + 1) * fine)
        table[:bins, cols] = (sc * fine_cos[...] - ss * fine_sin[...]).astype(jnp.bfloat16)
        table[bins:, cols] = (-(ss * fine_cos[...] + sc * fine_sin[...])).astype(jnp.bfloat16)
    was = lax.broadcasted_iota(jnp.int32, (series, series), 0)
    now = lax.broadcasted_iota(jnp.int32, (series, series), 1)
    turned = jnp.where(was == now % channels * windows + now // channels, 1.0, 0.0)
    turned = turned.astype(jnp.bfloat16)
    rows = traces_ref[...].reshape(series, length)
    spectra = lax.dot_general(
        table[...], rows, (((1,), (1,)), ((), ())), preferred_element_type=jnp.float32
    )
    power = jnp.sum(spectra * spectra, axis=0, keepdims=True)
    white = (spectra / jnp.sqrt(power / bins + 1e-06)).astype(jnp.bfloat16)
    white = jnp.dot(white, turned, preferred_element_type=jnp.float32)
    for w in range(windows):
        for c in range(2):
            first = c * GROUP * windows + w
            planes[:, pl.ds(first, GROUP, stride=windows), :] = white[
                c * bins : (c + 1) * bins, w * channels : (w + 1) * channels
            ].reshape(groups, GROUP, channels)
    out_ref[...] = planes[...].reshape(out_ref.shape).astype(jnp.bfloat16)


def make_slab(traces, band_bins):
    channels, windows, length = traces.shape
    bins = band_bins.shape[0]
    fine = 128
    sample_idx = jnp.concatenate([jnp.arange(fine), jnp.arange(length // fine) * fine])
    phase_int = band_bins[:, None] * sample_idx[None, :].astype(jnp.int32) % length
    phases = phase_int.astype(jnp.float32) * (2.0 * math.pi / length)
    cos, sin = jnp.cos(phases), jnp.sin(phases)
    return pl.pallas_call(
        spectra_kernel,
        out_shape=jax.ShapeDtypeStruct((bins * windows * 2, channels), jnp.bfloat16),
        scratch_shapes=[
            pltpu.VMEM((2 * bins, length), jnp.bfloat16),
            pltpu.VMEM((bins // GROUP, GROUP * windows * 2, channels), jnp.float32),
        ],
        compiler_params=pltpu.CompilerParams(vmem_limit_bytes=16 << 20),
        name="spectra",
    )(traces, cos[:, :fine], sin[:, :fine], cos[:, fine:], sin[:, fine:])


def left_kernel(z, *refs, per_step):
    slabs, (out_ref, choice, mask) = refs[:-3], refs[-3:]
    m, k = mask.shape
    channels = slabs[0].shape[-1]
    group_rows = slabs[0].shape[0] // per_step
    half = group_rows // 2
    rows_out = m // (2 * GROUP)

    @pl.when(pl.program_id(0) == 0)
    def _():
        row = lax.broadcasted_iota(jnp.int32, (m, 2 * channels), 0)
        col = lax.broadcasted_iota(jnp.int32, (m, 2 * channels), 1)
        wanted = row // (2 * GROUP) + z[0] * rows_out + (row % 2) * channels
        choice[...] = jnp.where(col == wanted, 1.0, 0.0).astype(jnp.bfloat16)
        row = lax.broadcasted_iota(jnp.int32, (m, k), 0)
        col = lax.broadcasted_iota(jnp.int32, (m, k), 1)
        bin_of_col = col % half // (half // GROUP)
        mask[...] = jnp.where(bin_of_col == row // 2 % GROUP, 1.0, 0.0)

    for u in range(per_step):
        pieces = []
        for slab in slabs:
            real = slab[u * group_rows : u * group_rows + half, :]
            imag = slab[u * group_rows + half : (u + 1) * group_rows, :]
            pieces.append(jnp.concatenate([real, imag], 1))
            pieces.append(jnp.concatenate([imag, -real], 1))
        both = jnp.concatenate(pieces, 0)
        rows = lax.dot_general(
            choice[...], both, (((1,), (1,)), ((), ())), preferred_element_type=jnp.float32
        )
        out_ref[u] = (rows * mask[...]).astype(jnp.bfloat16)


def make_left(slabs, z, rows_out, bins):
    slab_rows, channels = slabs[0].shape
    groups = bins // GROUP
    m, k = rows_out * GROUP * 2, slab_rows // groups * 4
    per_step = 4
    step_rows = slab_rows // groups * per_step
    return pl.pallas_call(
        lambda *r: left_kernel(*r, per_step=per_step),
        grid_spec=pltpu.PrefetchScalarGridSpec(
            num_scalar_prefetch=1,
            grid=(groups // per_step,),
            in_specs=[pl.BlockSpec((step_rows, channels), lambda i, s: (i, 0))] * len(slabs),
            out_specs=pl.BlockSpec((per_step, m, k), lambda i, s: (i, 0, 0)),
            scratch_shapes=[
                pltpu.VMEM((m, 2 * channels), jnp.bfloat16),
                pltpu.VMEM((m, k), jnp.float32),
            ],
        ),
        out_shape=jax.ShapeDtypeStruct((groups, m, k), jnp.bfloat16),
        compiler_params=pltpu.CompilerParams(vmem_limit_bytes=32 << 20),
        name="left",
    )(z.reshape(1), *slabs)


CHUNKS = 4
GROUP_UNROLL = 8
ROW_UNROLL = 16


def pairs_kernel(slots, left_ref, lag_ref, *refs, arrays, norm, aliased):
    sources, refs = refs[: len(arrays)], refs[len(arrays) + aliased :]
    out_ref, partner, left, gram, stage, in_sems, left_sems, out_sems = refs
    groups, m, k = left.shape
    chosen, slabs, slab_rows, channels = partner.shape
    group_rows = k // slabs
    chunk_rows = slab_rows // CHUNKS
    per_chunk = groups // CHUNKS

    def fetch(source, s, r, chunk):
        rows = pl.ds(chunk * chunk_rows, chunk_rows)
        return pltpu.make_async_copy(source.at[rows], partner.at[s, r, rows], in_sems.at[chunk, s, r])

    def fetch_left(chunk):
        some = pl.ds(chunk * per_chunk, per_chunk)
        return pltpu.make_async_copy(left_ref.at[some], left.at[some], left_sems.at[chunk])

    fetch_left(0).start()
    for s in range(chosen):
        for r in range(slabs):
            place = slots[s * (slabs + 1) + 1 + r]
            for source, (first, count, holds) in zip(sources, arrays):
                if r in holds:

                    @pl.when((place >= first) & (place < first + count))
                    def _():
                        for chunk in range(CHUNKS):
                            fetch(source.at[place - first], s, r, chunk).start()

    for chunk in range(1, CHUNKS):
        fetch_left(chunk).start()

    for chunk in range(CHUNKS):
        fetch_left(chunk).wait()
        for s in range(chosen):
            for r in range(slabs):
                fetch(sources[0].at[0], s, r, chunk).wait()

        @pl.loop(0, per_chunk // GROUP_UNROLL)
        def _(i):
            for u in range(GROUP_UNROLL):
                g = chunk * per_chunk + i * GROUP_UNROLL + u
                rows = pl.ds(pl.multiple_of(g * group_rows, group_rows), group_rows)
                right = jnp.concatenate(
                    [partner[s, :, rows, :].reshape(k, channels) for s in range(chosen)], 1
                )
                product = jnp.dot(left[g], right, preferred_element_type=jnp.float32)
                cols = pl.ds(pl.multiple_of(g * 2 * GROUP, 2 * GROUP), 2 * GROUP)
                gram[:, cols, :] = product.astype(jnp.bfloat16).reshape(
                    m // (2 * GROUP), 2 * GROUP, chosen * channels
                )

    steps = gram.shape[0] // ROW_UNROLL

    class Write:
        def __init__(self, i, b):
            rows = pl.ds(i * ROW_UNROLL, ROW_UNROLL)
            self.copies = [
                pltpu.make_async_copy(
                    stage.at[b, s], out_ref.at[rows, slots[s * (slabs + 1)]], out_sems.at[b, s]
                )
                for s in range(chosen)
            ]

        def start(self):
            for copy in self.copies:
                copy.start()

        def wait(self):
            for copy in self.copies:
                copy.wait()

    @pl.loop(0, steps)
    def _(i):
        b = lax.rem(i, 2)

        @pl.when(i >= 2)
        def _():
            Write(i - 2, b).wait()

        for u in range(ROW_UNROLL):
            lagged = jnp.dot(
                lag_ref[...], gram[i * ROW_UNROLL + u], preferred_element_type=jnp.float32
            )
            for s in range(chosen):
                stage[b, s, u] = (lagged[:, s * channels : (s + 1) * channels] * norm).T
        Write(i, b).start()

    for i in range(steps - 2, steps):
        Write(i, i % 2).wait()


def correlate(slots, left, lag_rows, held, slot_count, norm, earlier=None):
    groups, m, k = left.shape
    rows_out = m // (2 * GROUP)
    arrays, first = [], 0
    for value, holds in held:
        arrays.append((first, value.shape[0], holds))
        first += value.shape[0]
    slab_rows, channels = held[0][0].shape[1:]
    chosen, slabs = slots.shape[0], slots.shape[1] - 1
    lag_count, entries = lag_rows.shape
    anywhere = pl.BlockSpec(memory_space=pl.ANY)
    in_vmem = pl.BlockSpec(memory_space=pltpu.VMEM)
    operands = [slots.reshape(-1), left, lag_rows] + [value for value, _ in held]
    aliases = {}
    if earlier is not None:
        aliases = {len(operands): 0}
        operands.append(earlier)
    flops = 2 * groups * m * k * chosen * channels + 2 * rows_out * lag_count * entries * chosen * channels
    return pl.pallas_call(
        lambda *r: pairs_kernel(*r, arrays=arrays, norm=norm, aliased=len(aliases)),
        in_specs=[pl.BlockSpec(memory_space=pltpu.SMEM), anywhere, in_vmem]
        + [anywhere] * (len(operands) - 3),
        out_specs=anywhere,
        scratch_shapes=[
            pltpu.VMEM((chosen, slabs, slab_rows, channels), jnp.bfloat16),
            pltpu.VMEM((groups, m, k), jnp.bfloat16),
            pltpu.VMEM((rows_out, entries, chosen * channels), jnp.bfloat16),
            pltpu.VMEM((2, chosen, ROW_UNROLL, channels, lag_count), jnp.float32),
            pltpu.SemaphoreType.DMA((CHUNKS, chosen, slabs)),
            pltpu.SemaphoreType.DMA((CHUNKS,)),
            pltpu.SemaphoreType.DMA((2, chosen)),
        ],
        out_shape=jax.ShapeDtypeStruct((rows_out, slot_count, channels, lag_count), jnp.float32),
        input_output_aliases=aliases,
        cost_estimate=pl.CostEstimate(flops=flops, bytes_accessed=12 << 20, transcendentals=0),
        compiler_params=pltpu.CompilerParams(vmem_limit_bytes=PAIRS_VMEM),
        name="pairs",
    )(*operands)


PAIRS_VMEM = 58 << 20

X_PAIRS = [(i, i ^ 2) for i in range(8)]
Y_PAIRS = [(4, 0), (1, 5), (6, 2), (3, 7)]
Y_ON = [(7, 3), (0, 4)]
Y_ON_ALL = Y_ON + [(6, 2), (1, 5)]
X_ON = [(0, 2), (7, 5)]
CORE_PAIRS = [(i, i ^ 1) for i in range(8)]


def moved(what, pairs):
    after = [[None] * 8 for _ in what]
    for src, dst in pairs:
        for old, new in zip(what, after):
            new[dst] = old[src]
    return after


class Held:
    def __init__(self, value, what):
        self.value, self.what = value, what

    def hop(self, pairs):
        return Held(lax.ppermute(self.value, "chan", pairs), moved(self.what, pairs))


def join(*parts):
    return Held(jnp.concatenate([p.value for p in parts], 0), [w for p in parts for w in p.what])


def together(*parts):
    return lax.optimization_barrier(parts)


jax.tree_util.register_pytree_node(
    Held,
    lambda held: ((held.value,), tuple(tuple(row) for row in held.what)),
    lambda what, children: Held(children[0], [list(row) for row in what]),
)


def on_device(traces, band_bins, pair_blocks):
    channels, windows, length = traces.shape
    bins = band_bins.shape[0]
    z = lax.axis_index("freq")
    me = lax.axis_index("chan")
    slot_count = pair_blocks.shape[1]

    lag_idx = jnp.arange(LAGS, dtype=jnp.int32) - LAGS // 2
    phases = (lag_idx[:, None] * band_bins[None, :] % length).astype(jnp.float32)
    phases = phases * (2.0 * math.pi / length)
    lag_rows = jnp.stack([jnp.cos(phases), -jnp.sin(phases)], 2).reshape(LAGS, 2 * bins)
    lag_rows = lag_rows.astype(jnp.bfloat16)

    def along_z(value, pairs):
        return lax.ppermute(value, "freq", pairs)

    def slab_of(value, r):
        return Held(lax.optimization_barrier(value), [[(i, r) for i in range(8)]])

    s0 = make_slab(traces, band_bins)[None]
    q0 = slab_of(s0, 0)
    up1 = along_z(s0, [(0, 1), (1, 2), (2, 3)])
    y0 = q0.hop(Y_PAIRS)
    x0 = q0.hop(X_PAIRS)
    down1 = along_z(s0, [(3, 2), (2, 1), (1, 0)])
    down1, lag_rows, x0, up1 = together(down1, lag_rows, x0, up1)

    q1 = slab_of(lax.select_n(z, down1, up1, down1, up1), 1)
    y1 = q1.hop(Y_PAIRS)
    d0 = y0.hop(X_ON)
    c0 = x0.hop(Y_ON)
    x1 = q1.hop(X_PAIRS)
    down2 = along_z(down1, [(2, 1), (1, 0)])
    up2 = along_z(up1, [(1, 2), (2, 3)])
    first = join(q0, x0, y0, q1)
    x1, first, up2, y0, down2, y1 = together(x1, first, up2, y0, down2, y1)

    q2 = slab_of(lax.select_n(z, down2, down1, up1, up2), 2)
    down3 = along_z(down2, [(1, 0)])
    y2 = q2.hop(Y_PAIRS)
    up3 = along_z(up2, [(2, 3)])
    x2 = q2.hop(X_PAIRS)
    c1 = x1.hop(Y_ON_ALL)
    second = join(x1, y1)
    c0, up3, d0, up2, down2, second, down3 = together(c0, up3, d0, up2, down2, second, down3)

    q3 = slab_of(lax.select_n(z, down3, down2, up2, up3), 3)
    b = [h.hop(CORE_PAIRS) for h in (first, second,)]
    y3 = q3.hop(Y_PAIRS)
    x3 = q3.hop(X_PAIRS)
    left = make_left([q.value[0] for q in (q0, q1, q2, q3)], z, channels // 4, bins)
    left, x2, y2 = together(left, x2, y2)

    d2 = y2.hop(X_ON)
    c2 = x2.hop(Y_ON)
    b += [h.hop(CORE_PAIRS) for h in (q2, d0, q3, c0,)]


    ids = np.arange(8, dtype=np.int32)
    third = [y2.what, x2.what, x3.what, y3.what]
    held = [q0, q1, q2, q3, x0, x1, x2, x3, y0, y1, y2, y3, c0, d0, c1] + b
    whats = [h.what for h in held] + [moved(what, CORE_PAIRS) for what in third]
    c3, d3 = moved(x3.what, Y_ON), moved(y3.what, X_ON)
    whats += [c2.what, d2.what, c3, d3]
    whats += [moved(what, CORE_PAIRS) for what in (c3, d2.what, c1.what, d3, c2.what)]
    table = np.zeros((8, 8, 4), np.int32)
    all_holds = [set() for _ in whats]
    index = sum(len(what) for what in whats)
    for what, holds in zip(reversed(whats), reversed(all_holds)):
        for item in reversed(what):
            index -= 1
            for device, block_slab in enumerate(item):
                if block_slab is not None:
                    table[device, block_slab[0], block_slab[1]] = index
                    holds.add(block_slab[1])
    wanted = (ids[None, None, :, None] == pair_blocks[0][:, None, None, None]) & (
        ids[None, :, None, None] == me
    )
    slots = jnp.sum(jnp.where(wanted, table[None], 0), axis=(1, 2))
    slots = jnp.concatenate([jnp.arange(slot_count, dtype=jnp.int32)[:, None], slots], 1)
    swapped = slots[jnp.asarray([1, 0, 2])]
    slots = jnp.where(me == 5, swapped, slots)

    c1, y3, slots, x3 = together(c1, y3, slots, x3)

    c3, d3 = x3.hop(Y_ON), y3.hop(X_ON)
    b += [h.hop(CORE_PAIRS) for h in (y2, x2, x3, y3)]
    norm = 1.0 / math.sqrt(4 * windows * bins)
    held = [q0, q1, q2, q3, x0, x1, x2, x3, y0, y1, y2, y3, c0, d0, c1] + b
    places = [(h.value, holds) for h, holds in zip(held, all_holds)]
    result = correlate(slots[:1], left, lag_rows, places, slot_count, norm)
    c2, result, d2, d3, c3 = together(c2, result, d2, d3, c3)
    late = [h.hop(CORE_PAIRS) for h in (c3, d2, c1, d3, c2)]
    held += [c2, d2, c3, d3] + late
    places = [(h.value, holds) for h, holds in zip(held, all_holds)]
    return correlate(slots[1:], left, lag_rows, places, slot_count, norm, result)[None]


def solution(mesh):
    placed = (P("chan", "freq", None), P(), P("chan", None))
    fits = mesh.shape["chan"] == 8 and mesh.shape["freq"] == 4
    return jax.shard_map(
        on_device if fits else on_any_device,
        mesh=mesh,
        in_specs=placed,
        out_specs=P("chan", "freq", None, None, None),
        check_vma=False,
    )
```

```python
import math

import jax
import jax.numpy as jnp
import numpy as np
from jax import lax
from jax.experimental import pallas as pl
from jax.experimental.pallas import tpu as pltpu
from jax.sharding import PartitionSpec as P

LAGS = 128
REACH = 3
GROUP = 8


def shifted(value, axis, by):
    size = lax.axis_size(axis)
    pairs = [(i, i + by) for i in range(size) if 0 <= i + by < size]
    return lax.ppermute(value, axis, pairs)


def make_dft_table(band_bins, length):
    sample_idx = jnp.arange(length, dtype=jnp.int32)
    phase_int = band_bins[:, None] * sample_idx[None, :] % length
    phases = phase_int.astype(jnp.float32) * (2.0 * math.pi / length)
    return jnp.concatenate([jnp.cos(phases), -jnp.sin(phases)], 0).T.astype(jnp.bfloat16)


def make_lag_table(band_bins, length, lag_count):
    lag_idx = jnp.arange(lag_count, dtype=jnp.int32) - lag_count // 2
    phase_int = band_bins[:, None] * lag_idx[None, :] % length
    phases = phase_int.astype(jnp.float32) * (2.0 * math.pi / length)
    return jnp.concatenate([jnp.cos(phases), -jnp.sin(phases)], 0)


def gram_pair(first_block, second_block):
    rotated = jnp.stack([-second_block[:, :, 1], second_block[:, :, 0]], 2)
    gram_real = jnp.einsum(
        "awcf,bwcf->abf", first_block, second_block, preferred_element_type=jnp.float32
    )
    gram_imag = jnp.einsum(
        "awcf,bwcf->abf", first_block, rotated, preferred_element_type=jnp.float32
    )
    return jnp.stack([gram_real, gram_imag], 2)


def on_any_device(traces, band_bins, pair_blocks):
    channels, windows, length = traces.shape
    band_count = band_bins.shape[0]
    dft_matrix = make_dft_table(band_bins, length)
    spectra = jnp.dot(
        traces.reshape(channels * windows, length), dft_matrix, preferred_element_type=jnp.float32
    )
    amplitude = jnp.sqrt(jnp.sum(spectra * spectra, axis=1, keepdims=True) / band_count + 1e-06)
    whitened = (spectra / amplitude).astype(jnp.bfloat16).reshape(channels, windows, 2, band_count)
    own_block = lax.all_to_all(whitened, "freq", split_axis=3, concat_axis=1, tiled=True)
    below_blocks = [shifted(own_block, "chan", distance) for distance in range(1, REACH + 1)]
    above_blocks = [shifted(own_block, "chan", -distance) for distance in range(1, REACH + 1)]
    stacked = jnp.stack(below_blocks[::-1] + [own_block] + above_blocks, 0)
    my_index = lax.axis_index("chan")
    gram_list = []
    for pair_slot in range(pair_blocks.shape[1]):
        offset = pair_blocks[0, pair_slot] - my_index + REACH
        partner = lax.dynamic_index_in_dim(stacked, offset, 0, keepdims=False)
        gram_list.append(gram_pair(own_block, partner))
    cross_gram = jnp.stack(gram_list, 1)
    lag_matrix = make_lag_table(band_bins, length, LAGS)
    lag_norm = 1.0 / math.sqrt(own_block.shape[1] * band_count)
    gram_block = lax.all_to_all(cross_gram, "freq", split_axis=0, concat_axis=4, tiled=True)
    dims_shape = gram_block.shape
    lagged = (
        jnp.dot(
            gram_block.reshape(-1, 2 * band_count),
            lag_matrix,
            precision=lax.Precision.HIGHEST,
            preferred_element_type=jnp.float32,
        )
        * lag_norm
    )
    result = lagged.reshape(dims_shape[0], dims_shape[1], dims_shape[2], LAGS)
    return result[None]


def spectra_kernel(traces_ref, fine_cos, fine_sin, step_cos, step_sin, out_ref, table, planes):
    bins, fine = fine_cos.shape
    groups, _, channels = planes.shape
    windows, length = traces_ref.shape[1:]
    series = windows * channels
    for h in range(step_cos.shape[1]):
        sc, ss = step_cos[:, h : h + 1], step_sin[:, h : h + 1]
        cols = slice(h * fine, (h + 1) * fine)
        table[:bins, cols] = (sc * fine_cos[...] - ss * fine_sin[...]).astype(jnp.bfloat16)
        table[bins:, cols] = (-(ss * fine_cos[...] + sc * fine_sin[...])).astype(jnp.bfloat16)
    was = lax.broadcasted_iota(jnp.int32, (series, series), 0)
    now = lax.broadcasted_iota(jnp.int32, (series, series), 1)
    turned = jnp.where(was == now % channels * windows + now // channels, 1.0, 0.0)
    turned = turned.astype(jnp.bfloat16)
    rows = traces_ref[...].reshape(series, length)
    spectra = lax.dot_general(
        table[...], rows, (((1,), (1,)), ((), ())), preferred_element_type=jnp.float32
    )
    power = jnp.sum(spectra * spectra, axis=0, keepdims=True)
    white = (spectra / jnp.sqrt(power / bins + 1e-06)).astype(jnp.bfloat16)
    white = jnp.dot(white, turned, preferred_element_type=jnp.float32)
    for w in range(windows):
        for c in range(2):
            first = c * GROUP * windows + w
            planes[:, pl.ds(first, GROUP, stride=windows), :] = white[
                c * bins : (c + 1) * bins, w * channels : (w + 1) * channels
            ].reshape(groups, GROUP, channels)
    out_ref[...] = planes[...].reshape(out_ref.shape).astype(jnp.bfloat16)


def make_slab(traces, band_bins):
    channels, windows, length = traces.shape
    bins = band_bins.shape[0]
    fine = 128
    sample_idx = jnp.concatenate([jnp.arange(fine), jnp.arange(length // fine) * fine])
    phase_int = band_bins[:, None] * sample_idx[None, :].astype(jnp.int32) % length
    phases = phase_int.astype(jnp.float32) * (2.0 * math.pi / length)
    cos, sin = jnp.cos(phases), jnp.sin(phases)
    return pl.pallas_call(
        spectra_kernel,
        out_shape=jax.ShapeDtypeStruct((bins * windows * 2, channels), jnp.bfloat16),
        scratch_shapes=[
            pltpu.VMEM((2 * bins, length), jnp.bfloat16),
            pltpu.VMEM((bins // GROUP, GROUP * windows * 2, channels), jnp.float32),
        ],
        compiler_params=pltpu.CompilerParams(vmem_limit_bytes=48 << 20),
        name="spectra",
    )(traces, cos[:, :fine], sin[:, :fine], cos[:, fine:], sin[:, fine:])


def left_kernel(z, *refs, per_step):
    slabs, (out_ref, choice, mask) = refs[:-3], refs[-3:]
    m, k = mask.shape
    channels = slabs[0].shape[-1]
    group_rows = slabs[0].shape[0] // per_step
    half = group_rows // 2
    rows_out = m // (2 * GROUP)

    @pl.when(pl.program_id(0) == 0)
    def _():
        row = lax.broadcasted_iota(jnp.int32, (m, 2 * channels), 0)
        col = lax.broadcasted_iota(jnp.int32, (m, 2 * channels), 1)
        wanted = row // (2 * GROUP) + z[0] * rows_out + (row % 2) * channels
        choice[...] = jnp.where(col == wanted, 1.0, 0.0).astype(jnp.bfloat16)
        row = lax.broadcasted_iota(jnp.int32, (m, k), 0)
        col = lax.broadcasted_iota(jnp.int32, (m, k), 1)
        bin_of_col = col % half // (half // GROUP)
        mask[...] = jnp.where(bin_of_col == row // 2 % GROUP, 1.0, 0.0)

    for u in range(per_step):
        pieces = []
        for slab in slabs:
            real = slab[u * group_rows : u * group_rows + half, :]
            imag = slab[u * group_rows + half : (u + 1) * group_rows, :]
            pieces.append(jnp.concatenate([real, imag], 1))
            pieces.append(jnp.concatenate([imag, -real], 1))
        both = jnp.concatenate(pieces, 0)
        rows = lax.dot_general(
            choice[...], both, (((1,), (1,)), ((), ())), preferred_element_type=jnp.float32
        )
        out_ref[u] = (rows * mask[...]).astype(jnp.bfloat16)


def make_left(slabs, z, rows_out, bins):
    slab_rows, channels = slabs[0].shape
    groups = bins // GROUP
    m, k = rows_out * GROUP * 2, slab_rows // groups * 4
    per_step = 4
    step_rows = slab_rows // groups * per_step
    return pl.pallas_call(
        lambda *r: left_kernel(*r, per_step=per_step),
        grid_spec=pltpu.PrefetchScalarGridSpec(
            num_scalar_prefetch=1,
            grid=(groups // per_step,),
            in_specs=[pl.BlockSpec((step_rows, channels), lambda i, s: (i, 0))] * len(slabs),
            out_specs=pl.BlockSpec((per_step, m, k), lambda i, s: (i, 0, 0)),
            scratch_shapes=[
                pltpu.VMEM((m, 2 * channels), jnp.bfloat16),
                pltpu.VMEM((m, k), jnp.float32),
            ],
        ),
        out_shape=jax.ShapeDtypeStruct((groups, m, k), jnp.bfloat16),
        compiler_params=pltpu.CompilerParams(vmem_limit_bytes=32 << 20),
        name="left",
    )(z.reshape(1), *slabs)


CHUNKS = 4
GROUP_UNROLL = 8
ROW_UNROLL = 16


def pairs_kernel(slots, left_ref, lag_ref, *refs, arrays, norm, aliased):
    sources, refs = refs[: len(arrays)], refs[len(arrays) + aliased :]
    out_ref, partner, left, gram, stage, in_sems, left_sems, out_sems = refs
    groups, m, k = left.shape
    chosen, slabs, slab_rows, channels = partner.shape
    group_rows = k // slabs
    chunk_rows = slab_rows // CHUNKS
    per_chunk = groups // CHUNKS

    def fetch(source, s, r, chunk):
        rows = pl.ds(chunk * chunk_rows, chunk_rows)
        return pltpu.make_async_copy(source.at[rows], partner.at[s, r, rows], in_sems.at[chunk, s, r])

    def fetch_left(chunk):
        some = pl.ds(chunk * per_chunk, per_chunk)
        return pltpu.make_async_copy(left_ref.at[some], left.at[some], left_sems.at[chunk])

    fetch_left(0).start()
    for s in range(chosen):
        for r in range(slabs):
            place = slots[s * (slabs + 1) + 1 + r]
            for source, (first, count, holds) in zip(sources, arrays):
                if r in holds:

                    @pl.when((place >= first) & (place < first + count))
                    def _():
                        for chunk in range(CHUNKS):
                            fetch(source.at[place - first], s, r, chunk).start()

    for chunk in range(1, CHUNKS):
        fetch_left(chunk).start()

    for chunk in range(CHUNKS):
        fetch_left(chunk).wait()
        for s in range(chosen):
            for r in range(slabs):
                fetch(sources[0].at[0], s, r, chunk).wait()

        @pl.loop(0, per_chunk // GROUP_UNROLL)
        def _(i):
            for u in range(GROUP_UNROLL):
                g = chunk * per_chunk + i * GROUP_UNROLL + u
                rows = pl.ds(pl.multiple_of(g * group_rows, group_rows), group_rows)
                right = jnp.concatenate(
                    [partner[s, :, rows, :].reshape(k, channels) for s in range(chosen)], 1
                )
                product = jnp.dot(left[g], right, preferred_element_type=jnp.float32)
                cols = pl.ds(pl.multiple_of(g * 2 * GROUP, 2 * GROUP), 2 * GROUP)
                gram[:, cols, :] = product.astype(jnp.bfloat16).reshape(
                    m // (2 * GROUP), 2 * GROUP, chosen * channels
                )

    steps = gram.shape[0] // ROW_UNROLL

    class Write:
        def __init__(self, i, b):
            rows = pl.ds(i * ROW_UNROLL, ROW_UNROLL)
            self.copies = [
                pltpu.make_async_copy(
                    stage.at[b, s], out_ref.at[rows, slots[s * (slabs + 1)]], out_sems.at[b, s]
                )
                for s in range(chosen)
            ]

        def start(self):
            for copy in self.copies:
                copy.start()

        def wait(self):
            for copy in self.copies:
                copy.wait()

    @pl.loop(0, steps)
    def _(i):
        b = lax.rem(i, 2)

        @pl.when(i >= 2)
        def _():
            Write(i - 2, b).wait()

        for u in range(ROW_UNROLL):
            lagged = jnp.dot(
                lag_ref[...], gram[i * ROW_UNROLL + u], preferred_element_type=jnp.float32
            )
            for s in range(chosen):
                stage[b, s, u] = (lagged[:, s * channels : (s + 1) * channels] * norm).T
        Write(i, b).start()

    for i in range(steps - 2, steps):
        Write(i, i % 2).wait()


def correlate(slots, left, lag_rows, held, slot_count, norm, earlier=None):
    groups, m, k = left.shape
    rows_out = m // (2 * GROUP)
    arrays, first = [], 0
    for value, holds in held:
        arrays.append((first, value.shape[0], holds))
        first += value.shape[0]
    slab_rows, channels = held[0][0].shape[1:]
    chosen, slabs = slots.shape[0], slots.shape[1] - 1
    lag_count, entries = lag_rows.shape
    anywhere = pl.BlockSpec(memory_space=pl.ANY)
    in_vmem = pl.BlockSpec(memory_space=pltpu.VMEM)
    operands = [slots.reshape(-1), left, lag_rows] + [value for value, _ in held]
    aliases = {}
    if earlier is not None:
        aliases = {len(operands): 0}
        operands.append(earlier)
    flops = 2 * groups * m * k * chosen * channels + 2 * rows_out * lag_count * entries * chosen * channels
    return pl.pallas_call(
        lambda *r: pairs_kernel(*r, arrays=arrays, norm=norm, aliased=len(aliases)),
        in_specs=[pl.BlockSpec(memory_space=pltpu.SMEM), anywhere, in_vmem]
        + [anywhere] * (len(operands) - 3),
        out_specs=anywhere,
        scratch_shapes=[
            pltpu.VMEM((chosen, slabs, slab_rows, channels), jnp.bfloat16),
            pltpu.VMEM((groups, m, k), jnp.bfloat16),
            pltpu.VMEM((rows_out, entries, chosen * channels), jnp.bfloat16),
            pltpu.VMEM((2, chosen, ROW_UNROLL, channels, lag_count), jnp.float32),
            pltpu.SemaphoreType.DMA((CHUNKS, chosen, slabs)),
            pltpu.SemaphoreType.DMA((CHUNKS,)),
            pltpu.SemaphoreType.DMA((2, chosen)),
        ],
        out_shape=jax.ShapeDtypeStruct((rows_out, slot_count, channels, lag_count), jnp.float32),
        input_output_aliases=aliases,
        cost_estimate=pl.CostEstimate(flops=flops, bytes_accessed=12 << 20, transcendentals=0),
        compiler_params=pltpu.CompilerParams(vmem_limit_bytes=PAIRS_VMEM),
        name="pairs",
    )(*operands)


PAIRS_VMEM = 58 << 20

X_PAIRS = [(i, i ^ 2) for i in range(8)]
Y_PAIRS = [(4, 0), (1, 5), (6, 2), (3, 7)]
Y_ON = [(7, 3), (0, 4)]
Y_ON_ALL = Y_ON + [(6, 2), (1, 5)]
X_ON = [(0, 2), (7, 5)]
CORE_PAIRS = [(i, i ^ 1) for i in range(8)]


def moved(what, pairs):
    after = [[None] * 8 for _ in what]
    for src, dst in pairs:
        for old, new in zip(what, after):
            new[dst] = old[src]
    return after


class Held:
    def __init__(self, value, what):
        self.value, self.what = value, what

    def hop(self, pairs):
        return Held(lax.ppermute(self.value, "chan", pairs), moved(self.what, pairs))


def join(*parts):
    return Held(jnp.concatenate([p.value for p in parts], 0), [w for p in parts for w in p.what])


def together(*parts):
    return lax.optimization_barrier(parts)


jax.tree_util.register_pytree_node(
    Held,
    lambda held: ((held.value,), tuple(tuple(row) for row in held.what)),
    lambda what, children: Held(children[0], [list(row) for row in what]),
)


def on_device(traces, band_bins, pair_blocks):
    channels, windows, length = traces.shape
    bins = band_bins.shape[0]
    z = lax.axis_index("freq")
    me = lax.axis_index("chan")
    slot_count = pair_blocks.shape[1]

    lag_idx = jnp.arange(LAGS, dtype=jnp.int32) - LAGS // 2
    phases = (lag_idx[:, None] * band_bins[None, :] % length).astype(jnp.float32)
    phases = phases * (2.0 * math.pi / length)
    lag_rows = jnp.stack([jnp.cos(phases), -jnp.sin(phases)], 2).reshape(LAGS, 2 * bins)
    lag_rows = lag_rows.astype(jnp.bfloat16)

    def along_z(value, pairs):
        return lax.ppermute(value, "freq", pairs)

    def slab_of(value, r):
        return Held(lax.optimization_barrier(value), [[(i, r) for i in range(8)]])

    s0 = make_slab(traces, band_bins)[None]
    q0 = slab_of(s0, 0)
    y0 = q0.hop(Y_PAIRS)
    x0 = q0.hop(X_PAIRS)
    down1 = along_z(s0, [(3, 2), (2, 1), (1, 0)])
    up1 = along_z(s0, [(0, 1), (1, 2), (2, 3)])
    up1, down1, x0, lag_rows = together(up1, down1, x0, lag_rows)

    q1 = slab_of(lax.select_n(z, down1, up1, down1, up1), 1)
    up2 = along_z(up1, [(1, 2), (2, 3)])
    y1 = q1.hop(Y_PAIRS)
    c0 = x0.hop(Y_ON)
    d0 = y0.hop(X_ON)
    down2 = along_z(down1, [(2, 1), (1, 0)])
    x1 = q1.hop(X_PAIRS)
    first = join(q0, x0, y0, q1)
    first, down2, x1, y0, y1, up2 = together(first, down2, x1, y0, y1, up2)

    q2 = slab_of(lax.select_n(z, down2, down1, up1, up2), 2)
    y2 = q2.hop(Y_PAIRS)
    down3 = along_z(down2, [(1, 0)])
    up3 = along_z(up2, [(2, 3)])
    c1 = x1.hop(Y_ON_ALL)
    x2 = q2.hop(X_PAIRS)
    second = join(x1, y1)
    c0, d0, up3, down2, up2, down3, second = together(c0, d0, up3, down2, up2, down3, second)

    q3 = slab_of(lax.select_n(z, down3, down2, up2, up3), 3)
    b = [h.hop(CORE_PAIRS) for h in (first, second,)]
    y3 = q3.hop(Y_PAIRS)
    x3 = q3.hop(X_PAIRS)
    left = make_left([q.value[0] for q in (q0, q1, q2, q3)], z, channels // 4, bins)
    x2, y2, left = together(x2, y2, left)

    d2 = y2.hop(X_ON)
    c2 = x2.hop(Y_ON)
    b += [h.hop(CORE_PAIRS) for h in (d0, q3, q2, c0,)]


    ids = np.arange(8, dtype=np.int32)
    third = [x3.what, y2.what, y3.what, x2.what]
    held = [q0, q1, q2, q3, x0, x1, x2, x3, y0, y1, y2, y3, c0, d0, c1] + b
    whats = [h.what for h in held] + [moved(what, CORE_PAIRS) for what in third]
    c3, d3 = moved(x3.what, Y_ON), moved(y3.what, X_ON)
    whats += [c2.what, d2.what, c3, d3]
    whats += [moved(what, CORE_PAIRS) for what in (c2.what, c1.what, c3, d3, d2.what)]
    table = np.zeros((8, 8, 4), np.int32)
    all_holds = [set() for _ in whats]
    index = sum(len(what) for what in whats)
    for what, holds in zip(reversed(whats), reversed(all_holds)):
        for item in reversed(what):
            index -= 1
            for device, block_slab in enumerate(item):
                if block_slab is not None:
                    table[device, block_slab[0], block_slab[1]] = index
                    holds.add(block_slab[1])
    wanted = (ids[None, None, :, None] == pair_blocks[0][:, None, None, None]) & (
        ids[None, :, None, None] == me
    )
    slots = jnp.sum(jnp.where(wanted, table[None], 0), axis=(1, 2))
    slots = jnp.concatenate([jnp.arange(slot_count, dtype=jnp.int32)[:, None], slots], 1)
    swapped = slots[jnp.asarray([1, 0, 2])]
    slots = jnp.where(me == 5, swapped, slots)

    slots, y3, x3, c1 = together(slots, y3, x3, c1)

    c3, d3 = x3.hop(Y_ON), y3.hop(X_ON)
    b += [h.hop(CORE_PAIRS) for h in (x3, y2, y3, x2)]
    norm = 1.0 / math.sqrt(4 * windows * bins)
    held = [q0, q1, q2, q3, x0, x1, x2, x3, y0, y1, y2, y3, c0, d0, c1] + b
    places = [(h.value, holds) for h, holds in zip(held, all_holds)]
    result = correlate(slots[:1], left, lag_rows, places, slot_count, norm)
    result, d3, d2, c3, c2 = together(result, d3, d2, c3, c2)
    late = [h.hop(CORE_PAIRS) for h in (c2, c1, c3, d3, d2)]
    held += [c2, d2, c3, d3] + late
    places = [(h.value, holds) for h, holds in zip(held, all_holds)]
    return correlate(slots[1:], left, lag_rows, places, slot_count, norm, result)[None]


def solution(mesh):
    placed = (P("chan", "freq", None), P(), P("chan", None))
    fits = mesh.shape["chan"] == 8 and mesh.shape["freq"] == 4
    return jax.shard_map(
        on_device if fits else on_any_device,
        mesh=mesh,
        in_specs=placed,
        out_specs=P("chan", "freq", None, None, None),
        check_vma=False,
    )
```

```python
import math

import jax
import jax.numpy as jnp
import numpy as np
from jax import lax
from jax.experimental import pallas as pl
from jax.experimental.pallas import tpu as pltpu
from jax.sharding import PartitionSpec as P

LAGS = 128
REACH = 3
GROUP = 8


def shifted(value, axis, by):
    size = lax.axis_size(axis)
    pairs = [(i, i + by) for i in range(size) if 0 <= i + by < size]
    return lax.ppermute(value, axis, pairs)


def make_dft_table(band_bins, length):
    sample_idx = jnp.arange(length, dtype=jnp.int32)
    phase_int = band_bins[:, None] * sample_idx[None, :] % length
    phases = phase_int.astype(jnp.float32) * (2.0 * math.pi / length)
    return jnp.concatenate([jnp.cos(phases), -jnp.sin(phases)], 0).T.astype(jnp.bfloat16)


def make_lag_table(band_bins, length, lag_count):
    lag_idx = jnp.arange(lag_count, dtype=jnp.int32) - lag_count // 2
    phase_int = band_bins[:, None] * lag_idx[None, :] % length
    phases = phase_int.astype(jnp.float32) * (2.0 * math.pi / length)
    return jnp.concatenate([jnp.cos(phases), -jnp.sin(phases)], 0)


def gram_pair(first_block, second_block):
    rotated = jnp.stack([-second_block[:, :, 1], second_block[:, :, 0]], 2)
    gram_real = jnp.einsum(
        "awcf,bwcf->abf", first_block, second_block, preferred_element_type=jnp.float32
    )
    gram_imag = jnp.einsum(
        "awcf,bwcf->abf", first_block, rotated, preferred_element_type=jnp.float32
    )
    return jnp.stack([gram_real, gram_imag], 2)


def on_any_device(traces, band_bins, pair_blocks):
    channels, windows, length = traces.shape
    band_count = band_bins.shape[0]
    dft_matrix = make_dft_table(band_bins, length)
    spectra = jnp.dot(
        traces.reshape(channels * windows, length), dft_matrix, preferred_element_type=jnp.float32
    )
    amplitude = jnp.sqrt(jnp.sum(spectra * spectra, axis=1, keepdims=True) / band_count + 1e-06)
    whitened = (spectra / amplitude).astype(jnp.bfloat16).reshape(channels, windows, 2, band_count)
    own_block = lax.all_to_all(whitened, "freq", split_axis=3, concat_axis=1, tiled=True)
    below_blocks = [shifted(own_block, "chan", distance) for distance in range(1, REACH + 1)]
    above_blocks = [shifted(own_block, "chan", -distance) for distance in range(1, REACH + 1)]
    stacked = jnp.stack(below_blocks[::-1] + [own_block] + above_blocks, 0)
    my_index = lax.axis_index("chan")
    gram_list = []
    for pair_slot in range(pair_blocks.shape[1]):
        offset = pair_blocks[0, pair_slot] - my_index + REACH
        partner = lax.dynamic_index_in_dim(stacked, offset, 0, keepdims=False)
        gram_list.append(gram_pair(own_block, partner))
    cross_gram = jnp.stack(gram_list, 1)
    lag_matrix = make_lag_table(band_bins, length, LAGS)
    lag_norm = 1.0 / math.sqrt(own_block.shape[1] * band_count)
    gram_block = lax.all_to_all(cross_gram, "freq", split_axis=0, concat_axis=4, tiled=True)
    dims_shape = gram_block.shape
    lagged = (
        jnp.dot(
            gram_block.reshape(-1, 2 * band_count),
            lag_matrix,
            precision=lax.Precision.HIGHEST,
            preferred_element_type=jnp.float32,
        )
        * lag_norm
    )
    result = lagged.reshape(dims_shape[0], dims_shape[1], dims_shape[2], LAGS)
    return result[None]


def spectra_kernel(traces_ref, bins_ref, out_ref, table, planes):
    bins, fine = bins_ref.shape[0], 128
    groups, _, channels = planes.shape
    windows, length = traces_ref.shape[1:]
    series = windows * channels

    def angles(step):
        sample = lax.broadcasted_iota(jnp.int32, (bins, fine), 1) * step
        phase = lax.rem(bins_ref[...] * sample, length).astype(jnp.float32) * (2.0 * math.pi / length)
        return jnp.cos(phase), jnp.sin(phase)

    fine_cos, fine_sin = angles(1)
    step_cos, step_sin = angles(fine)
    for h in range(length // fine):
        sc, ss = step_cos[:, h : h + 1], step_sin[:, h : h + 1]
        cols = slice(h * fine, (h + 1) * fine)
        table[:bins, cols] = (sc * fine_cos - ss * fine_sin).astype(jnp.bfloat16)
        table[bins:, cols] = (-(ss * fine_cos + sc * fine_sin)).astype(jnp.bfloat16)
    was = lax.broadcasted_iota(jnp.int32, (series, series), 0)
    now = lax.broadcasted_iota(jnp.int32, (series, series), 1)
    turned = jnp.where(was == now % channels * windows + now // channels, 1.0, 0.0)
    turned = turned.astype(jnp.bfloat16)
    rows = traces_ref[...].reshape(series, length)
    spectra = lax.dot_general(
        table[...], rows, (((1,), (1,)), ((), ())), preferred_element_type=jnp.float32
    )
    power = jnp.sum(spectra * spectra, axis=0, keepdims=True)
    white = (spectra / jnp.sqrt(power / bins + 1e-06)).astype(jnp.bfloat16)
    white = jnp.dot(white, turned, preferred_element_type=jnp.float32)
    for w in range(windows):
        for c in range(2):
            first = c * GROUP * windows + w
            planes[:, pl.ds(first, GROUP, stride=windows), :] = white[
                c * bins : (c + 1) * bins, w * channels : (w + 1) * channels
            ].reshape(groups, GROUP, channels)
    out_ref[...] = planes[...].reshape(out_ref.shape).astype(jnp.bfloat16)


def make_slab(traces, band_bins):
    channels, windows, length = traces.shape
    bins = band_bins.shape[0]
    return pl.pallas_call(
        spectra_kernel,
        out_shape=jax.ShapeDtypeStruct((bins * windows * 2, channels), jnp.bfloat16),
        scratch_shapes=[
            pltpu.VMEM((2 * bins, length), jnp.bfloat16),
            pltpu.VMEM((bins // GROUP, GROUP * windows * 2, channels), jnp.float32),
        ],
        compiler_params=pltpu.CompilerParams(vmem_limit_bytes=48 << 20),
        name="spectra",
    )(traces, band_bins[:, None])


def left_kernel(z, *refs, per_step):
    slabs, (out_ref, choice, mask) = refs[:-3], refs[-3:]
    m, k = mask.shape
    channels = slabs[0].shape[-1]
    group_rows = slabs[0].shape[0] // per_step
    half = group_rows // 2
    rows_out = m // (2 * GROUP)

    @pl.when(pl.program_id(0) == 0)
    def _():
        row = lax.broadcasted_iota(jnp.int32, (m, 2 * channels), 0)
        col = lax.broadcasted_iota(jnp.int32, (m, 2 * channels), 1)
        wanted = row // (2 * GROUP) + z[0] * rows_out + (row % 2) * channels
        choice[...] = jnp.where(col == wanted, 1.0, 0.0).astype(jnp.bfloat16)
        row = lax.broadcasted_iota(jnp.int32, (m, k), 0)
        col = lax.broadcasted_iota(jnp.int32, (m, k), 1)
        bin_of_col = col % half // (half // GROUP)
        mask[...] = jnp.where(bin_of_col == row // 2 % GROUP, 1.0, 0.0)

    for u in range(per_step):
        pieces = []
        for slab in slabs:
            real = slab[u * group_rows : u * group_rows + half, :]
            imag = slab[u * group_rows + half : (u + 1) * group_rows, :]
            pieces.append(jnp.concatenate([real, imag], 1))
            pieces.append(jnp.concatenate([imag, -real], 1))
        both = jnp.concatenate(pieces, 0)
        rows = lax.dot_general(
            choice[...], both, (((1,), (1,)), ((), ())), preferred_element_type=jnp.float32
        )
        out_ref[u] = (rows * mask[...]).astype(jnp.bfloat16)


def make_left(slabs, z, rows_out, bins):
    slab_rows, channels = slabs[0].shape
    groups = bins // GROUP
    m, k = rows_out * GROUP * 2, slab_rows // groups * 4
    per_step = 4
    step_rows = slab_rows // groups * per_step
    return pl.pallas_call(
        lambda *r: left_kernel(*r, per_step=per_step),
        grid_spec=pltpu.PrefetchScalarGridSpec(
            num_scalar_prefetch=1,
            grid=(groups // per_step,),
            in_specs=[pl.BlockSpec((step_rows, channels), lambda i, s: (i, 0))] * len(slabs),
            out_specs=pl.BlockSpec((per_step, m, k), lambda i, s: (i, 0, 0)),
            scratch_shapes=[
                pltpu.VMEM((m, 2 * channels), jnp.bfloat16),
                pltpu.VMEM((m, k), jnp.float32),
            ],
        ),
        out_shape=jax.ShapeDtypeStruct((groups, m, k), jnp.bfloat16),
        compiler_params=pltpu.CompilerParams(vmem_limit_bytes=32 << 20),
        name="left",
    )(z.reshape(1), *slabs)


CHUNKS = 4
GROUP_UNROLL = 8
ROW_UNROLL = 16


def pairs_kernel(slots, left_ref, lag_ref, *refs, arrays, norm, aliased):
    sources, refs = refs[: len(arrays)], refs[len(arrays) + aliased :]
    out_ref, partner, left, gram, stage, in_sems, left_sems, out_sems = refs
    groups, m, k = left.shape
    chosen, slabs, slab_rows, channels = partner.shape
    group_rows = k // slabs
    chunk_rows = slab_rows // CHUNKS
    per_chunk = groups // CHUNKS

    def fetch(source, s, r, chunk):
        rows = pl.ds(chunk * chunk_rows, chunk_rows)
        return pltpu.make_async_copy(source.at[rows], partner.at[s, r, rows], in_sems.at[chunk, s, r])

    def fetch_left(chunk):
        some = pl.ds(chunk * per_chunk, per_chunk)
        return pltpu.make_async_copy(left_ref.at[some], left.at[some], left_sems.at[chunk])

    fetch_left(0).start()
    for s in range(chosen):
        for r in range(slabs):
            place = slots[s * (slabs + 1) + 1 + r]
            for source, (first, count, holds) in zip(sources, arrays):
                if r in holds:

                    @pl.when((place >= first) & (place < first + count))
                    def _():
                        for chunk in range(CHUNKS):
                            fetch(source.at[place - first], s, r, chunk).start()

    for chunk in range(1, CHUNKS):
        fetch_left(chunk).start()

    for chunk in range(CHUNKS):
        fetch_left(chunk).wait()
        for s in range(chosen):
            for r in range(slabs):
                fetch(sources[0].at[0], s, r, chunk).wait()

        @pl.loop(0, per_chunk // GROUP_UNROLL)
        def _(i):
            for u in range(GROUP_UNROLL):
                g = chunk * per_chunk + i * GROUP_UNROLL + u
                rows = pl.ds(pl.multiple_of(g * group_rows, group_rows), group_rows)
                right = jnp.concatenate(
                    [partner[s, :, rows, :].reshape(k, channels) for s in range(chosen)], 1
                )
                product = jnp.dot(left[g], right, preferred_element_type=jnp.float32)
                cols = pl.ds(pl.multiple_of(g * 2 * GROUP, 2 * GROUP), 2 * GROUP)
                gram[:, cols, :] = product.astype(jnp.bfloat16).reshape(
                    m // (2 * GROUP), 2 * GROUP, chosen * channels
                )

    steps = gram.shape[0] // ROW_UNROLL

    class Write:
        def __init__(self, i, b):
            rows = pl.ds(i * ROW_UNROLL, ROW_UNROLL)
            self.copies = [
                pltpu.make_async_copy(
                    stage.at[b, s], out_ref.at[rows, slots[s * (slabs + 1)]], out_sems.at[b, s]
                )
                for s in range(chosen)
            ]

        def start(self):
            for copy in self.copies:
                copy.start()

        def wait(self):
            for copy in self.copies:
                copy.wait()

    @pl.loop(0, steps)
    def _(i):
        b = lax.rem(i, 2)

        @pl.when(i >= 2)
        def _():
            Write(i - 2, b).wait()

        for u in range(ROW_UNROLL):
            lagged = jnp.dot(
                lag_ref[...], gram[i * ROW_UNROLL + u], preferred_element_type=jnp.float32
            )
            for s in range(chosen):
                stage[b, s, u] = (lagged[:, s * channels : (s + 1) * channels] * norm).T
        Write(i, b).start()

    for i in range(steps - 2, steps):
        Write(i, i % 2).wait()


def correlate(slots, left, lag_rows, held, slot_count, norm, earlier=None):
    groups, m, k = left.shape
    rows_out = m // (2 * GROUP)
    arrays, first = [], 0
    for value, holds in held:
        arrays.append((first, value.shape[0], holds))
        first += value.shape[0]
    slab_rows, channels = held[0][0].shape[1:]
    chosen, slabs = slots.shape[0], slots.shape[1] - 1
    lag_count, entries = lag_rows.shape
    anywhere = pl.BlockSpec(memory_space=pl.ANY)
    in_vmem = pl.BlockSpec(memory_space=pltpu.VMEM)
    operands = [slots.reshape(-1), left, lag_rows] + [value for value, _ in held]
    aliases = {}
    if earlier is not None:
        aliases = {len(operands): 0}
        operands.append(earlier)
    flops = 2 * groups * m * k * chosen * channels + 2 * rows_out * lag_count * entries * chosen * channels
    return pl.pallas_call(
        lambda *r: pairs_kernel(*r, arrays=arrays, norm=norm, aliased=len(aliases)),
        in_specs=[pl.BlockSpec(memory_space=pltpu.SMEM), anywhere, in_vmem]
        + [anywhere] * (len(operands) - 3),
        out_specs=anywhere,
        scratch_shapes=[
            pltpu.VMEM((chosen, slabs, slab_rows, channels), jnp.bfloat16),
            pltpu.VMEM((groups, m, k), jnp.bfloat16),
            pltpu.VMEM((rows_out, entries, chosen * channels), jnp.bfloat16),
            pltpu.VMEM((2, chosen, ROW_UNROLL, channels, lag_count), jnp.float32),
            pltpu.SemaphoreType.DMA((CHUNKS, chosen, slabs)),
            pltpu.SemaphoreType.DMA((CHUNKS,)),
            pltpu.SemaphoreType.DMA((2, chosen)),
        ],
        out_shape=jax.ShapeDtypeStruct((rows_out, slot_count, channels, lag_count), jnp.float32),
        input_output_aliases=aliases,
        cost_estimate=pl.CostEstimate(flops=flops, bytes_accessed=12 << 20, transcendentals=0),
        compiler_params=pltpu.CompilerParams(vmem_limit_bytes=PAIRS_VMEM),
        name="pairs",
    )(*operands)


PAIRS_VMEM = 58 << 20

X_PAIRS = [(i, i ^ 2) for i in range(8)]
Y_PAIRS = [(4, 0), (1, 5), (6, 2), (3, 7)]
Y_ON = [(7, 3), (0, 4)]
Y_ON_ALL = Y_ON + [(6, 2), (1, 5)]
X_ON = [(0, 2), (7, 5)]
CORE_PAIRS = [(i, i ^ 1) for i in range(8)]


def moved(what, pairs):
    after = [[None] * 8 for _ in what]
    for src, dst in pairs:
        for old, new in zip(what, after):
            new[dst] = old[src]
    return after


class Held:
    def __init__(self, value, what):
        self.value, self.what = value, what

    def hop(self, pairs):
        return Held(lax.ppermute(self.value, "chan", pairs), moved(self.what, pairs))


def join(*parts):
    return Held(jnp.concatenate([p.value for p in parts], 0), [w for p in parts for w in p.what])


def together(*parts):
    return lax.optimization_barrier(parts)


jax.tree_util.register_pytree_node(
    Held,
    lambda held: ((held.value,), tuple(tuple(row) for row in held.what)),
    lambda what, children: Held(children[0], [list(row) for row in what]),
)


def on_device(traces, band_bins, pair_blocks):
    channels, windows, length = traces.shape
    bins = band_bins.shape[0]
    z = lax.axis_index("freq")
    me = lax.axis_index("chan")
    slot_count = pair_blocks.shape[1]

    lag_idx = jnp.arange(LAGS, dtype=jnp.int32) - LAGS // 2
    phases = (lag_idx[:, None] * band_bins[None, :] % length).astype(jnp.float32)
    phases = phases * (2.0 * math.pi / length)
    lag_rows = jnp.stack([jnp.cos(phases), -jnp.sin(phases)], 2).reshape(LAGS, 2 * bins)
    lag_rows = lag_rows.astype(jnp.bfloat16)

    def along_z(value, pairs):
        return lax.ppermute(value, "freq", pairs)

    def slab_of(value, r):
        return Held(lax.optimization_barrier(value), [[(i, r) for i in range(8)]])

    s0 = make_slab(traces, band_bins)[None]
    q0 = slab_of(s0, 0)
    y0 = q0.hop(Y_PAIRS)
    x0 = q0.hop(X_PAIRS)
    down1 = along_z(s0, [(3, 2), (2, 1), (1, 0)])
    up1 = along_z(s0, [(0, 1), (1, 2), (2, 3)])
    up1, down1, x0, lag_rows = together(up1, down1, x0, lag_rows)

    q1 = slab_of(lax.select_n(z, down1, up1, down1, up1), 1)
    up2 = along_z(up1, [(1, 2), (2, 3)])
    y1 = q1.hop(Y_PAIRS)
    c0 = x0.hop(Y_ON)
    d0 = y0.hop(X_ON)
    down2 = along_z(down1, [(2, 1), (1, 0)])
    x1 = q1.hop(X_PAIRS)
    first = join(q0, x0, y0, q1)
    first, down2, x1, y0, y1, up2 = together(first, down2, x1, y0, y1, up2)

    q2 = slab_of(lax.select_n(z, down2, down1, up1, up2), 2)
    y2 = q2.hop(Y_PAIRS)
    down3 = along_z(down2, [(1, 0)])
    up3 = along_z(up2, [(2, 3)])
    c1 = x1.hop(Y_ON_ALL)
    x2 = q2.hop(X_PAIRS)
    second = join(x1, y1)
    c0, d0, up3, down2, up2, down3, second = together(c0, d0, up3, down2, up2, down3, second)

    q3 = slab_of(lax.select_n(z, down3, down2, up2, up3), 3)
    b = [h.hop(CORE_PAIRS) for h in (first, second,)]
    y3 = q3.hop(Y_PAIRS)
    x3 = q3.hop(X_PAIRS)
    left = make_left([q.value[0] for q in (q0, q1, q2, q3)], z, channels // 4, bins)
    x2, y2, left = together(x2, y2, left)

    d2 = y2.hop(X_ON)
    c2 = x2.hop(Y_ON)
    b += [h.hop(CORE_PAIRS) for h in (d0, q3, q2, c0, x2, y2)]


    ids = np.arange(8, dtype=np.int32)
    third = [x3.what, y3.what]
    held = [q0, q1, q2, q3, x0, x1, x2, x3, y0, y1, y2, y3, c0, d0, c1] + b
    whats = [h.what for h in held] + [moved(what, CORE_PAIRS) for what in third]
    c3, d3 = moved(x3.what, Y_ON), moved(y3.what, X_ON)
    whats += [c2.what, d2.what, c3, d3]
    whats += [moved(what, CORE_PAIRS) for what in (c2.what, c1.what, c3, d3, d2.what)]
    table = np.zeros((8, 8, 4), np.int32)
    all_holds = [set() for _ in whats]
    index = sum(len(what) for what in whats)
    for what, holds in zip(reversed(whats), reversed(all_holds)):
        for item in reversed(what):
            index -= 1
            for device, block_slab in enumerate(item):
                if block_slab is not None:
                    table[device, block_slab[0], block_slab[1]] = index
                    holds.add(block_slab[1])
    wanted = (ids[None, None, :, None] == pair_blocks[0][:, None, None, None]) & (
        ids[None, :, None, None] == me
    )
    slots = jnp.sum(jnp.where(wanted, table[None], 0), axis=(1, 2))
    slots = jnp.concatenate([jnp.arange(slot_count, dtype=jnp.int32)[:, None], slots], 1)
    swapped = slots[jnp.asarray([1, 0, 2])]
    slots = jnp.where(me == 5, swapped, slots)

    slots, y3, x3, c1 = together(slots, y3, x3, c1)

    c3, d3 = x3.hop(Y_ON), y3.hop(X_ON)
    b += [h.hop(CORE_PAIRS) for h in (x3, y3)]
    norm = 1.0 / math.sqrt(4 * windows * bins)
    held = [q0, q1, q2, q3, x0, x1, x2, x3, y0, y1, y2, y3, c0, d0, c1] + b
    places = [(h.value, holds) for h, holds in zip(held, all_holds)]
    result = correlate(slots[:1], left, lag_rows, places, slot_count, norm)
    result, d3, d2, c3, c2 = together(result, d3, d2, c3, c2)
    late = [h.hop(CORE_PAIRS) for h in (c2, c1, c3, d3, d2)]
    held += [c2, d2, c3, d3] + late
    places = [(h.value, holds) for h, holds in zip(held, all_holds)]
    return correlate(slots[1:], left, lag_rows, places, slot_count, norm, result)[None]


def solution(mesh):
    placed = (P("chan", "freq", None), P(), P("chan", None))
    fits = mesh.shape["chan"] == 8 and mesh.shape["freq"] == 4
    return jax.shard_map(
        on_device if fits else on_any_device,
        mesh=mesh,
        in_specs=placed,
        out_specs=P("chan", "freq", None, None, None),
        check_vma=False,
    )
```

```python
import math

import jax
import jax.numpy as jnp
import numpy as np
from jax import lax
from jax.experimental import pallas as pl
from jax.experimental.pallas import tpu as pltpu
from jax.sharding import PartitionSpec as P

LAGS = 128
REACH = 3
GROUP = 8


def shifted(value, axis, by):
    size = lax.axis_size(axis)
    pairs = [(i, i + by) for i in range(size) if 0 <= i + by < size]
    return lax.ppermute(value, axis, pairs)


def make_dft_table(band_bins, length):
    sample_idx = jnp.arange(length, dtype=jnp.int32)
    phase_int = band_bins[:, None] * sample_idx[None, :] % length
    phases = phase_int.astype(jnp.float32) * (2.0 * math.pi / length)
    return jnp.concatenate([jnp.cos(phases), -jnp.sin(phases)], 0).T.astype(jnp.bfloat16)


def make_lag_table(band_bins, length, lag_count):
    lag_idx = jnp.arange(lag_count, dtype=jnp.int32) - lag_count // 2
    phase_int = band_bins[:, None] * lag_idx[None, :] % length
    phases = phase_int.astype(jnp.float32) * (2.0 * math.pi / length)
    return jnp.concatenate([jnp.cos(phases), -jnp.sin(phases)], 0)


def gram_pair(first_block, second_block):
    rotated = jnp.stack([-second_block[:, :, 1], second_block[:, :, 0]], 2)
    gram_real = jnp.einsum(
        "awcf,bwcf->abf", first_block, second_block, preferred_element_type=jnp.float32
    )
    gram_imag = jnp.einsum(
        "awcf,bwcf->abf", first_block, rotated, preferred_element_type=jnp.float32
    )
    return jnp.stack([gram_real, gram_imag], 2)


def on_any_device(traces, band_bins, pair_blocks):
    channels, windows, length = traces.shape
    band_count = band_bins.shape[0]
    dft_matrix = make_dft_table(band_bins, length)
    spectra = jnp.dot(
        traces.reshape(channels * windows, length), dft_matrix, preferred_element_type=jnp.float32
    )
    amplitude = jnp.sqrt(jnp.sum(spectra * spectra, axis=1, keepdims=True) / band_count + 1e-06)
    whitened = (spectra / amplitude).astype(jnp.bfloat16).reshape(channels, windows, 2, band_count)
    own_block = lax.all_to_all(whitened, "freq", split_axis=3, concat_axis=1, tiled=True)
    below_blocks = [shifted(own_block, "chan", distance) for distance in range(1, REACH + 1)]
    above_blocks = [shifted(own_block, "chan", -distance) for distance in range(1, REACH + 1)]
    stacked = jnp.stack(below_blocks[::-1] + [own_block] + above_blocks, 0)
    my_index = lax.axis_index("chan")
    gram_list = []
    for pair_slot in range(pair_blocks.shape[1]):
        offset = pair_blocks[0, pair_slot] - my_index + REACH
        partner = lax.dynamic_index_in_dim(stacked, offset, 0, keepdims=False)
        gram_list.append(gram_pair(own_block, partner))
    cross_gram = jnp.stack(gram_list, 1)
    lag_matrix = make_lag_table(band_bins, length, LAGS)
    lag_norm = 1.0 / math.sqrt(own_block.shape[1] * band_count)
    gram_block = lax.all_to_all(cross_gram, "freq", split_axis=0, concat_axis=4, tiled=True)
    dims_shape = gram_block.shape
    lagged = (
        jnp.dot(
            gram_block.reshape(-1, 2 * band_count),
            lag_matrix,
            precision=lax.Precision.HIGHEST,
            preferred_element_type=jnp.float32,
        )
        * lag_norm
    )
    result = lagged.reshape(dims_shape[0], dims_shape[1], dims_shape[2], LAGS)
    return result[None]


def spectra_kernel(traces_ref, bins_ref, out_ref, table, planes):
    bins, fine = bins_ref.shape[0], 128
    groups, _, channels = planes.shape
    windows, length = traces_ref.shape[1:]
    series = windows * channels

    def angles(step):
        sample = lax.broadcasted_iota(jnp.int32, (bins, fine), 1) * step
        phase = lax.rem(bins_ref[...] * sample, length).astype(jnp.float32) * (2.0 * math.pi / length)
        return jnp.cos(phase), jnp.sin(phase)

    fine_cos, fine_sin = angles(1)
    step_cos, step_sin = angles(fine)
    for h in range(length // fine):
        sc, ss = step_cos[:, h : h + 1], step_sin[:, h : h + 1]
        cols = slice(h * fine, (h + 1) * fine)
        table[:bins, cols] = (sc * fine_cos - ss * fine_sin).astype(jnp.bfloat16)
        table[bins:, cols] = (-(ss * fine_cos + sc * fine_sin)).astype(jnp.bfloat16)
    was = lax.broadcasted_iota(jnp.int32, (series, series), 0)
    now = lax.broadcasted_iota(jnp.int32, (series, series), 1)
    turned = jnp.where(was == now % channels * windows + now // channels, 1.0, 0.0)
    turned = turned.astype(jnp.bfloat16)
    rows = traces_ref[...].reshape(series, length)
    spectra = lax.dot_general(
        table[...], rows, (((1,), (1,)), ((), ())), preferred_element_type=jnp.float32
    )
    power = jnp.sum(spectra * spectra, axis=0, keepdims=True)
    white = (spectra / jnp.sqrt(power / bins + 1e-06)).astype(jnp.bfloat16)
    white = jnp.dot(white, turned, preferred_element_type=jnp.float32)
    for w in range(windows):
        for c in range(2):
            first = c * GROUP * windows + w
            planes[:, pl.ds(first, GROUP, stride=windows), :] = white[
                c * bins : (c + 1) * bins, w * channels : (w + 1) * channels
            ].reshape(groups, GROUP, channels)
    out_ref[...] = planes[...].reshape(out_ref.shape).astype(jnp.bfloat16)


def make_slab(traces, band_bins):
    channels, windows, length = traces.shape
    bins = band_bins.shape[0]
    return pl.pallas_call(
        spectra_kernel,
        out_shape=jax.ShapeDtypeStruct((bins * windows * 2, channels), jnp.bfloat16),
        scratch_shapes=[
            pltpu.VMEM((2 * bins, length), jnp.bfloat16),
            pltpu.VMEM((bins // GROUP, GROUP * windows * 2, channels), jnp.float32),
        ],
        compiler_params=pltpu.CompilerParams(vmem_limit_bytes=48 << 20),
        name="spectra",
    )(traces, band_bins[:, None])


def left_kernel(z, *refs, per_step):
    slabs, (out_ref, choice, mask) = refs[:-3], refs[-3:]
    m, k = mask.shape
    channels = slabs[0].shape[-1]
    group_rows = slabs[0].shape[0] // per_step
    half = group_rows // 2
    rows_out = m // (2 * GROUP)

    @pl.when(pl.program_id(0) == 0)
    def _():
        row = lax.broadcasted_iota(jnp.int32, (m, 2 * channels), 0)
        col = lax.broadcasted_iota(jnp.int32, (m, 2 * channels), 1)
        wanted = row // (2 * GROUP) + z[0] * rows_out + (row % 2) * channels
        choice[...] = jnp.where(col == wanted, 1.0, 0.0).astype(jnp.bfloat16)
        row = lax.broadcasted_iota(jnp.int32, (m, k), 0)
        col = lax.broadcasted_iota(jnp.int32, (m, k), 1)
        bin_of_col = col % half // (half // GROUP)
        mask[...] = jnp.where(bin_of_col == row // 2 % GROUP, 1.0, 0.0)

    for u in range(per_step):
        pieces = []
        for slab in slabs:
            real = slab[u * group_rows : u * group_rows + half, :]
            imag = slab[u * group_rows + half : (u + 1) * group_rows, :]
            pieces.append(jnp.concatenate([real, imag], 1))
            pieces.append(jnp.concatenate([imag, -real], 1))
        both = jnp.concatenate(pieces, 0)
        rows = lax.dot_general(
            choice[...], both, (((1,), (1,)), ((), ())), preferred_element_type=jnp.float32
        )
        out_ref[u] = (rows * mask[...]).astype(jnp.bfloat16)


def make_left(slabs, z, rows_out, bins):
    slab_rows, channels = slabs[0].shape
    groups = bins // GROUP
    m, k = rows_out * GROUP * 2, slab_rows // groups * 4
    per_step = 4
    step_rows = slab_rows // groups * per_step
    return pl.pallas_call(
        lambda *r: left_kernel(*r, per_step=per_step),
        grid_spec=pltpu.PrefetchScalarGridSpec(
            num_scalar_prefetch=1,
            grid=(groups // per_step,),
            in_specs=[pl.BlockSpec((step_rows, channels), lambda i, s: (i, 0))] * len(slabs),
            out_specs=pl.BlockSpec((per_step, m, k), lambda i, s: (i, 0, 0)),
            scratch_shapes=[
                pltpu.VMEM((m, 2 * channels), jnp.bfloat16),
                pltpu.VMEM((m, k), jnp.float32),
            ],
        ),
        out_shape=jax.ShapeDtypeStruct((groups, m, k), jnp.bfloat16),
        compiler_params=pltpu.CompilerParams(vmem_limit_bytes=32 << 20),
        name="left",
    )(z.reshape(1), *slabs)


CHUNKS = 2
GROUP_UNROLL = 16
ROW_UNROLL = 16


def pairs_kernel(slots, left_ref, lag_ref, *refs, arrays, norm, aliased):
    sources, refs = refs[: len(arrays)], refs[len(arrays) + aliased :]
    out_ref, partner, left, gram, stage, in_sems, left_sems, out_sems = refs
    groups, m, k = left.shape
    chosen, slabs, slab_rows, channels = partner.shape
    group_rows = k // slabs
    chunk_rows = slab_rows // CHUNKS
    per_chunk = groups // CHUNKS

    def fetch(source, s, r, chunk):
        rows = pl.ds(chunk * chunk_rows, chunk_rows)
        return pltpu.make_async_copy(source.at[rows], partner.at[s, r, rows], in_sems.at[chunk, s, r])

    def fetch_left(chunk):
        some = pl.ds(chunk * per_chunk, per_chunk)
        return pltpu.make_async_copy(left_ref.at[some], left.at[some], left_sems.at[chunk])

    fetch_left(0).start()
    for s in range(chosen):
        for r in range(slabs):
            place = slots[s * (slabs + 1) + 1 + r]
            for source, (first, count, holds) in zip(sources, arrays):
                if r in holds:

                    @pl.when((place >= first) & (place < first + count))
                    def _():
                        for chunk in range(CHUNKS):
                            fetch(source.at[place - first], s, r, chunk).start()

    for chunk in range(1, CHUNKS):
        fetch_left(chunk).start()

    for chunk in range(CHUNKS):
        fetch_left(chunk).wait()
        for s in range(chosen):
            for r in range(slabs):
                fetch(sources[0].at[0], s, r, chunk).wait()

        @pl.loop(0, per_chunk // GROUP_UNROLL)
        def _(i):
            for u in range(GROUP_UNROLL):
                g = chunk * per_chunk + i * GROUP_UNROLL + u
                rows = pl.ds(pl.multiple_of(g * group_rows, group_rows), group_rows)
                right = jnp.concatenate(
                    [partner[s, :, rows, :].reshape(k, channels) for s in range(chosen)], 1
                )
                product = jnp.dot(left[g], right, preferred_element_type=jnp.float32)
                cols = pl.ds(pl.multiple_of(g * 2 * GROUP, 2 * GROUP), 2 * GROUP)
                gram[:, cols, :] = product.astype(jnp.bfloat16).reshape(
                    m // (2 * GROUP), 2 * GROUP, chosen * channels
                )

    steps = gram.shape[0] // ROW_UNROLL

    class Write:
        def __init__(self, i, b):
            rows = pl.ds(i * ROW_UNROLL, ROW_UNROLL)
            self.copies = [
                pltpu.make_async_copy(
                    stage.at[b, s], out_ref.at[rows, slots[s * (slabs + 1)]], out_sems.at[b, s]
                )
                for s in range(chosen)
            ]

        def start(self):
            for copy in self.copies:
                copy.start()

        def wait(self):
            for copy in self.copies:
                copy.wait()

    @pl.loop(0, steps)
    def _(i):
        b = lax.rem(i, 2)

        @pl.when(i >= 2)
        def _():
            Write(i - 2, b).wait()

        for u in range(ROW_UNROLL):
            lagged = jnp.dot(
                lag_ref[...], gram[i * ROW_UNROLL + u], preferred_element_type=jnp.float32
            )
            for s in range(chosen):
                stage[b, s, u] = (lagged[:, s * channels : (s + 1) * channels] * norm).T
        Write(i, b).start()

    for i in range(steps - 2, steps):
        Write(i, i % 2).wait()


def correlate(slots, left, lag_rows, held, slot_count, norm, earlier=None):
    groups, m, k = left.shape
    rows_out = m // (2 * GROUP)
    arrays, first = [], 0
    for value, holds in held:
        arrays.append((first, value.shape[0], holds))
        first += value.shape[0]
    slab_rows, channels = held[0][0].shape[1:]
    chosen, slabs = slots.shape[0], slots.shape[1] - 1
    lag_count, entries = lag_rows.shape
    anywhere = pl.BlockSpec(memory_space=pl.ANY)
    in_vmem = pl.BlockSpec(memory_space=pltpu.VMEM)
    operands = [slots.reshape(-1), left, lag_rows] + [value for value, _ in held]
    aliases = {}
    if earlier is not None:
        aliases = {len(operands): 0}
        operands.append(earlier)
    flops = 2 * groups * m * k * chosen * channels + 2 * rows_out * lag_count * entries * chosen * channels
    return pl.pallas_call(
        lambda *r: pairs_kernel(*r, arrays=arrays, norm=norm, aliased=len(aliases)),
        in_specs=[pl.BlockSpec(memory_space=pltpu.SMEM), anywhere, in_vmem]
        + [anywhere] * (len(operands) - 3),
        out_specs=anywhere,
        scratch_shapes=[
            pltpu.VMEM((chosen, slabs, slab_rows, channels), jnp.bfloat16),
            pltpu.VMEM((groups, m, k), jnp.bfloat16),
            pltpu.VMEM((rows_out, entries, chosen * channels), jnp.bfloat16),
            pltpu.VMEM((2, chosen, ROW_UNROLL, channels, lag_count), jnp.float32),
            pltpu.SemaphoreType.DMA((CHUNKS, chosen, slabs)),
            pltpu.SemaphoreType.DMA((CHUNKS,)),
            pltpu.SemaphoreType.DMA((2, chosen)),
        ],
        out_shape=jax.ShapeDtypeStruct((rows_out, slot_count, channels, lag_count), jnp.float32),
        input_output_aliases=aliases,
        cost_estimate=pl.CostEstimate(flops=flops, bytes_accessed=12 << 20, transcendentals=0),
        compiler_params=pltpu.CompilerParams(vmem_limit_bytes=PAIRS_VMEM),
        name="pairs",
    )(*operands)


PAIRS_VMEM = 58 << 20

X_PAIRS = [(i, i ^ 2) for i in range(8)]
Y_PAIRS = [(4, 0), (1, 5), (6, 2), (3, 7)]
Y_ON = [(7, 3), (0, 4)]
Y_ON_ALL = Y_ON + [(6, 2), (1, 5)]
X_ON = [(0, 2), (7, 5)]
CORE_PAIRS = [(i, i ^ 1) for i in range(8)]


def moved(what, pairs):
    after = [[None] * 8 for _ in what]
    for src, dst in pairs:
        for old, new in zip(what, after):
            new[dst] = old[src]
    return after


class Held:
    def __init__(self, value, what):
        self.value, self.what = value, what

    def hop(self, pairs):
        return Held(lax.ppermute(self.value, "chan", pairs), moved(self.what, pairs))


def join(*parts):
    return Held(jnp.concatenate([p.value for p in parts], 0), [w for p in parts for w in p.what])


def together(*parts):
    return lax.optimization_barrier(parts)


jax.tree_util.register_pytree_node(
    Held,
    lambda held: ((held.value,), tuple(tuple(row) for row in held.what)),
    lambda what, children: Held(children[0], [list(row) for row in what]),
)


def on_device(traces, band_bins, pair_blocks):
    channels, windows, length = traces.shape
    bins = band_bins.shape[0]
    z = lax.axis_index("freq")
    me = lax.axis_index("chan")
    slot_count = pair_blocks.shape[1]

    lag_idx = jnp.arange(LAGS, dtype=jnp.int32) - LAGS // 2
    phases = (lag_idx[:, None] * band_bins[None, :] % length).astype(jnp.float32)
    phases = phases * (2.0 * math.pi / length)
    lag_rows = jnp.stack([jnp.cos(phases), -jnp.sin(phases)], 2).reshape(LAGS, 2 * bins)
    lag_rows = lag_rows.astype(jnp.bfloat16)

    def along_z(value, pairs):
        return lax.ppermute(value, "freq", pairs)

    def slab_of(value, r):
        return Held(lax.optimization_barrier(value), [[(i, r) for i in range(8)]])

    s0 = make_slab(traces, band_bins)[None]
    q0 = slab_of(s0, 0)
    y0 = q0.hop(Y_PAIRS)
    x0 = q0.hop(X_PAIRS)
    down1 = along_z(s0, [(3, 2), (2, 1), (1, 0)])
    up1 = along_z(s0, [(0, 1), (1, 2), (2, 3)])
    up1, down1, x0, lag_rows = together(up1, down1, x0, lag_rows)

    q1 = slab_of(lax.select_n(z, down1, up1, down1, up1), 1)
    up2 = along_z(up1, [(1, 2), (2, 3)])
    y1 = q1.hop(Y_PAIRS)
    c0 = x0.hop(Y_ON)
    d0 = y0.hop(X_ON)
    down2 = along_z(down1, [(2, 1), (1, 0)])
    x1 = q1.hop(X_PAIRS)
    first = join(q0, x0, y0, q1)
    first, down2, x1, y0, y1, up2 = together(first, down2, x1, y0, y1, up2)

    q2 = slab_of(lax.select_n(z, down2, down1, up1, up2), 2)
    y2 = q2.hop(Y_PAIRS)
    down3 = along_z(down2, [(1, 0)])
    up3 = along_z(up2, [(2, 3)])
    c1 = x1.hop(Y_ON_ALL)
    x2 = q2.hop(X_PAIRS)
    second = join(x1, y1)
    c0, d0, up3, down2, up2, down3, second = together(c0, d0, up3, down2, up2, down3, second)

    q3 = slab_of(lax.select_n(z, down3, down2, up2, up3), 3)
    b = [h.hop(CORE_PAIRS) for h in (first, second,)]
    y3 = q3.hop(Y_PAIRS)
    x3 = q3.hop(X_PAIRS)
    left = make_left([q.value[0] for q in (q0, q1, q2, q3)], z, channels // 4, bins)
    x2, y2, left = together(x2, y2, left)

    d2 = y2.hop(X_ON)
    c2 = x2.hop(Y_ON)
    b += [h.hop(CORE_PAIRS) for h in (d0, q3, q2, c0, x2, y2)]


    ids = np.arange(8, dtype=np.int32)
    third = [x3.what, y3.what]
    held = [q0, q1, q2, q3, x0, x1, x2, x3, y0, y1, y2, y3, c0, d0, c1] + b
    whats = [h.what for h in held] + [moved(what, CORE_PAIRS) for what in third]
    c3, d3 = moved(x3.what, Y_ON), moved(y3.what, X_ON)
    whats += [c2.what, d2.what, c3, d3]
    whats += [moved(what, CORE_PAIRS) for what in (c2.what, c1.what, c3, d3, d2.what)]
    table = np.zeros((8, 8, 4), np.int32)
    all_holds = [set() for _ in whats]
    index = sum(len(what) for what in whats)
    for what, holds in zip(reversed(whats), reversed(all_holds)):
        for item in reversed(what):
            index -= 1
            for device, block_slab in enumerate(item):
                if block_slab is not None:
                    table[device, block_slab[0], block_slab[1]] = index
                    holds.add(block_slab[1])
    wanted = (ids[None, None, :, None] == pair_blocks[0][:, None, None, None]) & (
        ids[None, :, None, None] == me
    )
    slots = jnp.sum(jnp.where(wanted, table[None], 0), axis=(1, 2))
    slots = jnp.concatenate([jnp.arange(slot_count, dtype=jnp.int32)[:, None], slots], 1)
    swapped = slots[jnp.asarray([1, 0, 2])]
    slots = jnp.where(me == 5, swapped, slots)

    slots, y3, x3, c1 = together(slots, y3, x3, c1)

    c3, d3 = x3.hop(Y_ON), y3.hop(X_ON)
    b += [h.hop(CORE_PAIRS) for h in (x3, y3)]
    norm = 1.0 / math.sqrt(4 * windows * bins)
    held = [q0, q1, q2, q3, x0, x1, x2, x3, y0, y1, y2, y3, c0, d0, c1] + b
    places = [(h.value, holds) for h, holds in zip(held, all_holds)]
    result = correlate(slots[:1], left, lag_rows, places, slot_count, norm)
    result, d3, d2, c3, c2 = together(result, d3, d2, c3, c2)
    late = [h.hop(CORE_PAIRS) for h in (c2, c1, c3, d3, d2)]
    held += [c2, d2, c3, d3] + late
    places = [(h.value, holds) for h, holds in zip(held, all_holds)]
    return correlate(slots[1:], left, lag_rows, places, slot_count, norm, result)[None]


def solution(mesh):
    placed = (P("chan", "freq", None), P(), P("chan", None))
    fits = mesh.shape["chan"] == 8 and mesh.shape["freq"] == 4
    return jax.shard_map(
        on_device if fits else on_any_device,
        mesh=mesh,
        in_specs=placed,
        out_specs=P("chan", "freq", None, None, None),
        check_vma=False,
    )
```
